32 devices in a mesh: ctx: 8 (over z, y), tp: 4 (over x, core).
Axes of the slice: x: 2, y: 2, z: 4, core: 2. Of those that a mesh axis runs over, the one named last changes fastest.
Arguments:
- hidden: bfloat16 [2, 2, 384, 2048], P(None, None, 'ctx'), may hold values from -6 to 6
- cotangent: bfloat16 [2, 2, 384, 2048], P(None, None, 'ctx'), may hold values from -6 to 6
- lengths: int32 [2], replicated, may hold values from 192 to 768, as said below
- norm_gains: bfloat16 [2, 2, 2048], P(None, None, 'ctx'), may hold values from 0.5 to 1.5
- mix_weight: bfloat16 [2, 2048, 7168], P(None, 'ctx', 'tp'), may hold values from -0.125 to 0.125
- share_weight: bfloat16 [2, 2048, 1072], P(None, 'ctx'), may hold values from -0.125 to 0.125
- chan_params: float32 [2, 6, 3072], P(None, None, 'tp'), may hold values from -1.5 to 1.5
- shared_conv: float32 [2, 5, 512], replicated, may hold values from -1.5 to 1.5
- head_params: float32 [2, 3, 48], P(None, None, 'tp'), may hold values from -15 to 3
- out_weight: bfloat16 [2, 4096, 2048], P(None, 'tp', 'ctx'), may hold values from -0.15625 to 0.15625
- up_weight: bfloat16 [2, 2048, 8192], P(None, 'ctx', 'tp'), may hold values from -0.125 to 0.125
- down_weight: bfloat16 [2, 4096, 2048], P(None, 'tp', 'ctx'), may hold values from -0.1875 to 0.1875
Outputs:
- activations: float32 [2, 2, 384, 2048], P(None, None, 'ctx')
- input_grad: float32 [2, 2, 384, 2048], P(None, None, 'ctx')
- grad_norm_gains: float32 [2, 2, 2048], P(None, None, 'ctx')
- grad_mix_weight: float32 [2, 2048, 7168], P(None, 'ctx', 'tp')
- grad_share_weight: float32 [2, 2048, 1072], P(None, 'ctx')
- grad_chan_params: float32 [2, 6, 3072], P(None, None, 'tp')
- grad_shared_conv: float32 [2, 5, 512], replicated
- grad_head_params: float32 [2, 3, 48], P(None, None, 'tp')
- grad_out_weight: float32 [2, 4096, 2048], P(None, 'tp', 'ctx')
- grad_up_weight: float32 [2, 2048, 8192], P(None, 'ctx', 'tp')
- grad_down_weight: float32 [2, 4096, 2048], P(None, 'tp', 'ctx')
The draws below stay inside these ranges and needn't reach their ends.
Inputs may be any that keep to these rules, and one draw needn't show every extreme that they name: `lengths`: in every draw one slot has length 768.
All inputs are finite; a program needn't handle non-finite values.
Results may differ from the reference program's by a relative error of at most 0.03.
Values may be sent and summed in bfloat16 or wider, within the bound.
No kernel may reach another device: no remote copies, remote signals or barrier semaphores. Data moves between devices by JAX's collectives and lax.ppermute only.
A program may use at most 448 MiB of HBM per device.

```python
import math
import jax
import jax.numpy as jnp
from jax import lax

D = 2048
MH = 48
P_SIZE = 64
N = 256
CONV = 4
AH = 8
KVH = 2
HD = 128
FF = 4096
LAYERS = 2
SLOTS = 2
BLK = 48
SEQ = 768
MIXC = 7168
SHC = 1072
OUTR = 4096
N_CTX = 8
N_TP = 4


def draw_lengths(key, part):
    key = jax.random.fold_in(key, 3)
    key_len, key_full = jax.random.split(key)
    drawn_lengths = jax.random.randint(key_len, (SLOTS,), SEQ // 4, SEQ + 1)
    full_slot = jax.random.randint(key_full, (), 0, SLOTS)
    return jnp.where(jnp.arange(SLOTS) == full_slot, SEQ, drawn_lengths).astype(jnp.int32)


def draw_chan_params(key, part):
    key = jax.random.fold_in(key, 5)
    key_taps, key_gain = jax.random.split(key)
    conv_taps = 0.5 * jax.random.truncated_normal(key_taps, -3.0, 3.0, (LAYERS, CONV + 1, MH * P_SIZE), jnp.float32)
    gain_row = jax.random.uniform(key_gain, (LAYERS, 1, MH * P_SIZE), jnp.float32, 0.5, 1.5)
    return jnp.concatenate([conv_taps, gain_row], axis=1)


def draw_shared_conv(key, part):
    key = jax.random.fold_in(key, 7)
    conv_taps = 0.5 * jax.random.truncated_normal(key, -3.0, 3.0, (LAYERS, CONV + 1, 2 * N), jnp.float32)
    return conv_taps


def draw_head_params(key, part):
    key = jax.random.fold_in(key, 9)
    key_scale, key_rate, key_skip = jax.random.split(key, 3)
    log_scale = jax.random.uniform(key_scale, (LAYERS, MH), jnp.float32, 0.0, math.log(16.0))
    log_rate = jax.random.uniform(key_rate, (LAYERS, MH), jnp.float32, math.log(0.0001), math.log(0.05))
    step_zero = jnp.exp(log_rate - log_scale)
    step_bias = jnp.log(jnp.expm1(step_zero))
    skip_gain = jax.random.uniform(key_skip, (LAYERS, MH), jnp.float32, 0.5, 1.5)
    return jnp.stack([log_scale, step_bias, skip_gain], axis=1)


def shard_levels(stream_key, extent, cuts, least, top_value):
    level, own = 1.0, jax.random.fold_in(stream_key, 6)
    for position, shards_of in cuts:
        heights = jnp.exp(jax.random.uniform(jax.random.fold_in(own, position), (shards_of,), jnp.float32, least / len(cuts), top_value / len(cuts)))
        level = level * jnp.repeat(heights, extent[position] // shards_of).reshape([-1 if axis == position else 1 for axis in range(len(extent))])
    return level


def normal_values(key, extent, deviation, most, cuts=(), kind=jnp.bfloat16):
    entries = jax.random.normal(key, extent, jnp.float32) * deviation
    if len(cuts) > 0:
        entries = shard_levels(key, extent, cuts, -0.22, 0.18) * entries
    return jnp.clip(entries, min=-most, max=most).astype(kind)


def setup_inputs(seed: int = 0) -> dict:
    keys = jax.random.split(jax.random.key(seed), 13)
    return {
        "hidden": normal_values(keys[0], (SLOTS, 2, SEQ // 2, D), 1.0, 6.0, ((2, 8),)),
        "cotangent": normal_values(keys[1], (SLOTS, 2, SEQ // 2, D), 1.0, 6.0, ((2, 8),)),
        "lengths": draw_lengths(jax.random.fold_in(keys[12], 71), 0),
        "norm_gains": jnp.clip(1.0 + 0.1 * jax.random.normal(keys[3], (LAYERS, 2, D), jnp.float32), 0.5, 1.5).astype(jnp.bfloat16),
        "mix_weight": normal_values(keys[4], (LAYERS, D, MIXC), D ** -0.5, 0.125, ((1, 8), (2, 4))),
        "share_weight": normal_values(keys[5], (LAYERS, D, SHC), D ** -0.5, 0.125, ((1, 8),)),
        "chan_params": draw_chan_params(jax.random.fold_in(keys[12], 71), 0),
        "shared_conv": draw_shared_conv(jax.random.fold_in(keys[12], 71), 0),
        "head_params": draw_head_params(jax.random.fold_in(keys[12], 71), 0),
        "out_weight": normal_values(keys[9], (LAYERS, OUTR, D), (MH * P_SIZE // 2) ** -0.5, 0.15625, ((1, 4), (2, 8))),
        "up_weight": normal_values(keys[10], (LAYERS, D, 2 * FF), D ** -0.5, 0.125, ((1, 8), (2, 4))),
        "down_weight": normal_values(keys[11], (LAYERS, FF, D), (FF // 4) ** -0.5, 0.1875, ((1, 4), (2, 8))),
    }


eps_norm = 1e-05
rope_base = 100000000000.0
highest = lax.Precision.HIGHEST
ssd_block = 64

@jax.custom_vjp
def low(v):
    return lax.optimization_barrier(v.astype(jnp.bfloat16)).astype(jnp.float32)

@jax.custom_vjp
def low_back(v):
    return v

def low_keep(v):
    return (low(v), None)

def low_pass(kept, grad):
    return (grad,)

def back_keep(v):
    return (v, None)

def back_low(kept, grad):
    return (low(grad),)
low.defvjp(low_keep, low_pass)
low_back.defvjp(back_keep, back_low)

def matmul(left_op, right_op):
    return jnp.dot(left_op, right_op, precision=highest, preferred_element_type=jnp.float32)

def rotate(values, positions):
    half_dim = HD // 2
    inverse = jnp.exp(-jnp.log(rope_base) * (2.0 * jnp.arange(half_dim, dtype=jnp.float32) / HD))
    angles = positions.astype(jnp.float32)[..., None] * inverse
    cosine = jnp.cos(angles)
    sine_vals = jnp.sin(angles)
    front_half = values[..., :half_dim]
    back_half = values[..., half_dim:]
    return jnp.concatenate([front_half * cosine - back_half * sine_vals, back_half * cosine + front_half * sine_vals], axis=-1)

def causal_conv(values, conv_taps, conv_bias):
    length_all = values.shape[0]
    padded = jnp.pad(values, ((CONV - 1, 0), (0, 0)))
    running = conv_bias + conv_taps[0] * padded[0:length_all]
    for offset in range(1, CONV):
        running = running + conv_taps[offset] * padded[offset:offset + length_all]
    return running

def ssd_step(carry_state, piece_in):
    x_part, b_part, c_part, step_part, log_part = piece_in
    cumulative = jnp.cumsum(log_part, axis=0)
    segment = cumulative[:, None, :] - cumulative[None, :, :]
    lower_mask = (jnp.arange(ssd_block)[:, None] >= jnp.arange(ssd_block)[None, :])[:, :, None]
    decay_mat = jnp.where(lower_mask, jnp.exp(jnp.where(lower_mask, segment, 0.0)), 0.0)
    inner_bc = matmul(c_part, b_part.T)
    mixing = decay_mat * inner_bc[:, :, None] * step_part[None, :, :]
    local_part = jnp.einsum('tsh,shp->thp', mixing, x_part, precision=highest)
    carried = jnp.einsum('tn,hpn->thp', c_part, carry_state, precision=highest) * jnp.exp(cumulative)[:, :, None]
    total_log = cumulative[-1]
    weight = jnp.exp(total_log[None, :] - cumulative) * step_part
    new_state = jnp.exp(total_log)[:, None, None] * carry_state + jnp.einsum('sn,shp->hpn', b_part, x_part * weight[:, :, None], precision=highest)
    return (new_state, local_part + carried)

def run_ssd(x_heads, b_conv, c_conv, step_size, log_decay):
    groups = SEQ // ssd_block
    pieces = (x_heads.reshape(groups, ssd_block, MH, P_SIZE), b_conv.reshape(groups, ssd_block, N), c_conv.reshape(groups, ssd_block, N), step_size.reshape(groups, ssd_block, MH), log_decay.reshape(groups, ssd_block, MH))
    final_state, outputs = lax.scan(jax.checkpoint(ssd_step), jnp.zeros((MH, P_SIZE, N), jnp.float32), pieces)
    return outputs.reshape(SEQ, MH, P_SIZE)

def attention(queries, key_rows, value_rows):
    group = AH // KVH
    keys_all = jnp.repeat(key_rows, group, axis=1)
    values_all = jnp.repeat(value_rows, group, axis=1)
    positions = jnp.arange(SEQ, dtype=jnp.int32)
    qblock = 512 if SEQ % 512 == 0 else SEQ

    def one_block(start):
        q_part = lax.dynamic_slice_in_dim(queries, start, qblock, 0)
        q_positions = lax.dynamic_slice_in_dim(positions, start, qblock, 0)
        scores = low_back(jnp.einsum('qhd,khd->hqk', q_part, keys_all, precision=highest) * HD ** (-0.5))
        scores = jnp.where(positions[None, None, :] <= q_positions[None, :, None], scores, -1e+30)
        probability = low(jax.nn.softmax(scores, axis=-1))
        return jnp.einsum('hqk,khd->qhd', probability, values_all, precision=highest)
    starts = jnp.arange(SEQ // qblock, dtype=jnp.int32) * qblock
    outputs = lax.map(jax.checkpoint(one_block), starts)
    return outputs.reshape(SEQ, AH, HD)

def one_layer(stream, valid_rows, gain_rows, mix_full, share_full, chan_layer, conv_layer, head_layer, out_full, up_full, down_full):
    mh_tp = MH // N_TP
    ah_tp = AH // N_TP
    ff_tp = FF // N_TP
    positions = jnp.arange(SEQ, dtype=jnp.int32)
    factor_one = lax.rsqrt(lax.optimization_barrier(jnp.mean(stream * stream, axis=-1, keepdims=True)) + eps_norm)
    normed_one = low(stream * factor_one * gain_rows[0])
    mixed = low_back(matmul(normed_one, mix_full)).reshape(SEQ, N_TP, -1)
    shared = low_back(matmul(normed_one, share_full))
    gate_z = mixed[:, :, :mh_tp * P_SIZE].reshape(SEQ, MH * P_SIZE)
    x_pre = mixed[:, :, mh_tp * P_SIZE:2 * mh_tp * P_SIZE].reshape(SEQ, MH * P_SIZE)
    q_pre = mixed[:, :, 2 * mh_tp * P_SIZE:].reshape(SEQ, AH, HD)
    bc_pre = shared[:, :2 * N]
    k_pre = shared[:, 2 * N:2 * N + KVH * HD].reshape(SEQ, KVH, HD)
    v_pre = shared[:, 2 * N + KVH * HD:2 * N + 2 * KVH * HD].reshape(SEQ, KVH, HD)
    dt_pre = shared[:, 2 * N + 2 * KVH * HD:]
    x_conv = jax.nn.silu(causal_conv(x_pre, chan_layer[:CONV], chan_layer[CONV]))
    bc_conv = jax.nn.silu(causal_conv(bc_pre, conv_layer[:CONV], conv_layer[CONV]))
    step_size = jax.nn.softplus(dt_pre + head_layer[1])
    decay_rate = -jnp.exp(head_layer[0])
    x_heads = x_conv.reshape(SEQ, MH, P_SIZE)
    ssm_y = run_ssd(x_heads, bc_conv[:, :N], bc_conv[:, N:], step_size, step_size * decay_rate) + head_layer[2][:, None] * x_heads
    gated = ssm_y.reshape(SEQ, MH * P_SIZE) * jax.nn.silu(gate_z)
    gated_scale = lax.rsqrt(lax.optimization_barrier(jnp.mean(gated * gated, axis=-1, keepdims=True)) + eps_norm)
    gated_low = low(gated * chan_layer[CONV + 1])
    queries = low(rotate(q_pre, positions[:, None]))
    key_rows = low(rotate(k_pre, positions[:, None]))
    value_rows = low(v_pre)
    attended = low(low_back(attention(queries, key_rows, value_rows))).reshape(SEQ, AH * HD)
    out_blocks = out_full.reshape(N_TP, -1, D)
    out_ssm = out_blocks[:, :mh_tp * P_SIZE].reshape(MH * P_SIZE, D)
    out_att = out_blocks[:, mh_tp * P_SIZE:].reshape(AH * HD, D)
    branch = low_back(gated_scale * matmul(gated_low, out_ssm) + matmul(attended, out_att))
    middle = stream + branch
    factor_two = lax.rsqrt(lax.optimization_barrier(jnp.mean(middle * middle, axis=-1, keepdims=True)) + eps_norm)
    normed_two = low(middle * factor_two * gain_rows[1])
    gate_up = low_back(matmul(normed_two, up_full)).reshape(SEQ, N_TP, -1)
    gate_vals = gate_up[:, :, :ff_tp].reshape(SEQ, FF)
    up_vals = gate_up[:, :, ff_tp:].reshape(SEQ, FF)
    activation = low(jax.nn.silu(gate_vals) * up_vals)
    ffn_out = low_back(matmul(activation, down_full))
    return (middle + ffn_out) * valid_rows[:, None]

def forward(streams, norm_gains, mix_weight, share_weight, chan_params, shared_conv, head_params, out_weight, up_weight, down_weight, lengths):
    positions = jnp.arange(SEQ, dtype=jnp.int32)
    layer_fn = jax.checkpoint(one_layer)

    def one_slot(inputs):
        stream, length_one = inputs
        valid_rows = (positions < length_one).astype(jnp.float32)
        for layer_idx in range(LAYERS):
            stream = layer_fn(stream, valid_rows, norm_gains[layer_idx], mix_weight[layer_idx], share_weight[layer_idx], chan_params[layer_idx], shared_conv[layer_idx], head_params[layer_idx], out_weight[layer_idx], up_weight[layer_idx], down_weight[layer_idx])
        return stream
    return lax.map(one_slot, (streams, lengths))

def unpack(packed):
    blocks = packed.reshape(SLOTS, 2, N_CTX, BLK, packed.shape[-1])
    first_half = blocks[:, 0].reshape(SLOTS, N_CTX * BLK, -1)
    second_half = blocks[:, 1, ::-1].reshape(SLOTS, N_CTX * BLK, -1)
    return jnp.concatenate([first_half, second_half], axis=1)

def pack_slots(sequences):
    halves = sequences.reshape(SLOTS, 2, N_CTX, BLK, sequences.shape[-1])
    return jnp.stack([halves[:, 0], halves[:, 1, ::-1]], axis=1).reshape(SLOTS, 2, N_CTX * BLK, -1)

def reference(hidden, cotangent, lengths, norm_gains, mix_weight, share_weight, chan_params, shared_conv, head_params, out_weight, up_weight, down_weight):
    streams = unpack(hidden.astype(jnp.float32))
    cot_slots = unpack(cotangent.astype(jnp.float32))

    def model_fn(streams_in, gains_in, mix_in, share_in, chan_in, conv_in, head_in, out_in, up_in, down_in):
        return forward(streams_in, gains_in, mix_in, share_in, chan_in, conv_in, head_in, out_in, up_in, down_in, lengths)
    outputs, pullback = jax.vjp(model_fn, streams, norm_gains.astype(jnp.float32), mix_weight.astype(jnp.float32), share_weight.astype(jnp.float32), chan_params, shared_conv, head_params, out_weight.astype(jnp.float32), up_weight.astype(jnp.float32), down_weight.astype(jnp.float32))
    grads = pullback(cot_slots)
    return (pack_slots(outputs), pack_slots(grads[0]), grads[1], grads[2], grads[3], grads[4], grads[5], grads[6], grads[7], grads[8], grads[9])
```

```python
import jax
import jax.numpy as jnp
from jax import lax
from jax.sharding import Mesh
from jax.sharding import PartitionSpec as P

D = 2048
MH = 48
P_SIZE = 64
N = 256
CONV = 4
AH = 8
KVH = 2
HD = 128
FF = 4096
LAYERS = 2
HGROUPS = 4
CHUNK = 128

eps_norm = 1e-05
rope_base = 100000000000.0
highest = lax.Precision.HIGHEST
SWAP = [(0, 1), (1, 0)]
bf16 = jnp.bfloat16
f32 = jnp.float32


def matmul(left_op, right_op):
    return jnp.dot(left_op, right_op, preferred_element_type=f32)


def matmul_tn(left_op, right_op):
    return lax.dot_general(left_op, right_op, (((0,), (0,)), ((), ())), preferred_element_type=f32)


def matmul_nt(left_op, right_op):
    return lax.dot_general(left_op, right_op, (((1,), (1,)), ((), ())), preferred_element_type=f32)


def silu_grad(inputs):
    sigmoid = jax.nn.sigmoid(inputs)
    return sigmoid * (1.0 + inputs * (1.0 - sigmoid))


def pick(x, dim, index):
    return lax.dynamic_index_in_dim(x, index, dim, keepdims=False)


def rope_tables(positions):
    half_dim = HD // 2
    inverse = jnp.exp(-jnp.log(rope_base) * (2.0 * jnp.arange(half_dim, dtype=f32) / HD))
    angles = positions.astype(f32)[..., None] * inverse
    return jnp.cos(angles), jnp.sin(angles)


def rotate(values, tables, sign):
    cosine, sine = tables
    sine = sine * sign
    half_dim = HD // 2
    front = values[..., :half_dim]
    back = values[..., half_dim:]
    return jnp.concatenate([front * cosine - back * sine, back * cosine + front * sine], axis=-1)


def norm_piece(stream, gain_row):
    factor = lax.rsqrt(jnp.mean(stream * stream, axis=-1, keepdims=True) + eps_norm)
    return stream * factor * gain_row


def causal_conv(pre, taps, bias):
    length = pre.shape[0]
    padded = jnp.concatenate([jnp.zeros((CONV - 1, pre.shape[1]), pre.dtype), pre], axis=0)
    running = bias + taps[0] * padded[0:length]
    for offset in range(1, CONV):
        running = running + taps[offset] * padded[offset : offset + length]
    return jax.nn.silu(running)


def ssm_piece(x_pre, bc_pre, dt_raw, taps, shared_taps, params):
    length, width = x_pre.shape
    heads = dt_raw.shape[1]
    chunks = length // CHUNK
    x_conv = causal_conv(x_pre, taps[:CONV], taps[CONV]).reshape(chunks, CHUNK, heads, width // heads)
    bc_conv = causal_conv(bc_pre, shared_taps[:CONV], shared_taps[CONV]).reshape(chunks, CHUNK, 2 * N)
    b_conv, c_conv = bc_conv[..., :N], bc_conv[..., N:]
    step_size = jax.nn.softplus(dt_raw + params[1]).reshape(chunks, CHUNK, heads)
    decay_rate = -jnp.exp(params[0])
    cumulative = jnp.cumsum(step_size * decay_rate, axis=1)
    total_log = cumulative[:, -1]
    weight = jnp.exp(total_log[:, None, :] - cumulative) * step_size
    states = jnp.einsum("bsn,bshp->bhpn", b_conv, x_conv * weight[..., None], precision=highest)
    decay = jnp.exp(total_log)
    entering = [jnp.zeros_like(states[0])]
    for index in range(chunks - 1):
        entering.append(decay[index][:, None, None] * entering[-1] + states[index])
    entering = jnp.stack(entering)
    segment = cumulative[:, :, None, :] - cumulative[:, None, :, :]
    lower = (jnp.arange(CHUNK)[:, None] >= jnp.arange(CHUNK)[None, :])[None, :, :, None]
    decay_mat = jnp.where(lower, jnp.exp(jnp.where(lower, segment, 0.0)), 0.0)
    inner = jnp.einsum("btn,bsn->bts", c_conv, b_conv, precision=highest)
    mixing = decay_mat * inner[..., None] * step_size[:, None, :, :]
    local_part = jnp.einsum("btsh,bshp->bthp", mixing, x_conv, precision=highest)
    carried = (
        jnp.einsum("btn,bhpn->bthp", c_conv, entering, precision=highest)
        * jnp.exp(cumulative)[..., None]
    )
    return (local_part + carried + params[2][:, None] * x_conv).reshape(length, width)


def build(ctx_axes, tp_axes):
    half_axis = ctx_axes[0]
    group_axes = ctx_axes[1:]
    t_half, t_core = tp_axes
    ring_axes = group_axes + (t_half,)
    slot_axes = group_axes + tp_axes
    all_axes = ctx_axes + tp_axes
    span = len(ring_axes)

    def column_parts(width):
        unit = width // 128
        marks = [0] + [128 * (unit * (k + 1) // 3) for k in range(3)]
        return list(zip(marks[:-1], marks[1:]))

    def rotated(part):
        turn = part % span
        return ring_axes[turn:] + ring_axes[:turn]

    def gather_rows(x):
        rows, width = x.shape
        parts = []
        for part, (low, high) in enumerate(column_parts(width)):
            held = x[:, low:high].reshape((1,) * span + (rows, high - low))
            for axis in rotated(part):
                dim = ring_axes.index(axis)
                got = lax.ppermute(held, axis, SWAP)
                first = lax.axis_index(axis) == 0
                held = jnp.where(
                    first, jnp.concatenate([held, got], dim), jnp.concatenate([got, held], dim)
                )
            parts.append(held)
        held = jnp.concatenate(parts, -1).reshape(-1, 1, rows, width)
        got = lax.ppermute(held, t_core, SWAP)
        first = lax.axis_index(t_core) == 0
        held = jnp.where(first, jnp.concatenate([held, got], 1), jnp.concatenate([got, held], 1))
        return held.reshape(-1, width)

    def scatter_product(left, right):
        total = left.shape[0]
        width = right.shape[0]
        peers = 2 ** (span + 1)
        rows = total // peers
        split = left.reshape(peers // 2, 2, rows, left.shape[1])
        core = lax.axis_index(t_core)
        flat = (total // 2, left.shape[1])
        sent = matmul_nt(pick(split, 1, 1 - core).reshape(flat), right).astype(bf16)
        kept = matmul_nt(pick(split, 1, core).reshape(flat), right)
        held = kept + lax.ppermute(sent, t_core, SWAP).astype(f32)
        parts = []
        for part, (low, high) in enumerate(column_parts(width)):
            piece = held[:, low:high].reshape((2,) * span + (rows, high - low))
            names = list(ring_axes)
            for axis in rotated(part):
                dim = names.index(axis)
                names.pop(dim)
                index = lax.axis_index(axis)
                got = lax.ppermute(pick(piece, dim, 1 - index).astype(bf16), axis, SWAP)
                piece = pick(piece, dim, index) + got.astype(f32)
            parts.append(piece)
        return jnp.concatenate(parts, -1)

    def sum_over(x, axes):
        for axis in axes:
            x = x + lax.ppermute(x, axis, SWAP)
        return x

    def group_index():
        return lax.axis_index(group_axes)

    def group_swap(blocks):
        members = blocks.shape[0]
        me = group_index()
        came = [pick(blocks, 0, me)]
        for offset in range(1, members):
            route = [(i, i ^ offset) for i in range(members)]
            came.append(lax.ppermute(pick(blocks, 0, me ^ offset), group_axes, route))
        stacked = jnp.stack(came)
        shape = stacked.shape
        stacked = stacked.reshape((2,) * len(group_axes) + shape[1:])
        for dim, axis in enumerate(group_axes):
            stacked = jnp.where(lax.axis_index(axis) == 0, stacked, jnp.flip(stacked, dim))
        return stacked.reshape(shape)

    def spread(blocks):
        came = group_swap(blocks)
        other = lax.ppermute(came, half_axis, SWAP)
        first = lax.axis_index(half_axis) == 0
        return jnp.where(first, jnp.concatenate([came, other]), jnp.concatenate([other, came]))

    def collect(blocks):
        half = lax.axis_index(half_axis)
        paired = blocks.reshape((2, blocks.shape[0] // 2) + blocks.shape[1:])
        got = lax.ppermute(pick(paired, 0, 1 - half).astype(bf16), half_axis, SWAP)
        summed = pick(paired, 0, half).astype(f32) + got.astype(f32)
        return group_swap(summed.astype(bf16)).astype(f32)

    def local(
        hidden,
        cotangent,
        lengths,
        norm_gains,
        mix_weight,
        share_weight,
        chan_params,
        shared_conv,
        head_params,
        out_weight,
        up_weight,
        down_weight,
    ):
        members = 2 ** len(group_axes)
        ctx_count = 2 * members
        replicas = members // HGROUPS
        slot = lax.axis_index(half_axis)
        me = group_index()
        head_group = me // replicas
        head_part = me % replicas
        tp_half = lax.axis_index(t_half)
        tp_core = lax.axis_index(t_core)
        tp_index = tp_half * 2 + tp_core
        block_len = hidden.shape[2]
        depth = mix_weight.shape[1]
        seq_len = 2 * ctx_count * block_len
        own_len = 4 * block_len
        tp_heads = chan_params.shape[2] // P_SIZE
        heads = tp_heads // HGROUPS
        lanes = P_SIZE // replicas
        width = heads * lanes
        ssm_cols = tp_heads * P_SIZE
        qheads = AH // 4
        q_cols = qheads * HD
        ff_tp = FF // 4
        ff_own = ff_tp // members
        kv_cols = 2 * N
        dt_cols = 2 * N + 2 * KVH * HD
        kv_head = tp_index * qheads // (AH // KVH)
        score_scale = HD ** (-0.5)

        def block_of(member, half, cube):
            near = cube * members + member
            return jnp.where(half == 0, near, 2 * ctx_count - 1 - near)

        within = jnp.arange(block_len)
        own_pos = block_of(me, tp_half, tp_core) * block_len + within
        own_valid = (own_pos < lengths[slot]).astype(f32)[:, None]
        quarter = jnp.arange(4)
        query_pos = (
            block_of(me, quarter // 2, quarter % 2)[:, None] * block_len + within[None, :]
        ).reshape(own_len)
        key_pos = jnp.arange(seq_len)
        causal = key_pos[None, :] <= query_pos[:, None]
        key_tables = rope_tables(key_pos)
        query_tables = tuple(table[:, None] for table in rope_tables(query_pos))

        def to_sequence(x):
            blocks = x.reshape(members, 4, block_len, x.shape[1])
            parts = [blocks[:, 0], blocks[:, 1], blocks[::-1, 3], blocks[::-1, 2]]
            return jnp.concatenate([part.reshape(-1, x.shape[1]) for part in parts])

        def from_sequence(x):
            blocks = x.reshape(4, members, block_len, x.shape[1])
            parts = [blocks[0], blocks[1], blocks[3, ::-1], blocks[2, ::-1]]
            return jnp.stack(parts, axis=1).reshape(x.shape)

        def own_rows(x):
            return lax.dynamic_slice_in_dim(x, me * own_len, own_len, 0)

        def at_own_rows(x):
            return lax.dynamic_update_slice_in_dim(
                jnp.zeros((seq_len, x.shape[1]), x.dtype), x, me * own_len, 0
            )

        def bring_in(x):
            got = lax.ppermute(
                pick(pick(x, 0, 1 - slot), 0, tp_half), (half_axis, t_core), [(0, 2), (3, 1)]
            )
            return jnp.where(tp_core == slot, pick(pick(x, 0, slot), 0, tp_half), got)

        def bring_out(x):
            x = x.astype(bf16)
            got = lax.ppermute(x, (half_axis, t_core), [(1, 3), (2, 0)])
            pair = jnp.where(slot == 0, jnp.stack([x, got]), jnp.stack([got, x]))
            other = lax.ppermute(pair, t_core, SWAP)
            pair = jnp.where(tp_core == slot, pair, other)
            other = lax.ppermute(pair, t_half, SWAP)
            both = jnp.where(tp_half == 0, jnp.stack([pair, other], 1), jnp.stack([other, pair], 1))
            return both.astype(f32)

        def cut_heads(x, axis):
            shape = x.shape
            split = x.reshape(
                shape[:axis] + (HGROUPS, heads, replicas, lanes) + shape[axis + 1 :]
            )
            split = jnp.moveaxis(split, (axis, axis + 2), (0, 1))
            return split.reshape((members,) + shape[:axis] + (width,) + shape[axis + 1 :])

        def join_heads(x, axis):
            shape = x.shape[1:]
            split = x.reshape(
                (HGROUPS, replicas) + shape[:axis] + (heads, lanes) + shape[axis + 1 :]
            )
            split = jnp.moveaxis(split, (0, 1), (axis, axis + 2))
            return split.reshape(shape[:axis] + (ssm_cols,) + shape[axis + 1 :])

        def attend(queries, key_rows, value_rows):
            scores = jnp.einsum("qhd,kd->hqk", queries, key_rows, preferred_element_type=f32)
            scores = jnp.where(causal[None], scores * score_scale, -1e30)
            row_peak = jnp.max(scores, axis=-1, keepdims=True)
            exp_scores = jnp.exp(scores - row_peak)
            row_total = jnp.sum(exp_scores, axis=-1, keepdims=True)
            probability = (exp_scores / row_total).astype(bf16)
            attended = jnp.einsum(
                "hqk,kd->qhd", probability, value_rows, preferred_element_type=f32
            )
            return attended, row_peak + jnp.log(row_total)

        def attend_back(queries, key_rows, value_rows, logsum, grad_out):
            scores = jnp.einsum("qhd,kd->hqk", queries, key_rows, preferred_element_type=f32)
            scores = jnp.where(causal[None], scores * score_scale, -1e30)
            probability = jnp.exp(scores - logsum)
            probs_low = probability.astype(bf16)
            grad_probs = jnp.einsum(
                "qhd,kd->hqk", grad_out, value_rows, preferred_element_type=f32
            )
            inner_sum = jnp.sum(probability * grad_probs, axis=-1, keepdims=True)
            grad_scores = (probability * (grad_probs - inner_sum)).astype(bf16)
            grad_q = (
                jnp.einsum("hqk,kd->qhd", grad_scores, key_rows, preferred_element_type=f32)
                * score_scale
            )
            grad_k = (
                jnp.einsum("hqk,qhd->kd", grad_scores, queries, preferred_element_type=f32)
                * score_scale
            )
            grad_v = jnp.einsum("hqk,qhd->kd", probs_low, grad_out, preferred_element_type=f32)
            return grad_q, grad_k, grad_v

        stream = bring_in(hidden).astype(f32)
        gains = lax.all_gather(norm_gains, ctx_axes, axis=2, tiled=True).astype(f32)
        own_chan = pick(cut_heads(chan_params, 2), 0, me)
        own_heads = pick(head_params.reshape(LAYERS, 3, HGROUPS, heads), 2, head_group)
        share_rows = lax.dynamic_slice_in_dim(share_weight, tp_index * (depth // 4), depth // 4, 1)
        dt_start = dt_cols + tp_index * tp_heads + head_group * heads

        weights = []
        for layer in range(LAYERS):
            mix = mix_weight[layer]
            mix_blocks = jnp.concatenate(
                [cut_heads(mix[:, :ssm_cols], 1), cut_heads(mix[:, ssm_cols : 2 * ssm_cols], 1)], 2
            )
            mix_own = spread(mix_blocks).reshape(D, 2 * width)
            query_w = lax.all_gather(mix[:, 2 * ssm_cols :], ctx_axes, axis=0, tiled=True)
            share = lax.all_gather(share_rows[layer], all_axes, axis=0, tiled=True)
            key_w = lax.dynamic_slice_in_dim(share, kv_cols + kv_head * HD, HD, 1)
            value_w = lax.dynamic_slice_in_dim(share, kv_cols + (KVH + kv_head) * HD, HD, 1)
            dt_w = lax.dynamic_slice_in_dim(share, dt_start, heads, 1)
            in_w = jnp.concatenate(
                [mix_own, share[:, :kv_cols], key_w, value_w, query_w, dt_w], axis=1
            )
            out = out_weight[layer]
            out_own = jnp.moveaxis(spread(cut_heads(out[:ssm_cols], 0)), 0, 1).reshape(width, D)
            out_att = lax.all_gather(out[ssm_cols:], ctx_axes, axis=1, tiled=True)
            up_blocks = jnp.moveaxis(
                up_weight[layer].reshape(depth, 2, members, ff_own), 2, 0
            ).reshape(members, depth, 2 * ff_own)
            up_own = spread(up_blocks).reshape(D, 2 * ff_own)
            down_blocks = down_weight[layer].reshape(members, ff_own, depth)
            down_own = jnp.moveaxis(spread(down_blocks), 0, 1).reshape(ff_own, D)
            weights.append((in_w, jnp.concatenate([out_own, out_att]), up_own, down_own))

        cuts = [0, width, 2 * width]
        for size in (kv_cols, HD, HD, q_cols, heads):
            cuts.append(cuts[-1] + size)

        records = []
        for layer in range(LAYERS):
            in_w, out_w, up_w, down_w = weights[layer]
            rec = {}
            normed_f, rec["norm_one_back"] = jax.vjp(norm_piece, stream, gains[layer, 0])
            normed_rows = gather_rows(normed_f.astype(bf16))
            normed = to_sequence(normed_rows)
            mixed = matmul(normed, in_w)
            gate_z, x_pre, bc_pre, key_pre, value_pre, _, dt_raw = (
                mixed[:, low:high] for low, high in zip(cuts[:-1], cuts[1:])
            )
            q_pre = own_rows(from_sequence(mixed[:, cuts[5] : cuts[6]]))
            taps = own_chan[layer]
            ssm_y, rec["ssm_back"] = jax.vjp(
                ssm_piece, x_pre, bc_pre, dt_raw, taps[: CONV + 1], shared_conv[layer], own_heads[layer]
            )
            gated = ssm_y * jax.nn.silu(gate_z)
            squares = jnp.sum(gated * gated, axis=-1).reshape(-1, 128)
            sum_squares = sum_over(squares, (t_core,) + ring_axes[::-1]).reshape(seq_len, 1)
            gated_scale = lax.rsqrt(sum_squares / (MH * P_SIZE) + eps_norm)
            gated_low = (gated * taps[CONV + 1]).astype(bf16)
            scaled_low = (gated_low.astype(f32) * gated_scale).astype(bf16)
            queries = rotate(q_pre.reshape(own_len, qheads, HD), query_tables, 1.0).astype(bf16)
            key_rows = rotate(key_pre, key_tables, 1.0).astype(bf16)
            value_rows = value_pre.astype(bf16)
            attended, logsum = attend(queries, key_rows, value_rows)
            att_low = attended.reshape(own_len, q_cols).astype(bf16)
            mixer = jnp.concatenate([from_sequence(scaled_low), at_own_rows(att_low)], axis=1)
            middle = stream + scatter_product(mixer, out_w.T)
            normed_two_f, rec["norm_two_back"] = jax.vjp(norm_piece, middle, gains[layer, 1])
            normed_two = gather_rows(normed_two_f.astype(bf16))
            gate_up = matmul(normed_two, up_w)
            gate_vals, up_vals = gate_up[:, :ff_own], gate_up[:, ff_own:]
            activation = (jax.nn.silu(gate_vals) * up_vals).astype(bf16)
            stream = (middle + scatter_product(activation, down_w.T)) * own_valid
            rec.update(
                normed=normed, gate_z=gate_z, ssm_y=ssm_y, gated=gated, gated_low=gated_low,
                scaled_low=scaled_low, gated_scale=gated_scale, queries=queries, key_rows=key_rows,
                value_rows=value_rows, logsum=logsum, att_low=att_low, normed_two=normed_two,
                gate_vals=gate_vals, up_vals=up_vals, activation=activation,
            )
            records.append(rec)
        activations = bring_out(stream)

        grad_stream = bring_in(cotangent).astype(f32)
        out_grads = [None] * LAYERS
        for layer in reversed(range(LAYERS)):
            in_w, out_w, up_w, down_w = weights[layer]
            rec = records[layer]
            taps = own_chan[layer]
            grad_masked = grad_stream * own_valid
            grad_ffn = gather_rows(grad_masked.astype(bf16))
            grad_activation = matmul_nt(grad_ffn, down_w)
            grad_down = matmul_tn(rec["activation"], grad_ffn)
            gate_vals = rec["gate_vals"]
            grad_gate = grad_activation * rec["up_vals"] * silu_grad(gate_vals)
            grad_upper = grad_activation * jax.nn.silu(gate_vals)
            grad_gate_up = jnp.concatenate([grad_gate, grad_upper], axis=1).astype(bf16)
            grad_upw = matmul_tn(rec["normed_two"], grad_gate_up)
            grad_normed_two = scatter_product(grad_gate_up, up_w)
            grad_middle_norm, grad_gain_two = rec["norm_two_back"](grad_normed_two)
            grad_middle = grad_masked + grad_middle_norm
            branch_rows = gather_rows(grad_middle.astype(bf16))
            branch = to_sequence(branch_rows)
            branch_own = own_rows(branch_rows)
            grad_low_raw = matmul_nt(branch, out_w[:width])
            gated_scale = rec["gated_scale"]
            scale_part = jnp.sum(grad_low_raw * rec["gated_low"].astype(f32), axis=-1)
            grad_scale = sum_over(
                scale_part.reshape(-1, 128), (t_core,) + ring_axes[::-1]
            ).reshape(seq_len, 1)
            grad_squares = grad_scale * -0.5 * gated_scale * gated_scale * gated_scale / (MH * P_SIZE)
            grad_gated_low = gated_scale * grad_low_raw
            grad_out_ssm = matmul_tn(rec["scaled_low"], branch)
            grad_out_att = matmul_tn(rec["att_low"], branch_own)
            grad_att = matmul_nt(branch_own, out_w[width:]).astype(bf16)
            gated, gate_z = rec["gated"], rec["gate_z"]
            grad_gated = grad_gated_low * taps[CONV + 1] + 2.0 * grad_squares * gated
            grad_chan_gain = jnp.sum(grad_gated_low * gated, axis=0)
            grad_ssm_y = grad_gated * jax.nn.silu(gate_z)
            grad_z = grad_gated * rec["ssm_y"] * silu_grad(gate_z)
            grad_q, grad_k, grad_v = attend_back(
                rec["queries"], rec["key_rows"], rec["value_rows"], rec["logsum"],
                grad_att.reshape(own_len, qheads, HD),
            )
            grad_q = rotate(grad_q, query_tables, -1.0).reshape(own_len, q_cols).astype(bf16)
            grad_k = rotate(grad_k, key_tables, -1.0)
            grad_x, grad_bc, grad_dt, grad_taps, grad_conv, grad_heads = rec["ssm_back"](grad_ssm_y)
            grad_mix_own = jnp.concatenate([grad_z, grad_x], axis=1).astype(bf16)
            grad_share_part = jnp.concatenate([grad_bc, grad_k, grad_v], axis=1).astype(bf16)
            grad_dt = grad_dt.astype(bf16)
            grad_in = jnp.concatenate(
                [
                    from_sequence(jnp.concatenate([grad_mix_own, grad_share_part], axis=1)),
                    at_own_rows(grad_q),
                    from_sequence(grad_dt),
                ],
                axis=1,
            )
            grad_normed_one = scatter_product(grad_in, in_w)
            grad_stream_norm, grad_gain_one = rec["norm_one_back"](grad_normed_one)
            grad_stream = grad_middle + grad_stream_norm
            grad_share = jnp.zeros((seq_len, share_weight.shape[2]), bf16)
            grad_share = lax.dynamic_update_slice(grad_share, grad_share_part[:, :kv_cols], (0, 0))
            grad_share = lax.dynamic_update_slice(
                grad_share, grad_share_part[:, kv_cols : kv_cols + HD], (0, kv_cols + kv_head * HD)
            )
            grad_share = lax.dynamic_update_slice(
                grad_share, grad_share_part[:, kv_cols + HD :], (0, kv_cols + (KVH + kv_head) * HD)
            )
            grad_share = lax.dynamic_update_slice(grad_share, grad_dt, (0, dt_start))
            grad_share = lax.psum(grad_share, slot_axes)
            normed = rec["normed"]
            near = lax.dynamic_slice_in_dim(normed, (slot * members + me) * depth, depth, 1)
            far = lax.dynamic_slice_in_dim(normed, ((1 - slot) * members + me) * depth, depth, 1)
            share_far = lax.ppermute(matmul_tn(far, grad_share).astype(bf16), half_axis, SWAP)
            grad_sharew = matmul_tn(near, grad_share) + share_far.astype(f32)

            mix_blocks = matmul_tn(normed, grad_mix_own).reshape(ctx_count, depth, 2 * width)
            mix_came = collect(mix_blocks)
            normed_own = own_rows(from_sequence(normed))
            grad_query_w = lax.psum_scatter(
                matmul_tn(normed_own, grad_q).astype(bf16), ctx_axes, scatter_dimension=0, tiled=True
            ).astype(f32)
            grad_mixw = jnp.concatenate(
                [
                    join_heads(mix_came[:, :, :width], 1),
                    join_heads(mix_came[:, :, width:], 1),
                    grad_query_w,
                ],
                axis=1,
            )
            out_came = collect(jnp.moveaxis(grad_out_ssm.reshape(width, ctx_count, depth), 1, 0))
            grad_out_att = lax.psum_scatter(
                grad_out_att.astype(bf16), ctx_axes, scatter_dimension=1, tiled=True
            ).astype(f32)
            grad_outw = jnp.concatenate([join_heads(out_came, 0), grad_out_att], axis=0)
            up_came = collect(grad_upw.reshape(ctx_count, depth, 2 * ff_own))
            grad_upw = jnp.moveaxis(up_came.reshape(members, depth, 2, ff_own), 0, 2).reshape(
                depth, 2 * ff_tp
            )
            down_came = collect(jnp.moveaxis(grad_down.reshape(ff_own, ctx_count, depth), 1, 0))
            grad_down = down_came.reshape(ff_tp, depth)
            chan_grad = jnp.concatenate([grad_taps, grad_chan_gain[None]], axis=0)
            out_grads[layer] = (
                jnp.stack([grad_gain_one, grad_gain_two]), grad_mixw, grad_sharew, chan_grad,
                grad_conv, grad_heads, grad_outw, grad_upw, grad_down,
            )
        input_grad = bring_out(grad_stream)
        stacked = [
            jnp.stack([out_grads[layer][index] for layer in range(LAYERS)]) for index in range(9)
        ]
        gain_g, mix_g, share_g, chan_g, conv_g, head_g, out_g, up_g, down_g = stacked
        chan_rows = jnp.zeros((LAYERS, CONV + 2, HGROUPS, heads, replicas, lanes), f32)
        chan_rows = lax.dynamic_update_slice(
            chan_rows,
            chan_g.reshape(LAYERS, CONV + 2, 1, heads, 1, lanes),
            (0, 0, head_group, 0, head_part, 0),
        ).reshape(LAYERS, CONV + 2, ssm_cols)
        head_rows = lax.dynamic_update_slice(
            jnp.zeros((LAYERS, 3, HGROUPS, heads), f32), head_g[:, :, None], (0, 0, head_group, 0)
        ).reshape(LAYERS, 3, tp_heads)
        chan_sum, head_sum = lax.psum((chan_rows, head_rows), ctx_axes)
        conv_sum, gain_sum = lax.psum((conv_g, gain_g), all_axes)
        ctx_index = slot * members + me
        gain_own = lax.dynamic_slice_in_dim(gain_sum, ctx_index * depth, depth, 2)
        return (
            activations,
            input_grad,
            gain_own,
            mix_g,
            share_g,
            chan_sum,
            conv_sum,
            head_sum,
            out_g,
            up_g,
            down_g,
        )

    return local


def solution(mesh):
    ctx_bits = mesh.shape["ctx"].bit_length() - 1
    tp_bits = mesh.shape["tp"].bit_length() - 1
    ctx_axes = tuple(f"c{k}" for k in range(ctx_bits))
    tp_axes = tuple(f"t{k}" for k in range(tp_bits))
    fine = Mesh(mesh.devices.reshape((2,) * (ctx_bits + tp_bits)), ctx_axes + tp_axes)
    return jax.shard_map(
        build(ctx_axes, tp_axes),
        mesh=fine,
        in_specs=(
            P(None, None, ctx_axes, None),
            P(None, None, ctx_axes, None),
            P(),
            P(None, None, ctx_axes),
            P(None, ctx_axes, tp_axes),
            P(None, ctx_axes, None),
            P(None, None, tp_axes),
            P(),
            P(None, None, tp_axes),
            P(None, tp_axes, ctx_axes),
            P(None, ctx_axes, tp_axes),
            P(None, tp_axes, ctx_axes),
        ),
        out_specs=(
            P(None, None, ctx_axes, None),
            P(None, None, ctx_axes, None),
            P(None, None, ctx_axes),
            P(None, ctx_axes, tp_axes),
            P(None, ctx_axes, None),
            P(None, None, tp_axes),
            P(),
            P(None, None, tp_axes),
            P(None, tp_axes, ctx_axes),
            P(None, ctx_axes, tp_axes),
            P(None, tp_axes, ctx_axes),
        ),
        check_vma=False,
    )
```

```python
import functools

import jax
import jax.numpy as jnp
from jax import lax
from jax.experimental import pallas as pl
from jax.experimental.pallas import tpu as pltpu
from jax.sharding import Mesh
from jax.sharding import PartitionSpec as P

D = 2048
MH = 48
P_SIZE = 64
N = 256
CONV = 4
AH = 8
KVH = 2
HD = 128
FF = 4096
LAYERS = 2
HGROUPS = 4
PAD = 8

eps_norm = 1e-05
rope_base = 100000000000.0
highest = lax.Precision.HIGHEST
SWAP = [(0, 1), (1, 0)]
bf16 = jnp.bfloat16
f32 = jnp.float32


def matmul(left_op, right_op):
    return jnp.dot(left_op, right_op, preferred_element_type=f32)


def matmul_tn(left_op, right_op):
    return lax.dot_general(left_op, right_op, (((0,), (0,)), ((), ())), preferred_element_type=f32)


def matmul_nt(left_op, right_op):
    return lax.dot_general(left_op, right_op, (((1,), (1,)), ((), ())), preferred_element_type=f32)


def product_tn_block(left, right, out):
    out[...] = dot_tn(left[...], right[...]).astype(bf16)


def product_tn(left, right):
    rows, m = left.shape
    n = right.shape[1]
    block = min(m, 1024 if rows <= 768 else 256)
    return pl.pallas_call(
        product_tn_block,
        grid=(m // block,),
        in_specs=[
            pl.BlockSpec((rows, block), lambda i: (0, i)),
            pl.BlockSpec((rows, n), lambda i: (0, 0)),
        ],
        out_specs=pl.BlockSpec((block, n), lambda i: (i, 0)),
        out_shape=jax.ShapeDtypeStruct((m, n), bf16),
        compiler_params=pltpu.CompilerParams(vmem_limit_bytes=30 * 2**20),
        cost_estimate=pl.CostEstimate(
            flops=2 * rows * m * n, bytes_accessed=2 * (rows * m + rows * n + m * n), transcendentals=0
        ),
    )(left, right)


def silu_grad(inputs):
    sigmoid = jax.nn.sigmoid(inputs)
    return sigmoid * (1.0 + inputs * (1.0 - sigmoid))


def after(x, point):
    return lax.optimization_barrier((x, point))[0]


def pick(x, dim, index):
    return lax.dynamic_index_in_dim(x, index, dim, keepdims=False)


def norm_piece(stream, gain_row):
    factor = lax.rsqrt(jnp.mean(stream * stream, axis=-1, keepdims=True) + eps_norm)
    return stream * factor * gain_row


def dot_nn(a, b):
    return lax.dot_general(a, b, (((1,), (0,)), ((), ())), preferred_element_type=f32)


def dot_nt(a, b):
    return lax.dot_general(a, b, (((1,), (1,)), ((), ())), preferred_element_type=f32)


def dot_tn(a, b):
    return lax.dot_general(a, b, (((0,), (0,)), ((), ())), preferred_element_type=f32)


def dot_exact(a, b):
    return lax.dot_general(
        a, b, (((1,), (0,)), ((), ())), precision=highest, preferred_element_type=f32
    )


def sigmoid(v):
    return 1.0 / (1.0 + jnp.exp(-v))


def block_place(block, members):
    quarter, at = block // members, block % members
    if quarter < 2:
        return at, 0, quarter
    return members - 1 - at, 1, 3 - quarter


class Plan:
    def __init__(self, seq_len, block_len, heads, lanes):
        self.seq_len = seq_len
        self.block_len = block_len
        self.heads = heads
        self.lanes = lanes
        self.width = heads * lanes
        self.members = seq_len // (4 * block_len)
        self.chunk = 4 * block_len
        self.chunks = seq_len // self.chunk
        self.query_parts = self.members // 2
        self.query_rows = seq_len // self.query_parts
        self.bc = 2 * N
        self.key_at = self.bc
        self.value_at = self.bc + HD
        self.q_at = self.bc + 2 * HD
        self.gate_at = self.bc + 3 * HD
        self.pair_cols = 2 * self.width
        self.pair_tiles = self.pair_cols + -self.pair_cols % 128
        self.step_at = self.gate_at + self.pair_tiles
        self.cols = self.step_at + 128

    def rows(self, core, block):
        member, half, place = block_place(block, self.members)
        other = core if place == 0 else 1 - core
        start = other * (self.seq_len // 2) + (2 * member + half) * self.block_len
        return pl.ds(pl.multiple_of(start, 16), self.block_len)

    def blocks(self):
        return range(self.seq_len // self.block_len)


def head_masks(plan):
    lane = lax.broadcasted_iota(jnp.int32, (1, plan.width), 1)
    return [
        ((lane >= h * plan.lanes) & (lane < (h + 1) * plan.lanes)).astype(f32)
        for h in range(plan.heads)
    ]


def over_heads(plan, tile, masks):
    return sum(tile[:, h : h + 1] * masks[h] for h in range(plan.heads))


def per_head(plan, values, masks):
    lane = lax.broadcasted_iota(jnp.int32, (1, 128), 1)
    total = None
    for h in range(plan.heads):
        column = jnp.sum(values * masks[h], axis=1, keepdims=True)
        part = column * (lane == h).astype(f32)
        total = part if total is None else total + part
    return total


def conv_values(source, taps_ref, rows, start, low, high):
    total = taps_ref[CONV : CONV + 1, low:high]
    for k in range(CONV):
        at = PAD + start - (CONV - 1) + k
        total = total + taps_ref[k : k + 1, low:high] * source[pl.ds(at, rows), low:high]
    return total


def prepare(plan, core, mixed, nat_bc, nat_x, nat_step):
    width = plan.width
    nat_bc[0:PAD, :] = jnp.zeros((PAD, plan.bc), f32)
    nat_x[0:PAD, :] = jnp.zeros((PAD, width), f32)
    for block in plan.blocks():
        at = PAD + block * plan.block_len
        rows = plan.rows(core, block)
        nat_bc[pl.ds(at, plan.block_len), :] = mixed[rows, 0 : plan.bc]
        pair = mixed[rows, plan.gate_at : plan.gate_at + plan.pair_tiles]
        nat_x[pl.ds(at, plan.block_len), :] = pltpu.roll(pair, plan.pair_tiles - width, 1)[:, :width]
        nat_step[pl.ds(at - PAD, plan.block_len), :] = mixed[rows, plan.step_at : plan.step_at + 128]


def chunk_decays(plan, nat_step, head_rows, c, tri):
    q = plan.chunk
    real = lax.broadcasted_iota(jnp.int32, (1, 128), 1) < plan.heads
    raw = jnp.where(real, nat_step[pl.ds(c * q, q), :] + head_rows[1:2, :], 0.0)
    step = jnp.where(real, jnp.maximum(raw, 0.0) + jnp.log(1.0 + jnp.exp(-jnp.abs(raw))), 0.0)
    cumulative = dot_exact(tri, step * head_rows[0:1, :])
    return raw, step, cumulative


def triangle(plan):
    q = plan.chunk
    row = lax.broadcasted_iota(jnp.int32, (q, q), 0)
    col = lax.broadcasted_iota(jnp.int32, (q, q), 1)
    return row, col


def ssm_forward(plan, core_ref, mixed, taps, shared_taps, head_rows, y_out, low_out, states_out, squares_out,
                nat_bc, nat_x, nat_step):
    q = plan.chunk
    masks = head_masks(plan)
    core = core_ref[0]
    prepare(plan, core, mixed, nat_bc, nat_x, nat_step)
    row, col = triangle(plan)
    lower = row >= col
    tri = lower.astype(f32)
    state = jnp.zeros((N, plan.width), f32)
    for c in range(plan.chunks):
        start = c * q
        x = conv_values(nat_x, taps, q, start, 0, plan.width)
        x = x * sigmoid(x)
        bc = conv_values(nat_bc, shared_taps, q, start, 0, plan.bc)
        bc = (bc * sigmoid(bc)).astype(bf16)
        b, cc = bc[:, :N], bc[:, N:]
        _, step, cum = chunk_decays(plan, nat_step, head_rows, c, tri)
        cum_rows = cum.T
        cum_full = over_heads(plan, cum, masks)
        total_full = cum_full[q - 1 : q, :]
        u = x * over_heads(plan, step, masks)
        inner = dot_nt(cc, b)
        states_out[c] = state
        y = dot_nn(cc, state.astype(bf16)) * jnp.exp(cum_full) + taps[6:7, :] * x
        for h in range(plan.heads):
            seg = jnp.where(lower, cum[:, h : h + 1] - cum_rows[h : h + 1, :], -1e30)
            mixing = (jnp.exp(seg) * inner).astype(bf16)
            y = y + dot_nn(mixing, (u * masks[h]).astype(bf16))
        weighted = (u * jnp.exp(total_full - cum_full)).astype(bf16)
        state = jnp.exp(total_full) * state + dot_tn(b, weighted)
        for k in range(4):
            block = 4 * c + k
            y_out[plan.rows(core, block), :] = y[k * plan.block_len : (k + 1) * plan.block_len, :]
    z = mixed[:, plan.gate_at : plan.gate_at + plan.width]
    gated = y_out[...] * (z * sigmoid(z))
    low_out[...] = (gated * taps[5:6, :]).astype(bf16)
    squares_out[...] = lax.dot_general(
        jnp.ones((8, plan.width), f32), gated * gated, (((1,), (1,)), ((), ())),
        precision=highest, preferred_element_type=f32,
    )


def ssm_backward(plan, core_ref, mixed, taps, shared_taps, head_rows, y_in, states, grad_mixer, scales,
                 bc_out, pair_out, step_out, taps_out, shared_out, heads_out,
                 nat_bc, nat_x, nat_step, nat_dy, grad_x, grad_bc, grad_y_ref):
    q = plan.chunk
    width = plan.width
    masks = head_masks(plan)
    core = core_ref[0]
    prepare(plan, core, mixed, nat_bc, nat_x, nat_step)
    row, col = triangle(plan)
    lower, upper = row >= col, row <= col
    strict_lower, strict_upper = row > col, row < col
    tri, tri_back = lower.astype(f32), upper.astype(f32)

    z = mixed[:, plan.gate_at : plan.gate_at + width]
    y = y_in[...]
    sig = sigmoid(z)
    silu = z * sig
    gated = y * silu
    scaled = grad_mixer[:, HD : HD + width] * scales[:, 0:1]
    grad_gated = scaled * taps[5:6, :] + scales[:, 1:2] * gated
    gain_grad = jnp.sum(scaled * gated, axis=0, keepdims=True)
    grad_z = grad_gated * y * (sig * (1.0 + z * (1.0 - sig)))
    spare = plan.pair_tiles - width
    pair_out[...] = jnp.concatenate(
        [grad_z, jnp.zeros((plan.seq_len, spare), f32)], axis=1
    ).astype(bf16)
    grad_y_ref[...] = grad_gated * silu
    for block in plan.blocks():
        at = block * plan.block_len
        nat_dy[pl.ds(at, plan.block_len), :] = grad_y_ref[plan.rows(core, block), :]

    grad_x[plan.seq_len : plan.seq_len + PAD, :] = jnp.zeros((PAD, width), f32)
    grad_bc[plan.seq_len : plan.seq_len + PAD, :] = jnp.zeros((PAD, plan.bc), f32)
    grad_state = jnp.zeros((N, width), f32)
    skip_grad = jnp.zeros((1, width), f32)
    rate_grad = jnp.zeros((1, 128), f32)
    bias_grad = jnp.zeros((1, 128), f32)
    for c in reversed(range(plan.chunks)):
        start = c * q
        x_lin = conv_values(nat_x, taps, q, start, 0, width)
        x_sig = sigmoid(x_lin)
        x = x_lin * x_sig
        bc_lin = conv_values(nat_bc, shared_taps, q, start, 0, plan.bc)
        bc_sig = sigmoid(bc_lin)
        bc = (bc_lin * bc_sig).astype(bf16)
        b, cc = bc[:, :N], bc[:, N:]
        raw, step, cum = chunk_decays(plan, nat_step, head_rows, c, tri)
        cum_rows = cum.T
        cum_full = over_heads(plan, cum, masks)
        total_full = cum_full[q - 1 : q, :]
        step_full = over_heads(plan, step, masks)
        u = x * step_full
        u_low = u.astype(bf16)
        dy = nat_dy[pl.ds(start, q), :]
        dy_low = dy.astype(bf16)
        state = states[c]
        state_low = state.astype(bf16)
        grad_state_low = grad_state.astype(bf16)
        entry = jnp.exp(cum_full)
        exit_w = jnp.exp(total_full - cum_full)
        total_decay = jnp.exp(total_full)
        dy_entry = (dy * entry).astype(bf16)
        grad_c = dot_nt(dy_entry, state_low)
        carried = dot_nn(cc, state_low) * entry
        du_state = dot_nn(b, grad_state_low) * exit_w
        grad_b = dot_nt((u * exit_w).astype(bf16), grad_state_low)
        inner = dot_nt(cc, b)
        inner_t = dot_nt(b, cc)
        du = du_state
        grad_inner = jnp.zeros((q, q), f32)
        grad_inner_t = jnp.zeros((q, q), f32)
        lane = lax.broadcasted_iota(jnp.int32, (1, 128), 1)
        dcum = per_head(plan, dy * carried - u * du_state, masks)
        for h in range(plan.heads):
            here = (lane == h).astype(f32)
            u_head = (u * masks[h]).astype(bf16)
            dy_head = (dy * masks[h]).astype(bf16)
            seg = cum[:, h : h + 1] - cum_rows[h : h + 1, :]
            decay = jnp.exp(jnp.where(lower, seg, -1e30))
            decay_t = jnp.exp(jnp.where(upper, -seg, -1e30))
            grad_mix = dot_nt(dy_head, u_low) * decay
            grad_mix_t = dot_nt(u_head, dy_low) * decay_t
            grad_inner = grad_inner + grad_mix
            grad_inner_t = grad_inner_t + grad_mix_t
            du = du + dot_nn((decay_t * inner_t).astype(bf16), dy_head)
            out_sum = jnp.sum(jnp.where(strict_lower, grad_mix * inner, 0.0), axis=1, keepdims=True)
            in_sum = jnp.sum(
                jnp.where(strict_upper, grad_mix_t * inner_t, 0.0), axis=1, keepdims=True
            )
            dcum = dcum + (out_sum - in_sum) * here
        grad_c = grad_c + dot_nn(grad_inner.astype(bf16), b)
        grad_b = grad_b + dot_nn(grad_inner_t.astype(bf16), cc)
        whole = jnp.sum(u * du_state, axis=0, keepdims=True) + jnp.sum(
            grad_state * state, axis=0, keepdims=True
        ) * total_decay
        dlog = dot_exact(tri_back, dcum) + per_head(plan, whole, masks)
        rate_grad = rate_grad + jnp.sum(dlog * step, axis=0, keepdims=True)
        grad_step = dlog * head_rows[0:1, :] + per_head(plan, du * x, masks)
        grad_raw = grad_step * sigmoid(raw)
        bias_grad = bias_grad + jnp.sum(grad_raw, axis=0, keepdims=True)
        grad_xc = du * step_full + taps[6:7, :] * dy
        skip_grad = skip_grad + jnp.sum(dy * x, axis=0, keepdims=True)
        grad_state = total_decay * grad_state + dot_tn(cc, dy_entry)
        grad_x[pl.ds(start, q), :] = grad_xc * (x_sig * (1.0 + x_lin * (1.0 - x_sig)))
        grad_bc[pl.ds(start, q), :] = jnp.concatenate([grad_b, grad_c], axis=1) * (
            bc_sig * (1.0 + bc_lin * (1.0 - bc_sig))
        )
        for k in range(4):
            step_out[plan.rows(core, 4 * c + k), :] = grad_raw[
                k * plan.block_len : (k + 1) * plan.block_len, :
            ].astype(bf16)

    size = plan.block_len
    tap_grads = [jnp.zeros((1, width), f32) for _ in range(CONV + 1)]
    shared_grads = [jnp.zeros((1, plan.bc), f32) for _ in range(CONV + 1)]
    lane = lax.broadcasted_iota(jnp.int32, (1, plan.pair_tiles), 1)
    for c in range(plan.chunks):
        start = c * q
        dx = grad_x[pl.ds(start, q), :]
        dbc = grad_bc[pl.ds(start, q), :]
        tap_grads[CONV] += jnp.sum(dx, axis=0, keepdims=True)
        shared_grads[CONV] += jnp.sum(dbc, axis=0, keepdims=True)
        pre_dx = None
        pre_dbc = None
        for k in range(CONV):
            at = PAD + start - (CONV - 1) + k
            tap_grads[k] += jnp.sum(dx * nat_x[pl.ds(at, q), :], axis=0, keepdims=True)
            shared_grads[k] += jnp.sum(dbc * nat_bc[pl.ds(at, q), :], axis=0, keepdims=True)
            ahead = start + (CONV - 1) - k
            part = taps[k : k + 1, :] * grad_x[pl.ds(ahead, q), :]
            pre_dx = part if k == 0 else pre_dx + part
            part = shared_taps[k : k + 1, :] * grad_bc[pl.ds(ahead, q), :]
            pre_dbc = part if k == 0 else pre_dbc + part
        tile = jnp.concatenate([pre_dx, jnp.zeros((q, spare), f32)], axis=1)
        tile = pltpu.roll(tile, width, 1).astype(bf16)
        for k in range(4):
            rows = plan.rows(core, 4 * c + k)
            pair_out[rows, :] = jnp.where(
                lane < width, pair_out[rows, :], tile[k * size : (k + 1) * size, :]
            )
            bc_out[rows, :] = pre_dbc[k * size : (k + 1) * size, :].astype(bf16)
    for k in range(CONV + 1):
        taps_out[k : k + 1, :] = tap_grads[k]
        shared_out[k : k + 1, :] = shared_grads[k]
    taps_out[5:6, :] = gain_grad
    taps_out[6:7, :] = skip_grad
    heads_out[0:1, :] = rate_grad * head_rows[0:1, :]
    heads_out[1:2, :] = bias_grad


def whole_specs(arrays):
    def spec(array):
        zeros = (0,) * len(array.shape)
        return pl.BlockSpec(array.shape, lambda i: zeros, pipeline_mode=pl.Buffered(1))

    return [spec(array) for array in arrays]


def call_whole(plan, kernel, outs, scratch, flops, inputs, scalars=()):
    return pl.pallas_call(
        kernel,
        grid=(1,),
        in_specs=[pl.BlockSpec(memory_space=pltpu.SMEM) for _ in scalars] + whole_specs(inputs),
        out_specs=tuple(whole_specs(outs)),
        out_shape=tuple(outs),
        scratch_shapes=scratch,
        compiler_params=ssm_params(plan),
        cost_estimate=pl.CostEstimate(
            flops=flops, bytes_accessed=plan.seq_len * 8192, transcendentals=0
        ),
    )(*scalars, *inputs)


def ssm_params(plan):
    limit = 30 * 2**20 if plan.seq_len <= 768 else 58 * 2**20
    return pltpu.CompilerParams(vmem_limit_bytes=limit)


def run_forward(plan, core, *inputs):
    t, w = plan.seq_len, plan.width
    outs = [
        jax.ShapeDtypeStruct((t, w), f32),
        jax.ShapeDtypeStruct((t, w), bf16),
        jax.ShapeDtypeStruct((plan.chunks, N, w), f32),
        jax.ShapeDtypeStruct((8, t), f32),
    ]
    scratch = [
        pltpu.VMEM((PAD + t, plan.bc), f32),
        pltpu.VMEM((PAD + t, w), f32),
        pltpu.VMEM((t, 128), f32),
    ]
    return call_whole(
        plan, functools.partial(ssm_forward, plan), outs, scratch, 40000 * t * w, inputs, (core,)
    )


def run_backward(plan, core, *inputs):
    t, w = plan.seq_len, plan.width
    outs = [
        jax.ShapeDtypeStruct((t, plan.bc), bf16),
        jax.ShapeDtypeStruct((t, plan.pair_tiles), bf16),
        jax.ShapeDtypeStruct((t, 128), bf16),
        jax.ShapeDtypeStruct((8, w), f32),
        jax.ShapeDtypeStruct((8, plan.bc), f32),
        jax.ShapeDtypeStruct((8, 128), f32),
    ]
    scratch = [
        pltpu.VMEM((PAD + t, plan.bc), f32),
        pltpu.VMEM((PAD + t, w), f32),
        pltpu.VMEM((t, 128), f32),
        pltpu.VMEM((t, w), f32),
        pltpu.VMEM((t + PAD, w), f32),
        pltpu.VMEM((t + PAD, plan.bc), f32),
        pltpu.VMEM((t, w), f32),
    ]
    return call_whole(
        plan, functools.partial(ssm_backward, plan), outs, scratch, 90000 * t * w, inputs, (core,)
    )


def attend_scores(plan, queries, keys, query_pos, key_pos):
    scores = dot_nt(queries, keys) * HD ** (-0.5)
    return jnp.where(key_pos <= query_pos, scores, -1e30)


def turned(x, cosine, sine):
    return x * cosine + pltpu.roll(x, HD // 2, 1) * sine


def attend_forward(plan, part, mixed, cosine, sine, query_pos, key_pos,
                   att_out, log_out, q_out, kv_out):
    rows = pl.ds(pl.multiple_of(part[0] * plan.query_rows, 8), plan.query_rows)
    keys = turned(mixed[:, plan.key_at : plan.key_at + HD], cosine[...], sine[...]).astype(bf16)
    values = mixed[:, plan.value_at : plan.value_at + HD].astype(bf16)
    kv_out[:, :HD] = keys
    kv_out[:, HD:] = values
    queries = mixed[rows, plan.q_at : plan.q_at + HD]
    queries = turned(queries, cosine[rows, :], sine[rows, :]).astype(bf16)
    q_out[...] = queries
    scores = attend_scores(plan, queries, keys, query_pos[rows, :], key_pos[...])
    peak = jnp.max(scores, axis=1, keepdims=True)
    weights = jnp.exp(scores - peak)
    total = jnp.sum(weights, axis=1, keepdims=True)
    probs = (weights / total).astype(bf16)
    att_out[...] = jnp.zeros((plan.seq_len, HD), bf16)
    att_out[rows, :] = dot_nn(probs, values).astype(bf16)
    log_out[...] = peak + jnp.log(total)


def attend_backward(plan, part, queries, kv, logs, grad_mixer, cosine, sine, query_pos, key_pos,
                    q_out, kv_out):
    rows = pl.ds(pl.multiple_of(part[0] * plan.query_rows, 8), plan.query_rows)
    keys, values = kv[:, :HD], kv[:, HD:]
    scale = HD ** (-0.5)
    q, grad = queries[...], grad_mixer[rows, :HD].astype(bf16)
    probs = jnp.exp(attend_scores(plan, q, keys, query_pos[rows, :], key_pos[...]) - logs[...])
    grad_probs = dot_nt(grad, values)
    inner = jnp.sum(probs * grad_probs, axis=1, keepdims=True)
    grad_scores = (probs * (grad_probs - inner)).astype(bf16)
    grad_q = dot_nn(grad_scores, keys) * scale
    q_out[...] = jnp.zeros((plan.seq_len, HD), bf16)
    q_out[rows, :] = turned(grad_q, cosine[rows, :], -sine[rows, :]).astype(bf16)
    grad_k = dot_tn(grad_scores, q) * scale
    kv_out[:, :HD] = turned(grad_k, cosine[...], -sine[...]).astype(bf16)
    kv_out[:, HD:] = dot_tn(probs.astype(bf16), grad).astype(bf16)


def run_attend(plan, part, *inputs):
    t, rows = plan.seq_len, plan.query_rows
    outs = [
        jax.ShapeDtypeStruct((t, HD), bf16),
        jax.ShapeDtypeStruct((rows, 1), f32),
        jax.ShapeDtypeStruct((rows, HD), bf16),
        jax.ShapeDtypeStruct((t, 2 * HD), bf16),
    ]
    kernel = functools.partial(attend_forward, plan)
    return call_whole(plan, kernel, outs, [], 4 * rows * t * HD, inputs, (part,))


def run_attend_back(plan, part, *inputs):
    t = plan.seq_len
    outs = [jax.ShapeDtypeStruct((t, HD), bf16), jax.ShapeDtypeStruct((t, 2 * HD), bf16)]
    kernel = functools.partial(attend_backward, plan)
    return call_whole(plan, kernel, outs, [], 10 * plan.query_rows * t * HD, inputs, (part,))


def build(ctx_axes, tp_axes):
    half_axis = ctx_axes[0]
    group_axes = ctx_axes[1:]
    t_half, t_core = tp_axes
    ring_axes = group_axes + (t_half,)
    slot_axes = group_axes + tp_axes
    all_axes = ctx_axes + tp_axes
    span = len(ring_axes)

    def column_parts(width):
        unit = width // 128
        marks = [0] + [128 * (unit * (k + 1) // 3) for k in range(3)]
        return list(zip(marks[:-1], marks[1:]))

    def rotated(part):
        turn = part % span
        return ring_axes[turn:] + ring_axes[:turn]

    def gather_rows(x):
        rows, width = x.shape
        parts = []
        for part, (low, high) in enumerate(column_parts(width)):
            held = x[:, low:high].reshape((1,) * span + (rows, high - low))
            for axis in rotated(part):
                dim = ring_axes.index(axis)
                got = lax.ppermute(held, axis, SWAP)
                first = lax.axis_index(axis) == 0
                held = jnp.where(
                    first, jnp.concatenate([held, got], dim), jnp.concatenate([got, held], dim)
                )
            parts.append(held)
        held = lax.optimization_barrier(jnp.concatenate(parts, -1).reshape(-1, width))
        return jnp.concatenate([held, lax.ppermute(held, t_core, SWAP)])

    def scatter_product(left, right, extra=None):
        total = left.shape[0]
        width = right.shape[0]
        peers = 2 ** (span + 1)
        rows = total // peers
        own = total // 2
        sent = matmul_nt(left[own:], right).astype(bf16)
        kept = matmul_nt(left[:own], right)
        if extra is not None:
            width += extra.shape[1]
            sent = jnp.concatenate([sent, extra[own:]], axis=1)
            kept = jnp.concatenate([kept, extra[:own].astype(f32)], axis=1)
        held = kept + lax.ppermute(sent, t_core, SWAP).astype(f32)
        parts = []
        for part, (low, high) in enumerate(column_parts(width)):
            piece = held[:, low:high].reshape((2,) * span + (rows, high - low))
            names = list(ring_axes)
            for axis in rotated(part):
                dim = names.index(axis)
                names.pop(dim)
                index = lax.axis_index(axis)
                got = lax.ppermute(pick(piece, dim, 1 - index).astype(bf16), axis, SWAP)
                piece = pick(piece, dim, index) + got.astype(f32)
            parts.append(piece)
        return jnp.concatenate(parts, -1)

    def sum_slot(x):
        turn = lax.axis_index(t_core) == 1
        x = x.reshape(2, -1, 128)
        x = jnp.where(turn, x[::-1], x)
        came = lax.all_to_all(
            jnp.broadcast_to(x[None], (2 ** (span + 1),) + x.shape), slot_axes, 0, 0, tiled=True
        )
        x = jnp.sum(came, axis=0)
        return jnp.where(turn, x[::-1], x).reshape(-1, 1)

    def sum_over(x, axes):
        for axis in axes:
            x = x + lax.ppermute(x, axis, SWAP)
        return x

    def group_index():
        return lax.axis_index(group_axes)

    def group_swap(blocks):
        return lax.all_to_all(blocks, group_axes, 0, 0, tiled=True)

    def both_halves(came):
        return lax.all_gather(came, half_axis, axis=0, tiled=True)

    def spread_first(blocks):
        return lax.all_to_all(jnp.concatenate([blocks, blocks]), ctx_axes, 0, 0, tiled=True)

    def fold_halves(blocks):
        return lax.psum_scatter(blocks.astype(bf16), half_axis, scatter_dimension=0, tiled=True)

    def fold_last(blocks):
        half = lax.axis_index(half_axis)
        paired = blocks.reshape((2, blocks.shape[0] // 2) + blocks.shape[1:])
        got = lax.ppermute(pick(paired, 0, 1 - half).astype(bf16), half_axis, SWAP)
        return pick(paired, 0, half).astype(f32), got

    def gather_lanes(x):
        for axis in ctx_axes[::-1]:
            got = lax.ppermute(x, axis, SWAP)
            first = lax.axis_index(axis) == 0
            x = jnp.where(first, jnp.concatenate([x, got], -1), jnp.concatenate([got, x], -1))
        return x

    def local(
        hidden,
        cotangent,
        lengths,
        norm_gains,
        mix_weight,
        share_weight,
        chan_params,
        shared_conv,
        head_params,
        out_weight,
        up_weight,
        down_weight,
    ):
        members = 2 ** len(group_axes)
        ctx_count = 2 * members
        replicas = members // HGROUPS
        slot = lax.axis_index(half_axis)
        me = group_index()
        head_group = me // replicas
        head_part = me % replicas
        tp_half = lax.axis_index(t_half)
        tp_core = lax.axis_index(t_core)
        tp_index = tp_half * 2 + tp_core
        block_len = hidden.shape[2]
        depth = mix_weight.shape[1]
        seq_len = 2 * ctx_count * block_len
        own_len = 4 * block_len
        tp_heads = chan_params.shape[2] // P_SIZE
        heads = tp_heads // HGROUPS
        lanes = P_SIZE // replicas
        width = heads * lanes
        ssm_cols = tp_heads * P_SIZE
        qheads = AH // 4
        q_cols = qheads * HD
        ff_tp = FF // 4
        ff_own = ff_tp // members
        plan = Plan(seq_len, block_len, heads, lanes)
        own_head = me // plan.query_parts
        core_scalar = tp_core.astype(jnp.int32).reshape(1)
        query_part = (me % plan.query_parts).astype(jnp.int32).reshape(1)
        share_cols = share_weight.shape[2]
        kv_cols = 2 * N
        dt_cols = 2 * N + 2 * KVH * HD
        kv_head = tp_index * qheads // (AH // KVH)
        score_scale = HD ** (-0.5)

        def block_of(member, half, cube):
            near = cube * members + member
            return jnp.where(half == 0, near, 2 * ctx_count - 1 - near)

        within = jnp.arange(block_len)
        own_pos = block_of(me, tp_half, tp_core) * block_len + within
        own_valid = (own_pos < lengths[slot]).astype(f32)[:, None]
        ring = jnp.arange(2 * members)

        def core_positions(core):
            first = block_of(ring // 2, ring % 2, core) * block_len
            return (first[:, None] + within[None, :]).reshape(-1)

        key_pos = jnp.concatenate([core_positions(tp_core), core_positions(1 - tp_core)])
        half_dim = HD // 2
        inverse = jnp.exp(-jnp.log(rope_base) * (2.0 * jnp.arange(half_dim, dtype=f32) / HD))
        angles = key_pos.astype(f32)[:, None] * inverse
        cosine = jnp.concatenate([jnp.cos(angles)] * 2, axis=1)
        sine = jnp.concatenate([-jnp.sin(angles), jnp.sin(angles)], axis=1)

        tables = (cosine, sine, key_pos[:, None], key_pos[None, :])

        def cut_query_heads(x, axis):
            shape = x.shape
            split = x.reshape(shape[:axis] + (qheads, HD) + shape[axis + 1 :])
            return jnp.repeat(jnp.moveaxis(split, axis, 0), plan.query_parts, axis=0)

        def join_query_heads(x, axis):
            summed = jnp.sum(x.astype(f32).reshape((qheads, plan.query_parts) + x.shape[1:]), axis=1)
            joined = jnp.moveaxis(summed, 0, axis)
            shape = joined.shape
            return joined.reshape(shape[:axis] + (q_cols,) + shape[axis + 2 :])

        def bring_in(x):
            got = lax.ppermute(
                pick(pick(x, 0, 1 - slot), 0, tp_half), (half_axis, t_core), [(0, 2), (3, 1)]
            )
            return jnp.where(tp_core == slot, pick(pick(x, 0, slot), 0, tp_half), got)

        def bring_out(x, points=None):
            x = x.astype(bf16)
            got = lax.ppermute(x, (half_axis, t_core), [(1, 3), (2, 0)])
            if points is not None:
                got = after(got, points[0])
            pair = jnp.where(slot == 0, jnp.stack([x, got]), jnp.stack([got, x]))
            other = lax.ppermute(pair, t_core, SWAP)
            pair = jnp.where(tp_core == slot, pair, other)
            other = lax.ppermute(pair, t_half, SWAP)
            if points is not None:
                other = after(other, points[1])
            both = jnp.where(tp_half == 0, jnp.stack([pair, other], 1), jnp.stack([other, pair], 1))
            return both.astype(f32)

        def cut_heads(x, axis):
            shape = x.shape
            split = x.reshape(
                shape[:axis] + (HGROUPS, heads, replicas, lanes) + shape[axis + 1 :]
            )
            split = jnp.moveaxis(split, (axis, axis + 2), (0, 1))
            return split.reshape((members,) + shape[:axis] + (width,) + shape[axis + 1 :])

        def join_heads(x, axis):
            if replicas == 1:
                return jnp.concatenate([x[g] for g in range(members)], axis=axis)
            shape = x.shape[1:]
            split = x.reshape(
                (HGROUPS, replicas) + shape[:axis] + (heads, lanes) + shape[axis + 1 :]
            )
            split = jnp.moveaxis(split, (0, 1), (axis, axis + 2))
            return split.reshape(shape[:axis] + (ssm_cols,) + shape[axis + 1 :])

        gains = gather_lanes(norm_gains).astype(f32)
        hidden_rows = bring_in(after(hidden, gains))
        stream = hidden_rows.astype(f32)
        own_chan = pick(cut_heads(chan_params, 2), 0, me)
        own_heads = pick(head_params.reshape(LAYERS, 3, HGROUPS, heads), 2, head_group)
        skip_full = jnp.repeat(own_heads[:, 2], lanes, axis=1)[:, None]
        tap_rows = jnp.concatenate([own_chan, skip_full, jnp.zeros_like(skip_full)], axis=1)
        shared_rows = jnp.pad(shared_conv, ((0, 0), (0, 3), (0, 0)))
        head_rows = jnp.pad(
            jnp.stack([-jnp.exp(own_heads[:, 0]), own_heads[:, 1]], axis=1),
            ((0, 0), (0, 6), (0, 128 - heads)),
        )
        share_rows = lax.dynamic_slice_in_dim(share_weight, tp_core * (depth // 2), depth // 2, 1)
        dt_start = dt_cols + tp_index * tp_heads + head_group * heads

        def weight_blocks(layer):
            mix = mix_weight[layer]
            mix_blocks = jnp.concatenate(
                [
                    cut_query_heads(mix[:, 2 * ssm_cols :], 1),
                    cut_heads(mix[:, :ssm_cols], 1),
                    cut_heads(mix[:, ssm_cols : 2 * ssm_cols], 1),
                ],
                2,
            )
            out = out_weight[layer].T
            out_blocks = jnp.concatenate(
                [cut_query_heads(out[:, ssm_cols:], 1), cut_heads(out[:, :ssm_cols], 1)], 2
            )
            up = up_weight[layer]
            down = down_weight[layer].T
            ffn_blocks = jnp.stack(
                [
                    jnp.concatenate(
                        [
                            up[:, g * ff_own : (g + 1) * ff_own],
                            up[:, ff_tp + g * ff_own : ff_tp + (g + 1) * ff_own],
                            down[:, g * ff_own : (g + 1) * ff_own],
                        ],
                        axis=1,
                    )
                    for g in range(members)
                ]
            )
            return mix_blocks, out_blocks, ffn_blocks

        def share_whole(share):
            share = jnp.concatenate(
                [
                    share[:, :kv_cols],
                    lax.dynamic_slice_in_dim(share, kv_cols + kv_head * HD, HD, 1),
                    lax.dynamic_slice_in_dim(share, kv_cols + (KVH + kv_head) * HD, HD, 1),
                    share[:, dt_cols:],
                ],
                axis=1,
            )
            return lax.all_gather(share, ctx_axes + (t_core,), axis=0, tiled=True)

        def input_weights(mix_own, share):
            dt_w = lax.dynamic_slice_in_dim(share, kv_cols + 2 * HD + dt_start - dt_cols, heads, 1)
            return jnp.concatenate(
                [
                    share[:, : plan.q_at],
                    jnp.pad(
                        mix_own.reshape(D, HD + 2 * width),
                        ((0, 0), (0, plan.pair_tiles - plan.pair_cols)),
                    ),
                    jnp.pad(dt_w, ((0, 0), (0, 128 - heads))),
                ],
                axis=1,
            )

        def ffn_weights(ffn_own):
            ffn_own = ffn_own.reshape(D, 3 * ff_own)
            return ffn_own[:, : 2 * ff_own], ffn_own[:, 2 * ff_own :]

        blocks = [weight_blocks(layer) for layer in range(LAYERS)]
        mix_own = [None] * LAYERS
        out_own = [None] * LAYERS
        ffn_own = [None] * LAYERS
        shares = [None] * LAYERS
        blocks = after(blocks, hidden_rows)
        mix_own[0] = spread_first(blocks[0][0])
        swapped = [[group_swap(x) for x in blocks[layer][layer == 0 :]] for layer in range(LAYERS)]
        for layer in range(LAYERS):
            if layer > 0:
                mix_own[layer] = both_halves(swapped[layer][0])
            shares[layer] = share_whole(share_rows[layer])
            out_own[layer] = both_halves(swapped[layer][-2])
            ffn_own[layer] = both_halves(swapped[layer][-1])

        records = []
        for layer in range(LAYERS):
            rec = {}
            normed_f, rec["norm_one_back"] = jax.vjp(norm_piece, stream, gains[layer, 0])
            if layer == 0:
                normed = norm_piece(gather_rows(hidden_rows).astype(f32), gains[0, 0]).astype(bf16)
            else:
                normed = gather_rows(normed_f.astype(bf16))
            in_w = input_weights(*after((mix_own[layer], shares[layer]), normed))
            mixed = matmul(normed, in_w)
            ssm_y, gated_low, states, squares = run_forward(
                plan, core_scalar, mixed, tap_rows[layer], shared_rows[layer], head_rows[layer]
            )
            sum_squares = sum_slot(squares[0])
            gated_scale = lax.rsqrt(sum_squares / (MH * P_SIZE) + eps_norm)
            scaled_low = (gated_low.astype(f32) * gated_scale).astype(bf16)
            attended, logsum, queries, keyval = run_attend(plan, query_part, mixed, *tables)
            mixer = jnp.concatenate([attended, scaled_low], axis=1)
            out_w = after(out_own[layer], gated_low).reshape(D, HD + width)
            middle = stream + scatter_product(mixer, out_w)
            normed_two_f, rec["norm_two_back"] = jax.vjp(norm_piece, middle, gains[layer, 1])
            normed_two = gather_rows(normed_two_f.astype(bf16))
            up_w, down_w = ffn_weights(after(ffn_own[layer], normed_two))
            gate_up = matmul(normed_two, up_w)
            gate_vals, up_vals = gate_up[:, :ff_own], gate_up[:, ff_own:]
            activation = (jax.nn.silu(gate_vals) * up_vals).astype(bf16)
            stream = (middle + scatter_product(activation, down_w)) * own_valid
            rec.update(
                normed=normed, mixed=mixed, ssm_y=ssm_y, gated_low=gated_low, states=states,
                mixer=mixer, gated_scale=gated_scale, queries=queries, keyval=keyval,
                logsum=logsum, normed_two=normed_two,
                gate_vals=gate_vals, up_vals=up_vals, activation=activation,
            )
            rec["weights"] = (in_w, out_w, up_w, down_w)
            records.append(rec)

        grad_stream = bring_in(cotangent).astype(f32)
        out_grads = [None] * LAYERS
        share_sums = []
        folded = [None] * LAYERS
        points = []
        came = [[] for _ in range(LAYERS)]
        for layer in reversed(range(LAYERS)):
            rec = records[layer]
            in_w, out_w, up_w, down_w = rec["weights"]
            grad_masked = grad_stream * own_valid
            if layer == LAYERS - 1:
                grad_ffn = gather_rows(grad_masked.astype(bf16))
            else:
                gathered = jnp.concatenate([grad_masked, share_own], axis=1).astype(bf16)
                gathered = gather_rows(after(gathered, folded[layer + 1][1]))
                grad_ffn = gathered[:, :D]
                share_sums.append(gathered[:, D:])
            points.append([grad_ffn])
            grad_activation = matmul(grad_ffn, down_w)
            grad_down = product_tn(grad_ffn, rec["activation"])
            gate_vals = rec["gate_vals"]
            grad_gate = grad_activation * rec["up_vals"] * silu_grad(gate_vals)
            grad_upper = grad_activation * jax.nn.silu(gate_vals)
            grad_gate_up = jnp.concatenate([grad_gate, grad_upper], axis=1).astype(bf16)
            if layer + 1 < LAYERS:
                came[layer + 1].append(
                    after(group_swap(after(folded[layer + 1][0], grad_ffn)), grad_gate_up)
                )
            grad_upw = product_tn(rec["normed_two"], grad_gate_up)
            grad_normed_two = scatter_product(grad_gate_up, up_w)
            grad_middle_norm, grad_gain_two = rec["norm_two_back"](grad_normed_two)
            grad_middle = grad_masked + grad_middle_norm
            ffn_blocks = jnp.concatenate([grad_upw, grad_down], axis=1).reshape(
                ctx_count, depth, 3 * ff_own
            )
            folded[layer] = [fold_halves(ffn_blocks)]
            branch_rows = gather_rows(after(grad_middle.astype(bf16), ffn_blocks))
            points[-1].append(branch_rows)
            grad_mixer = matmul(branch_rows, out_w)
            out_blocks = product_tn(branch_rows, rec["mixer"]).reshape(
                ctx_count, depth, HD + width
            )
            folded[layer].append(fold_halves(out_blocks))
            gated_scale = rec["gated_scale"]
            scale_part = jnp.sum(grad_mixer[:, HD:] * rec["gated_low"].astype(f32), axis=-1)
            grad_scale = after(sum_slot(scale_part), out_blocks)
            grad_squares = grad_scale * -0.5 * gated_scale * gated_scale * gated_scale / (MH * P_SIZE)
            grad_mixer_here = grad_mixer
            if layer + 1 < LAYERS:
                earlier = after(folded[layer + 1][1:], branch_rows)
                came[layer + 1] += [group_swap(x) for x in earlier]
                grad_mixer_here = after(grad_mixer, came[layer + 1][1:])
            grad_q, grad_kv = run_attend_back(
                plan, query_part, rec["queries"], rec["keyval"], rec["logsum"], grad_mixer_here,
                *tables,
            )
            grad_bc, grad_pair, grad_step, taps_grad, grad_conv, heads_grad = run_backward(
                plan, core_scalar, rec["mixed"], tap_rows[layer], shared_rows[layer], head_rows[layer],
                rec["ssm_y"], rec["states"], grad_mixer,
                jnp.concatenate([gated_scale, 2.0 * grad_squares], axis=1),
            )
            chan_grad = taps_grad[: CONV + 2]
            grad_conv = grad_conv[: CONV + 1]
            grad_heads = jnp.concatenate(
                [heads_grad[:2, :heads], jnp.sum(taps_grad[6].reshape(heads, lanes), axis=1)[None]]
            )
            grad_mix_own = jnp.concatenate([grad_q, grad_pair], axis=1)
            grad_in = jnp.concatenate([grad_bc, grad_kv, grad_mix_own, grad_step], axis=1)
            grad_in = after(grad_in, folded[layer][0])
            at_heads = [
                jnp.where(kv_head == head, grad_kv[:, part * HD : (part + 1) * HD], 0)
                for part in range(2)
                for head in range(KVH)
            ]
            step_cols = lax.dynamic_update_slice(
                jnp.zeros((seq_len, 128), bf16), grad_step[:, :heads], (0, dt_start - dt_cols)
            )
            grad_share = jnp.concatenate([grad_bc] + at_heads + [step_cols], axis=1)
            scattered = scatter_product(grad_in, in_w, grad_share)
            grad_normed_one, share_own = scattered[:, :D], scattered[:, D:]
            points[-1] += [grad_in, grad_normed_one]
            grad_stream_norm, grad_gain_one = rec["norm_one_back"](grad_normed_one)
            grad_stream = grad_middle + grad_stream_norm
            grad_mix = product_tn(rec["normed"], grad_mix_own)[:, : HD + 2 * width]
            fold = fold_last if layer == 0 else fold_halves
            folded[layer].append(fold(grad_mix.reshape(ctx_count, depth, HD + 2 * width)))
            out_grads[layer] = (
                jnp.stack([grad_gain_one, grad_gain_two]), chan_grad, grad_conv, grad_heads,
            )
        share_sums.append(gather_rows(share_own.astype(bf16)))
        last = points[-1]
        activations = bring_out(stream, (points[0][1], last[1]))
        share_grads = []
        for layer in range(LAYERS):
            normed = records[layer]["normed"]
            grad_share = share_sums[LAYERS - 1 - layer]
            near = lax.dynamic_slice_in_dim(normed, (slot * members + me) * depth, depth, 1)
            far = lax.dynamic_slice_in_dim(normed, ((1 - slot) * members + me) * depth, depth, 1)
            share_far = lax.ppermute(product_tn(far, grad_share), half_axis, SWAP)
            if layer > 0:
                share_far = after(share_far, last[3])
            share_sum = product_tn(near, grad_share).astype(f32) + share_far.astype(f32)
            share_grads.append(share_sum[:, :share_cols])
        share_g = jnp.stack(share_grads)
        input_grad = bring_out(grad_stream)

        mix_kept, mix_got = folded[0][2]
        mix_sum = (mix_kept + after(mix_got, share_sums[-1]).astype(f32)).astype(bf16)
        came[0] = [
            group_swap(after(folded[0][0], last[3])),
            group_swap(after(folded[0][1], last[3])),
            group_swap(mix_sum),
        ]

        def weight_grads(layer):
            got = came[layer] if layer == 0 else after(came[layer], last[3])
            ffn_came, out_came, mix_came = got
            mix = jnp.concatenate(
                [
                    join_heads(mix_came[:, :, HD : HD + width], 1),
                    join_heads(mix_came[:, :, HD + width :], 1),
                    join_query_heads(mix_came[:, :, :HD], 1),
                ],
                axis=1,
            ).astype(f32)
            out = jnp.concatenate(
                [join_heads(out_came[:, :, HD:], 1), join_query_heads(out_came[:, :, :HD], 1)],
                axis=1,
            )
            up = jnp.concatenate(
                [
                    ffn_came[g, :, part * ff_own : (part + 1) * ff_own]
                    for part in range(2)
                    for g in range(members)
                ],
                axis=1,
            ).astype(f32)
            down = jnp.concatenate([ffn_came[g, :, 2 * ff_own :] for g in range(members)], axis=1)
            return mix, out.T.astype(f32), up, down.T.astype(f32)

        by_layer = [weight_grads(layer) for layer in range(LAYERS)]
        mix_g, out_g, up_g, down_g = (jnp.stack(grads) for grads in zip(*by_layer))
        gain_g, chan_g, conv_g, head_g = (jnp.stack(grads) for grads in zip(*out_grads))
        chan_rows = jnp.zeros((LAYERS, CONV + 2, HGROUPS, heads, replicas, lanes), f32)
        chan_rows = lax.dynamic_update_slice(
            chan_rows,
            chan_g.reshape(LAYERS, CONV + 2, 1, heads, 1, lanes),
            (0, 0, head_group, 0, head_part, 0),
        ).reshape(LAYERS, CONV + 2, ssm_cols)
        head_rows = lax.dynamic_update_slice(
            jnp.zeros((LAYERS, 3, HGROUPS, heads), f32), head_g[:, :, None], (0, 0, head_group, 0)
        ).reshape(LAYERS, 3, tp_heads)

        def packed(arrays):
            flat = jnp.concatenate([a.reshape(-1) for a in arrays])
            return jnp.pad(flat, (0, -flat.shape[0] % 1024)).reshape(-1, 128)

        def unpacked(flat, arrays):
            flat, marks = flat.reshape(-1), [0]
            for a in arrays:
                marks.append(marks[-1] + a.size)
            return [flat[marks[k] : marks[k + 1]].reshape(a.shape) for k, a in enumerate(arrays)]

        early = (conv_g, gain_g[0, 1], gain_g[1:])
        whole = sum_over(packed(early), tp_axes[::-1])
        local_sums = (chan_rows, head_rows, whole)
        chan_sum, head_sum, whole = unpacked(
            sum_over(packed(local_sums), group_axes[::-1] + (half_axis,)), local_sums
        )
        conv_sum, gain_two, gain_rest = unpacked(whole, early)
        ctx_index = slot * members + me
        last_gain = jnp.repeat(gain_g[0, 0].reshape(ctx_count, 1, depth), 4, axis=1)
        last_gain = lax.all_to_all(
            last_gain.reshape(4 * ctx_count, 1, depth), all_axes, 0, 0, tiled=True
        )
        last_gain = jnp.sum(last_gain, axis=0)
        gain_rest = lax.dynamic_slice_in_dim(gain_rest, ctx_index * depth, depth, 2)
        gain_two = lax.dynamic_slice_in_dim(gain_two, ctx_index * depth, depth, 0)
        gain_own = jnp.concatenate([jnp.concatenate([last_gain, gain_two[None]])[None], gain_rest])
        return (
            activations,
            input_grad,
            gain_own,
            mix_g,
            share_g,
            chan_sum,
            conv_sum,
            head_sum,
            out_g,
            up_g,
            down_g,
        )

    return local


def solution(mesh):
    ctx_bits = mesh.shape["ctx"].bit_length() - 1
    tp_bits = mesh.shape["tp"].bit_length() - 1
    ctx_axes = tuple(f"c{k}" for k in range(ctx_bits))
    tp_axes = tuple(f"t{k}" for k in range(tp_bits))
    fine = Mesh(mesh.devices.reshape((2,) * (ctx_bits + tp_bits)), ctx_axes + tp_axes)
    return jax.shard_map(
        build(ctx_axes, tp_axes),
        mesh=fine,
        in_specs=(
            P(None, None, ctx_axes, None),
            P(None, None, ctx_axes, None),
            P(),
            P(None, None, ctx_axes),
            P(None, ctx_axes, tp_axes),
            P(None, ctx_axes, None),
            P(None, None, tp_axes),
            P(),
            P(None, None, tp_axes),
            P(None, tp_axes, ctx_axes),
            P(None, ctx_axes, tp_axes),
            P(None, tp_axes, ctx_axes),
        ),
        out_specs=(
            P(None, None, ctx_axes, None),
            P(None, None, ctx_axes, None),
            P(None, None, ctx_axes),
            P(None, ctx_axes, tp_axes),
            P(None, ctx_axes, None),
            P(None, None, tp_axes),
            P(),
            P(None, None, tp_axes),
            P(None, tp_axes, ctx_axes),
            P(None, ctx_axes, tp_axes),
            P(None, tp_axes, ctx_axes),
        ),
        check_vma=False,
    )
```

```python
import functools

import jax
import jax.numpy as jnp
from jax import lax
from jax.experimental import pallas as pl
from jax.experimental.pallas import tpu as pltpu
from jax.sharding import Mesh
from jax.sharding import PartitionSpec as P

D = 2048
MH = 48
P_SIZE = 64
N = 256
CONV = 4
AH = 8
KVH = 2
HD = 128
FF = 4096
LAYERS = 2
HGROUPS = 4
PAD = 8

eps_norm = 1e-05
rope_base = 100000000000.0
highest = lax.Precision.HIGHEST
SWAP = [(0, 1), (1, 0)]
bf16 = jnp.bfloat16
f32 = jnp.float32


def matmul(left_op, right_op):
    return jnp.dot(left_op, right_op, preferred_element_type=f32)


def matmul_tn(left_op, right_op):
    return lax.dot_general(left_op, right_op, (((0,), (0,)), ((), ())), preferred_element_type=f32)


def matmul_nt(left_op, right_op):
    return lax.dot_general(left_op, right_op, (((1,), (1,)), ((), ())), preferred_element_type=f32)


def product_tn_block(left, right, out):
    out[...] = dot_tn(left[...], right[...]).astype(bf16)


def product_tn(left, right):
    rows, m = left.shape
    n = right.shape[1]
    block = min(m, 1024 if rows <= 768 else 256)
    return pl.pallas_call(
        product_tn_block,
        grid=(m // block,),
        in_specs=[
            pl.BlockSpec((rows, block), lambda i: (0, i)),
            pl.BlockSpec((rows, n), lambda i: (0, 0)),
        ],
        out_specs=pl.BlockSpec((block, n), lambda i: (i, 0)),
        out_shape=jax.ShapeDtypeStruct((m, n), bf16),
        compiler_params=pltpu.CompilerParams(vmem_limit_bytes=30 * 2**20),
        cost_estimate=pl.CostEstimate(
            flops=2 * rows * m * n, bytes_accessed=2 * (rows * m + rows * n + m * n), transcendentals=0
        ),
    )(left, right)


def silu_grad(inputs):
    sigmoid = jax.nn.sigmoid(inputs)
    return sigmoid * (1.0 + inputs * (1.0 - sigmoid))


def after(x, point):
    return lax.optimization_barrier((x, point))[0]


def pick(x, dim, index):
    return lax.dynamic_index_in_dim(x, index, dim, keepdims=False)


def norm_piece(stream, gain_row):
    factor = lax.rsqrt(jnp.mean(stream * stream, axis=-1, keepdims=True) + eps_norm)
    return stream * factor * gain_row


def dot_nn(a, b):
    return lax.dot_general(a, b, (((1,), (0,)), ((), ())), preferred_element_type=f32)


def dot_nt(a, b):
    return lax.dot_general(a, b, (((1,), (1,)), ((), ())), preferred_element_type=f32)


def dot_tn(a, b):
    return lax.dot_general(a, b, (((0,), (0,)), ((), ())), preferred_element_type=f32)


def dot_exact(a, b):
    return lax.dot_general(
        a, b, (((1,), (0,)), ((), ())), precision=highest, preferred_element_type=f32
    )


def sigmoid(v):
    return 1.0 / (1.0 + jnp.exp(-v))


def block_place(block, members):
    quarter, at = block // members, block % members
    if quarter < 2:
        return at, 0, quarter
    return members - 1 - at, 1, 3 - quarter


class Plan:
    def __init__(self, seq_len, block_len, heads, lanes):
        self.seq_len = seq_len
        self.block_len = block_len
        self.heads = heads
        self.lanes = lanes
        self.width = heads * lanes
        self.members = seq_len // (4 * block_len)
        self.chunk = 4 * block_len
        self.chunks = seq_len // self.chunk
        self.query_parts = self.members // 2
        self.query_rows = seq_len // self.query_parts
        self.bc = 2 * N
        self.key_at = self.bc
        self.value_at = self.bc + HD
        self.q_at = self.bc + 2 * HD
        self.gate_at = self.bc + 3 * HD
        self.pair_cols = 2 * self.width
        self.pair_tiles = self.pair_cols + -self.pair_cols % 128
        self.step_at = self.gate_at + self.pair_tiles
        self.cols = self.step_at + 128

    def rows(self, core, block):
        member, half, place = block_place(block, self.members)
        other = core if place == 0 else 1 - core
        start = other * (self.seq_len // 2) + (2 * member + half) * self.block_len
        return pl.ds(pl.multiple_of(start, 16), self.block_len)

    def blocks(self):
        return range(self.seq_len // self.block_len)


def head_masks(plan):
    lane = lax.broadcasted_iota(jnp.int32, (1, plan.width), 1)
    return [
        ((lane >= h * plan.lanes) & (lane < (h + 1) * plan.lanes)).astype(f32)
        for h in range(plan.heads)
    ]


def over_heads(plan, tile, masks):
    return sum(tile[:, h : h + 1] * masks[h] for h in range(plan.heads))


def per_head(plan, values, masks):
    lane = lax.broadcasted_iota(jnp.int32, (1, 128), 1)
    total = None
    for h in range(plan.heads):
        column = jnp.sum(values * masks[h], axis=1, keepdims=True)
        part = column * (lane == h).astype(f32)
        total = part if total is None else total + part
    return total


def conv_values(source, taps_ref, rows, start, low, high):
    total = taps_ref[CONV : CONV + 1, low:high]
    for k in range(CONV):
        at = PAD + start - (CONV - 1) + k
        total = total + taps_ref[k : k + 1, low:high] * source[pl.ds(at, rows), low:high]
    return total


def prepare(plan, core, mixed, nat_bc, nat_x, nat_step):
    width = plan.width
    nat_bc[0:PAD, :] = jnp.zeros((PAD, plan.bc), f32)
    nat_x[0:PAD, :] = jnp.zeros((PAD, width), f32)
    for block in plan.blocks():
        at = PAD + block * plan.block_len
        rows = plan.rows(core, block)
        nat_bc[pl.ds(at, plan.block_len), :] = mixed[rows, 0 : plan.bc]
        pair = mixed[rows, plan.gate_at : plan.gate_at + plan.pair_tiles]
        nat_x[pl.ds(at, plan.block_len), :] = pltpu.roll(pair, plan.pair_tiles - width, 1)[:, :width]
        nat_step[pl.ds(at - PAD, plan.block_len), :] = mixed[rows, plan.step_at : plan.step_at + 128]


def chunk_decays(plan, nat_step, head_rows, c, tri):
    q = plan.chunk
    real = lax.broadcasted_iota(jnp.int32, (1, 128), 1) < plan.heads
    raw = jnp.where(real, nat_step[pl.ds(c * q, q), :] + head_rows[1:2, :], 0.0)
    step = jnp.where(real, jnp.maximum(raw, 0.0) + jnp.log(1.0 + jnp.exp(-jnp.abs(raw))), 0.0)
    cumulative = dot_exact(tri, step * head_rows[0:1, :])
    return raw, step, cumulative


def triangle(plan):
    q = plan.chunk
    row = lax.broadcasted_iota(jnp.int32, (q, q), 0)
    col = lax.broadcasted_iota(jnp.int32, (q, q), 1)
    return row, col


def ssm_forward(plan, core_ref, mixed, taps, shared_taps, head_rows, y_out, low_out, states_out, squares_out,
                nat_bc, nat_x, nat_step):
    q = plan.chunk
    masks = head_masks(plan)
    core = core_ref[0]
    prepare(plan, core, mixed, nat_bc, nat_x, nat_step)
    row, col = triangle(plan)
    lower = row >= col
    tri = lower.astype(f32)
    state = jnp.zeros((N, plan.width), f32)
    for c in range(plan.chunks):
        start = c * q
        x = conv_values(nat_x, taps, q, start, 0, plan.width)
        x = x * sigmoid(x)
        bc = conv_values(nat_bc, shared_taps, q, start, 0, plan.bc)
        bc = (bc * sigmoid(bc)).astype(bf16)
        b, cc = bc[:, :N], bc[:, N:]
        _, step, cum = chunk_decays(plan, nat_step, head_rows, c, tri)
        cum_rows = cum.T
        cum_full = over_heads(plan, cum, masks)
        total_full = cum_full[q - 1 : q, :]
        u = x * over_heads(plan, step, masks)
        inner = dot_nt(cc, b)
        states_out[c] = state
        y = dot_nn(cc, state.astype(bf16)) * jnp.exp(cum_full) + taps[6:7, :] * x
        for h in range(plan.heads):
            seg = jnp.where(lower, cum[:, h : h + 1] - cum_rows[h : h + 1, :], -1e30)
            mixing = (jnp.exp(seg) * inner).astype(bf16)
            y = y + dot_nn(mixing, (u * masks[h]).astype(bf16))
        weighted = (u * jnp.exp(total_full - cum_full)).astype(bf16)
        state = jnp.exp(total_full) * state + dot_tn(b, weighted)
        for k in range(4):
            block = 4 * c + k
            y_out[plan.rows(core, block), :] = y[k * plan.block_len : (k + 1) * plan.block_len, :]
    z = mixed[:, plan.gate_at : plan.gate_at + plan.width]
    gated = y_out[...] * (z * sigmoid(z))
    low_out[...] = (gated * taps[5:6, :]).astype(bf16)
    squares_out[...] = lax.dot_general(
        jnp.ones((8, plan.width), f32), gated * gated, (((1,), (1,)), ((), ())),
        precision=highest, preferred_element_type=f32,
    )


def ssm_backward(plan, core_ref, mixed, taps, shared_taps, head_rows, y_in, states, grad_mixer, scales,
                 bc_out, pair_out, step_out, taps_out, shared_out, heads_out,
                 nat_bc, nat_x, nat_step, nat_dy, grad_x, grad_bc, grad_y_ref):
    q = plan.chunk
    width = plan.width
    masks = head_masks(plan)
    core = core_ref[0]
    prepare(plan, core, mixed, nat_bc, nat_x, nat_step)
    row, col = triangle(plan)
    lower, upper = row >= col, row <= col
    strict_lower, strict_upper = row > col, row < col
    tri, tri_back = lower.astype(f32), upper.astype(f32)

    z = mixed[:, plan.gate_at : plan.gate_at + width]
    y = y_in[...]
    sig = sigmoid(z)
    silu = z * sig
    gated = y * silu
    scaled = grad_mixer[:, HD : HD + width] * scales[:, 0:1]
    grad_gated = scaled * taps[5:6, :] + scales[:, 1:2] * gated
    gain_grad = jnp.sum(scaled * gated, axis=0, keepdims=True)
    grad_z = grad_gated * y * (sig * (1.0 + z * (1.0 - sig)))
    spare = plan.pair_tiles - width
    pair_out[...] = jnp.concatenate(
        [grad_z, jnp.zeros((plan.seq_len, spare), f32)], axis=1
    ).astype(bf16)
    grad_y_ref[...] = grad_gated * silu
    for block in plan.blocks():
        at = block * plan.block_len
        nat_dy[pl.ds(at, plan.block_len), :] = grad_y_ref[plan.rows(core, block), :]

    grad_x[plan.seq_len : plan.seq_len + PAD, :] = jnp.zeros((PAD, width), f32)
    grad_bc[plan.seq_len : plan.seq_len + PAD, :] = jnp.zeros((PAD, plan.bc), f32)
    grad_state = jnp.zeros((N, width), f32)
    skip_grad = jnp.zeros((1, width), f32)
    rate_grad = jnp.zeros((1, 128), f32)
    bias_grad = jnp.zeros((1, 128), f32)
    for c in reversed(range(plan.chunks)):
        start = c * q
        x_lin = conv_values(nat_x, taps, q, start, 0, width)
        x_sig = sigmoid(x_lin)
        x = x_lin * x_sig
        bc_lin = conv_values(nat_bc, shared_taps, q, start, 0, plan.bc)
        bc_sig = sigmoid(bc_lin)
        bc = (bc_lin * bc_sig).astype(bf16)
        b, cc = bc[:, :N], bc[:, N:]
        raw, step, cum = chunk_decays(plan, nat_step, head_rows, c, tri)
        cum_rows = cum.T
        cum_full = over_heads(plan, cum, masks)
        total_full = cum_full[q - 1 : q, :]
        step_full = over_heads(plan, step, masks)
        u = x * step_full
        u_low = u.astype(bf16)
        dy = nat_dy[pl.ds(start, q), :]
        dy_low = dy.astype(bf16)
        state = states[c]
        state_low = state.astype(bf16)
        grad_state_low = grad_state.astype(bf16)
        entry = jnp.exp(cum_full)
        exit_w = jnp.exp(total_full - cum_full)
        total_decay = jnp.exp(total_full)
        dy_entry = (dy * entry).astype(bf16)
        grad_c = dot_nt(dy_entry, state_low)
        carried = dot_nn(cc, state_low) * entry
        du_state = dot_nn(b, grad_state_low) * exit_w
        grad_b = dot_nt((u * exit_w).astype(bf16), grad_state_low)
        inner = dot_nt(cc, b)
        inner_t = dot_nt(b, cc)
        du = du_state
        grad_inner = jnp.zeros((q, q), f32)
        grad_inner_t = jnp.zeros((q, q), f32)
        lane = lax.broadcasted_iota(jnp.int32, (1, 128), 1)
        dcum = per_head(plan, dy * carried - u * du_state, masks)
        for h in range(plan.heads):
            here = (lane == h).astype(f32)
            u_head = (u * masks[h]).astype(bf16)
            dy_head = (dy * masks[h]).astype(bf16)
            seg = cum[:, h : h + 1] - cum_rows[h : h + 1, :]
            decay = jnp.exp(jnp.where(lower, seg, -1e30))
            decay_t = jnp.exp(jnp.where(upper, -seg, -1e30))
            grad_mix = dot_nt(dy_head, u_low) * decay
            grad_mix_t = dot_nt(u_head, dy_low) * decay_t
            grad_inner = grad_inner + grad_mix
            grad_inner_t = grad_inner_t + grad_mix_t
            du = du + dot_nn((decay_t * inner_t).astype(bf16), dy_head)
            out_sum = jnp.sum(jnp.where(strict_lower, grad_mix * inner, 0.0), axis=1, keepdims=True)
            in_sum = jnp.sum(
                jnp.where(strict_upper, grad_mix_t * inner_t, 0.0), axis=1, keepdims=True
            )
            dcum = dcum + (out_sum - in_sum) * here
        grad_c = grad_c + dot_nn(grad_inner.astype(bf16), b)
        grad_b = grad_b + dot_nn(grad_inner_t.astype(bf16), cc)
        whole = jnp.sum(u * du_state, axis=0, keepdims=True) + jnp.sum(
            grad_state * state, axis=0, keepdims=True
        ) * total_decay
        dlog = dot_exact(tri_back, dcum) + per_head(plan, whole, masks)
        rate_grad = rate_grad + jnp.sum(dlog * step, axis=0, keepdims=True)
        grad_step = dlog * head_rows[0:1, :] + per_head(plan, du * x, masks)
        grad_raw = grad_step * sigmoid(raw)
        bias_grad = bias_grad + jnp.sum(grad_raw, axis=0, keepdims=True)
        grad_xc = du * step_full + taps[6:7, :] * dy
        skip_grad = skip_grad + jnp.sum(dy * x, axis=0, keepdims=True)
        grad_state = total_decay * grad_state + dot_tn(cc, dy_entry)
        grad_x[pl.ds(start, q), :] = grad_xc * (x_sig * (1.0 + x_lin * (1.0 - x_sig)))
        grad_bc[pl.ds(start, q), :] = jnp.concatenate([grad_b, grad_c], axis=1) * (
            bc_sig * (1.0 + bc_lin * (1.0 - bc_sig))
        )
        for k in range(4):
            step_out[plan.rows(core, 4 * c + k), :] = grad_raw[
                k * plan.block_len : (k + 1) * plan.block_len, :
            ].astype(bf16)

    size = plan.block_len
    tap_grads = [jnp.zeros((1, width), f32) for _ in range(CONV + 1)]
    shared_grads = [jnp.zeros((1, plan.bc), f32) for _ in range(CONV + 1)]
    lane = lax.broadcasted_iota(jnp.int32, (1, plan.pair_tiles), 1)
    for c in range(plan.chunks):
        start = c * q
        dx = grad_x[pl.ds(start, q), :]
        dbc = grad_bc[pl.ds(start, q), :]
        tap_grads[CONV] += jnp.sum(dx, axis=0, keepdims=True)
        shared_grads[CONV] += jnp.sum(dbc, axis=0, keepdims=True)
        pre_dx = None
        pre_dbc = None
        for k in range(CONV):
            at = PAD + start - (CONV - 1) + k
            tap_grads[k] += jnp.sum(dx * nat_x[pl.ds(at, q), :], axis=0, keepdims=True)
            shared_grads[k] += jnp.sum(dbc * nat_bc[pl.ds(at, q), :], axis=0, keepdims=True)
            ahead = start + (CONV - 1) - k
            part = taps[k : k + 1, :] * grad_x[pl.ds(ahead, q), :]
            pre_dx = part if k == 0 else pre_dx + part
            part = shared_taps[k : k + 1, :] * grad_bc[pl.ds(ahead, q), :]
            pre_dbc = part if k == 0 else pre_dbc + part
        tile = jnp.concatenate([pre_dx, jnp.zeros((q, spare), f32)], axis=1)
        tile = pltpu.roll(tile, width, 1).astype(bf16)
        for k in range(4):
            rows = plan.rows(core, 4 * c + k)
            pair_out[rows, :] = jnp.where(
                lane < width, pair_out[rows, :], tile[k * size : (k + 1) * size, :]
            )
            bc_out[rows, :] = pre_dbc[k * size : (k + 1) * size, :].astype(bf16)
    for k in range(CONV + 1):
        taps_out[k : k + 1, :] = tap_grads[k]
        shared_out[k : k + 1, :] = shared_grads[k]
    taps_out[5:6, :] = gain_grad
    taps_out[6:7, :] = skip_grad
    heads_out[0:1, :] = rate_grad * head_rows[0:1, :]
    heads_out[1:2, :] = bias_grad


def whole_specs(arrays):
    def spec(array):
        zeros = (0,) * len(array.shape)
        return pl.BlockSpec(array.shape, lambda i: zeros, pipeline_mode=pl.Buffered(1))

    return [spec(array) for array in arrays]


def call_whole(plan, kernel, outs, scratch, flops, inputs, scalars=()):
    return pl.pallas_call(
        kernel,
        grid=(1,),
        in_specs=[pl.BlockSpec(memory_space=pltpu.SMEM) for _ in scalars] + whole_specs(inputs),
        out_specs=tuple(whole_specs(outs)),
        out_shape=tuple(outs),
        scratch_shapes=scratch,
        compiler_params=ssm_params(plan),
        cost_estimate=pl.CostEstimate(
            flops=flops, bytes_accessed=plan.seq_len * 8192, transcendentals=0
        ),
    )(*scalars, *inputs)


def ssm_params(plan):
    limit = 58 * 2**20
    return pltpu.CompilerParams(vmem_limit_bytes=limit)


def run_forward(plan, core, *inputs):
    t, w = plan.seq_len, plan.width
    outs = [
        jax.ShapeDtypeStruct((t, w), f32),
        jax.ShapeDtypeStruct((t, w), bf16),
        jax.ShapeDtypeStruct((plan.chunks, N, w), f32),
        jax.ShapeDtypeStruct((8, t), f32),
    ]
    scratch = [
        pltpu.VMEM((PAD + t, plan.bc), f32),
        pltpu.VMEM((PAD + t, w), f32),
        pltpu.VMEM((t, 128), f32),
    ]
    return call_whole(
        plan, functools.partial(ssm_forward, plan), outs, scratch, 40000 * t * w, inputs, (core,)
    )


def run_backward(plan, core, *inputs):
    t, w = plan.seq_len, plan.width
    outs = [
        jax.ShapeDtypeStruct((t, plan.bc), bf16),
        jax.ShapeDtypeStruct((t, plan.pair_tiles), bf16),
        jax.ShapeDtypeStruct((t, 128), bf16),
        jax.ShapeDtypeStruct((8, w), f32),
        jax.ShapeDtypeStruct((8, plan.bc), f32),
        jax.ShapeDtypeStruct((8, 128), f32),
    ]
    scratch = [
        pltpu.VMEM((PAD + t, plan.bc), f32),
        pltpu.VMEM((PAD + t, w), f32),
        pltpu.VMEM((t, 128), f32),
        pltpu.VMEM((t, w), f32),
        pltpu.VMEM((t + PAD, w), f32),
        pltpu.VMEM((t + PAD, plan.bc), f32),
        pltpu.VMEM((t, w), f32),
    ]
    return call_whole(
        plan, functools.partial(ssm_backward, plan), outs, scratch, 90000 * t * w, inputs, (core,)
    )


def attend_scores(plan, queries, keys, query_pos, key_pos):
    scores = dot_nt(queries, keys) * HD ** (-0.5)
    return jnp.where(key_pos <= query_pos, scores, -1e30)


def turned(x, cosine, sine):
    return x * cosine + pltpu.roll(x, HD // 2, 1) * sine


def attend_forward(plan, part, mixed, cosine, sine, query_pos, key_pos,
                   att_out, log_out, q_out, kv_out):
    rows = pl.ds(pl.multiple_of(part[0] * plan.query_rows, 8), plan.query_rows)
    keys = turned(mixed[:, plan.key_at : plan.key_at + HD], cosine[...], sine[...]).astype(bf16)
    values = mixed[:, plan.value_at : plan.value_at + HD].astype(bf16)
    kv_out[:, :HD] = keys
    kv_out[:, HD:] = values
    queries = mixed[rows, plan.q_at : plan.q_at + HD]
    queries = turned(queries, cosine[rows, :], sine[rows, :]).astype(bf16)
    q_out[...] = queries
    scores = attend_scores(plan, queries, keys, query_pos[rows, :], key_pos[...])
    peak = jnp.max(scores, axis=1, keepdims=True)
    weights = jnp.exp(scores - peak)
    total = jnp.sum(weights, axis=1, keepdims=True)
    probs = (weights / total).astype(bf16)
    att_out[...] = jnp.zeros((plan.seq_len, HD), bf16)
    att_out[rows, :] = dot_nn(probs, values).astype(bf16)
    log_out[...] = peak + jnp.log(total)


def attend_backward(plan, part, queries, kv, logs, grad_mixer, cosine, sine, query_pos, key_pos,
                    q_out, kv_out):
    rows = pl.ds(pl.multiple_of(part[0] * plan.query_rows, 8), plan.query_rows)
    keys, values = kv[:, :HD], kv[:, HD:]
    scale = HD ** (-0.5)
    q, grad = queries[...], grad_mixer[rows, :HD].astype(bf16)
    probs = jnp.exp(attend_scores(plan, q, keys, query_pos[rows, :], key_pos[...]) - logs[...])
    grad_probs = dot_nt(grad, values)
    inner = jnp.sum(probs * grad_probs, axis=1, keepdims=True)
    grad_scores = (probs * (grad_probs - inner)).astype(bf16)
    grad_q = dot_nn(grad_scores, keys) * scale
    q_out[...] = jnp.zeros((plan.seq_len, HD), bf16)
    q_out[rows, :] = turned(grad_q, cosine[rows, :], -sine[rows, :]).astype(bf16)
    grad_k = dot_tn(grad_scores, q) * scale
    kv_out[:, :HD] = turned(grad_k, cosine[...], -sine[...]).astype(bf16)
    kv_out[:, HD:] = dot_tn(probs.astype(bf16), grad).astype(bf16)


def run_attend(plan, part, *inputs):
    t, rows = plan.seq_len, plan.query_rows
    outs = [
        jax.ShapeDtypeStruct((t, HD), bf16),
        jax.ShapeDtypeStruct((rows, 1), f32),
        jax.ShapeDtypeStruct((rows, HD), bf16),
        jax.ShapeDtypeStruct((t, 2 * HD), bf16),
    ]
    kernel = functools.partial(attend_forward, plan)
    return call_whole(plan, kernel, outs, [], 4 * rows * t * HD, inputs, (part,))


def run_attend_back(plan, part, *inputs):
    t = plan.seq_len
    outs = [jax.ShapeDtypeStruct((t, HD), bf16), jax.ShapeDtypeStruct((t, 2 * HD), bf16)]
    kernel = functools.partial(attend_backward, plan)
    return call_whole(plan, kernel, outs, [], 10 * plan.query_rows * t * HD, inputs, (part,))


def build(ctx_axes, tp_axes):
    half_axis = ctx_axes[0]
    group_axes = ctx_axes[1:]
    t_half, t_core = tp_axes
    ring_axes = group_axes + (t_half,)
    slot_axes = group_axes + tp_axes
    all_axes = ctx_axes + tp_axes
    span = len(ring_axes)

    def column_parts(width):
        unit = width // 128
        marks = [0] + [128 * (unit * (k + 1) // 3) for k in range(3)]
        return list(zip(marks[:-1], marks[1:]))

    def rotated(part):
        turn = part % span
        return ring_axes[turn:] + ring_axes[:turn]

    def gather_rows(x):
        rows, width = x.shape
        parts = []
        for part, (low, high) in enumerate(column_parts(width)):
            held = x[:, low:high].reshape((1,) * span + (rows, high - low))
            for axis in rotated(part):
                dim = ring_axes.index(axis)
                got = lax.ppermute(held, axis, SWAP)
                first = lax.axis_index(axis) == 0
                held = jnp.where(
                    first, jnp.concatenate([held, got], dim), jnp.concatenate([got, held], dim)
                )
            parts.append(held)
        held = lax.optimization_barrier(jnp.concatenate(parts, -1).reshape(-1, width))
        return jnp.concatenate([held, lax.ppermute(held, t_core, SWAP)])

    def scatter_product(left, right, extra=None):
        total = left.shape[0]
        width = right.shape[0]
        peers = 2 ** (span + 1)
        rows = total // peers
        own = total // 2
        sent = matmul_nt(left[own:], right).astype(bf16)
        kept = matmul_nt(left[:own], right)
        if extra is not None:
            width += extra.shape[1]
            sent = jnp.concatenate([sent, extra[own:]], axis=1)
            kept = jnp.concatenate([kept, extra[:own].astype(f32)], axis=1)
        held = kept + lax.ppermute(sent, t_core, SWAP).astype(f32)
        parts = []
        for part, (low, high) in enumerate(column_parts(width)):
            piece = held[:, low:high].reshape((2,) * span + (rows, high - low))
            names = list(ring_axes)
            for axis in rotated(part):
                dim = names.index(axis)
                names.pop(dim)
                index = lax.axis_index(axis)
                got = lax.ppermute(pick(piece, dim, 1 - index).astype(bf16), axis, SWAP)
                piece = pick(piece, dim, index) + got.astype(f32)
            parts.append(piece)
        return jnp.concatenate(parts, -1)

    def sum_slot(x):
        turn = lax.axis_index(t_core) == 1
        x = x.reshape(2, -1, 128)
        x = jnp.where(turn, x[::-1], x)
        came = lax.all_to_all(
            jnp.broadcast_to(x[None], (2 ** (span + 1),) + x.shape), slot_axes, 0, 0, tiled=True
        )
        x = jnp.sum(came, axis=0)
        return jnp.where(turn, x[::-1], x).reshape(-1, 1)

    def sum_over(x, axes):
        for axis in axes:
            x = x + lax.ppermute(x, axis, SWAP)
        return x

    def group_index():
        return lax.axis_index(group_axes)

    def group_swap(blocks):
        return lax.all_to_all(blocks, group_axes, 0, 0, tiled=True)

    def both_halves(came):
        return lax.all_gather(came, half_axis, axis=0, tiled=True)

    def spread_first(blocks):
        return lax.all_to_all(jnp.concatenate([blocks, blocks]), ctx_axes, 0, 0, tiled=True)

    def fold_halves(blocks):
        return lax.psum_scatter(blocks.astype(bf16), half_axis, scatter_dimension=0, tiled=True)

    def fold_last(blocks):
        half = lax.axis_index(half_axis)
        paired = blocks.reshape((2, blocks.shape[0] // 2) + blocks.shape[1:])
        got = lax.ppermute(pick(paired, 0, 1 - half).astype(bf16), half_axis, SWAP)
        return pick(paired, 0, half).astype(f32), got

    def gather_lanes(x):
        for axis in ctx_axes[::-1]:
            got = lax.ppermute(x, axis, SWAP)
            first = lax.axis_index(axis) == 0
            x = jnp.where(first, jnp.concatenate([x, got], -1), jnp.concatenate([got, x], -1))
        return x

    def local(
        hidden,
        cotangent,
        lengths,
        norm_gains,
        mix_weight,
        share_weight,
        chan_params,
        shared_conv,
        head_params,
        out_weight,
        up_weight,
        down_weight,
    ):
        members = 2 ** len(group_axes)
        ctx_count = 2 * members
        replicas = members // HGROUPS
        slot = lax.axis_index(half_axis)
        me = group_index()
        head_group = me // replicas
        head_part = me % replicas
        tp_half = lax.axis_index(t_half)
        tp_core = lax.axis_index(t_core)
        tp_index = tp_half * 2 + tp_core
        block_len = hidden.shape[2]
        depth = mix_weight.shape[1]
        seq_len = 2 * ctx_count * block_len
        own_len = 4 * block_len
        tp_heads = chan_params.shape[2] // P_SIZE
        heads = tp_heads // HGROUPS
        lanes = P_SIZE // replicas
        width = heads * lanes
        ssm_cols = tp_heads * P_SIZE
        qheads = AH // 4
        q_cols = qheads * HD
        ff_tp = FF // 4
        ff_own = ff_tp // members
        plan = Plan(seq_len, block_len, heads, lanes)
        own_head = me // plan.query_parts
        core_scalar = tp_core.astype(jnp.int32).reshape(1)
        query_part = (me % plan.query_parts).astype(jnp.int32).reshape(1)
        share_cols = share_weight.shape[2]
        kv_cols = 2 * N
        dt_cols = 2 * N + 2 * KVH * HD
        kv_head = tp_index * qheads // (AH // KVH)
        score_scale = HD ** (-0.5)

        def block_of(member, half, cube):
            near = cube * members + member
            return jnp.where(half == 0, near, 2 * ctx_count - 1 - near)

        within = jnp.arange(block_len)
        own_pos = block_of(me, tp_half, tp_core) * block_len + within
        own_valid = (own_pos < lengths[slot]).astype(f32)[:, None]
        ring = jnp.arange(2 * members)

        def core_positions(core):
            first = block_of(ring // 2, ring % 2, core) * block_len
            return (first[:, None] + within[None, :]).reshape(-1)

        key_pos = jnp.concatenate([core_positions(tp_core), core_positions(1 - tp_core)])
        half_dim = HD // 2
        inverse = jnp.exp(-jnp.log(rope_base) * (2.0 * jnp.arange(half_dim, dtype=f32) / HD))
        angles = key_pos.astype(f32)[:, None] * inverse
        cosine = jnp.concatenate([jnp.cos(angles)] * 2, axis=1)
        sine = jnp.concatenate([-jnp.sin(angles), jnp.sin(angles)], axis=1)

        tables = (cosine, sine, key_pos[:, None], key_pos[None, :])

        def cut_query_heads(x, axis):
            shape = x.shape
            split = x.reshape(shape[:axis] + (qheads, HD) + shape[axis + 1 :])
            return jnp.repeat(jnp.moveaxis(split, axis, 0), plan.query_parts, axis=0)

        def join_query_heads(x, axis):
            summed = jnp.sum(x.astype(f32).reshape((qheads, plan.query_parts) + x.shape[1:]), axis=1)
            joined = jnp.moveaxis(summed, 0, axis)
            shape = joined.shape
            return joined.reshape(shape[:axis] + (q_cols,) + shape[axis + 2 :])

        def bring_in(x):
            got = lax.ppermute(
                pick(pick(x, 0, 1 - slot), 0, tp_half), (half_axis, t_core), [(0, 2), (3, 1)]
            )
            return jnp.where(tp_core == slot, pick(pick(x, 0, slot), 0, tp_half), got)

        def share_columns(own):
            quarter = own.shape[1] // 4
            chunks = jnp.moveaxis(own.reshape(block_len, 4, quarter), 1, 0)
            chunks = jnp.broadcast_to(chunks[None], (members,) + chunks.shape)
            rows = lax.all_to_all(
                chunks.reshape(4 * members, block_len, quarter), slot_axes, 0, 0, tiled=True
            )
            rows = jnp.moveaxis(rows.reshape(2 * members, 2, block_len, quarter), 1, 0)
            return jnp.where(tp_core == 0, rows, rows[::-1]).reshape(seq_len, quarter)

        def bring_out(x):
            x = x.astype(bf16)
            got = lax.ppermute(x, (half_axis, t_core), [(1, 3), (2, 0)])
            pair = jnp.where(slot == 0, jnp.stack([x, got]), jnp.stack([got, x]))
            other = lax.ppermute(pair, t_core, SWAP)
            pair = jnp.where(tp_core == slot, pair, other)
            other = lax.ppermute(pair, t_half, SWAP)
            both = jnp.where(tp_half == 0, jnp.stack([pair, other], 1), jnp.stack([other, pair], 1))
            return both.astype(f32)

        def cut_heads(x, axis):
            shape = x.shape
            split = x.reshape(
                shape[:axis] + (HGROUPS, heads, replicas, lanes) + shape[axis + 1 :]
            )
            split = jnp.moveaxis(split, (axis, axis + 2), (0, 1))
            return split.reshape((members,) + shape[:axis] + (width,) + shape[axis + 1 :])

        def join_heads(x, axis):
            if replicas == 1:
                return jnp.concatenate([x[g] for g in range(members)], axis=axis)
            shape = x.shape[1:]
            split = x.reshape(
                (HGROUPS, replicas) + shape[:axis] + (heads, lanes) + shape[axis + 1 :]
            )
            split = jnp.moveaxis(split, (0, 1), (axis, axis + 2))
            return split.reshape(shape[:axis] + (ssm_cols,) + shape[axis + 1 :])

        gains = gather_lanes(norm_gains).astype(f32)
        hidden_rows = bring_in(after(hidden, gains))
        stream = hidden_rows.astype(f32)
        own_chan = pick(cut_heads(chan_params, 2), 0, me)
        own_heads = pick(head_params.reshape(LAYERS, 3, HGROUPS, heads), 2, head_group)
        skip_full = jnp.repeat(own_heads[:, 2], lanes, axis=1)[:, None]
        tap_rows = jnp.concatenate([own_chan, skip_full, jnp.zeros_like(skip_full)], axis=1)
        shared_rows = jnp.pad(shared_conv, ((0, 0), (0, 3), (0, 0)))
        head_rows = jnp.pad(
            jnp.stack([-jnp.exp(own_heads[:, 0]), own_heads[:, 1]], axis=1),
            ((0, 0), (0, 6), (0, 128 - heads)),
        )
        share_rows = lax.dynamic_slice_in_dim(share_weight, tp_core * (depth // 2), depth // 2, 1)
        dt_start = dt_cols + tp_index * tp_heads + head_group * heads

        def weight_blocks(layer):
            mix = mix_weight[layer]
            mix_blocks = jnp.concatenate(
                [
                    cut_query_heads(mix[:, 2 * ssm_cols :], 1),
                    cut_heads(mix[:, :ssm_cols], 1),
                    cut_heads(mix[:, ssm_cols : 2 * ssm_cols], 1),
                ],
                2,
            )
            out = out_weight[layer].T
            out_blocks = jnp.concatenate(
                [cut_query_heads(out[:, ssm_cols:], 1), cut_heads(out[:, :ssm_cols], 1)], 2
            )
            up = up_weight[layer]
            down = down_weight[layer].T
            ffn_blocks = jnp.stack(
                [
                    jnp.concatenate(
                        [
                            up[:, g * ff_own : (g + 1) * ff_own],
                            up[:, ff_tp + g * ff_own : ff_tp + (g + 1) * ff_own],
                            down[:, g * ff_own : (g + 1) * ff_own],
                        ],
                        axis=1,
                    )
                    for g in range(members)
                ]
            )
            return mix_blocks, out_blocks, ffn_blocks

        def share_whole(share):
            share = jnp.concatenate(
                [
                    share[:, :kv_cols],
                    lax.dynamic_slice_in_dim(share, kv_cols + kv_head * HD, HD, 1),
                    lax.dynamic_slice_in_dim(share, kv_cols + (KVH + kv_head) * HD, HD, 1),
                    share[:, dt_cols:],
                ],
                axis=1,
            )
            return lax.all_gather(share, ctx_axes + (t_core,), axis=0, tiled=True)

        def input_weights(mix_own, share):
            dt_w = lax.dynamic_slice_in_dim(share, kv_cols + 2 * HD + dt_start - dt_cols, heads, 1)
            return jnp.concatenate(
                [
                    share[:, : plan.q_at],
                    jnp.pad(
                        mix_own.reshape(D, HD + 2 * width),
                        ((0, 0), (0, plan.pair_tiles - plan.pair_cols)),
                    ),
                    jnp.pad(dt_w, ((0, 0), (0, 128 - heads))),
                ],
                axis=1,
            )

        def ffn_weights(ffn_own):
            ffn_own = ffn_own.reshape(D, 3 * ff_own)
            return ffn_own[:, : 2 * ff_own], ffn_own[:, 2 * ff_own :]

        blocks = [weight_blocks(layer) for layer in range(LAYERS)]
        mix_own = [None] * LAYERS
        out_own = [None] * LAYERS
        ffn_own = [None] * LAYERS
        shares = [None] * LAYERS
        mix_own[0] = spread_first(after(blocks[0][0], hidden_rows))
        out_cols = HD + width
        swapped = [[group_swap(x) for x in after(blocks[0][1:], hidden_rows)]]
        for layer in range(1, LAYERS):
            both = group_swap(jnp.concatenate(blocks[layer][:2], axis=2))
            swapped.append([both[:, :, -out_cols:], group_swap(blocks[layer][2])])
            mix_own[layer] = both_halves(both[:, :, :-out_cols])
        for layer in range(LAYERS):
            shares[layer] = share_whole(share_rows[layer])
            out_own[layer] = both_halves(swapped[layer][0])
            ffn_own[layer] = both_halves(swapped[layer][1])

        records = []
        for layer in range(LAYERS):
            rec = {}
            normed_f, rec["norm_one_back"] = jax.vjp(norm_piece, stream, gains[layer, 0])
            if layer == 0:
                normed = norm_piece(gather_rows(hidden_rows).astype(f32), gains[0, 0]).astype(bf16)
            else:
                normed = gather_rows(normed_f.astype(bf16))
            in_w = input_weights(*after((mix_own[layer], shares[layer]), normed))
            mixed = matmul(normed, in_w)
            mixed_here = mixed
            if layer == 0:
                mixed_here = after(mixed, (swapped[0][1], swapped[1][0]))
            ssm_y, gated_low, states, squares = run_forward(
                plan, core_scalar, mixed, tap_rows[layer], shared_rows[layer], head_rows[layer]
            )
            sum_squares = sum_slot(squares[0])
            gated_scale = lax.rsqrt(sum_squares / (MH * P_SIZE) + eps_norm)
            scaled_low = (gated_low.astype(f32) * gated_scale).astype(bf16)
            attended, logsum, queries, keyval = run_attend(plan, query_part, mixed_here, *tables)
            mixer = jnp.concatenate([attended, scaled_low], axis=1)
            out_w = after(out_own[layer], gated_low).reshape(D, HD + width)
            middle = stream + scatter_product(mixer, out_w)
            normed_two_f, rec["norm_two_back"] = jax.vjp(norm_piece, middle, gains[layer, 1])
            normed_two = gather_rows(normed_two_f.astype(bf16))
            up_w, down_w = ffn_weights(after(ffn_own[layer], normed_two))
            gate_up = matmul(normed_two, up_w)
            gate_vals, up_vals = gate_up[:, :ff_own], gate_up[:, ff_own:]
            activation = (jax.nn.silu(gate_vals) * up_vals).astype(bf16)
            stream = (middle + scatter_product(activation, down_w)) * own_valid
            rec.update(
                normed=normed, mixed=mixed, ssm_y=ssm_y, gated_low=gated_low, states=states,
                mixer=mixer, gated_scale=gated_scale, queries=queries, keyval=keyval,
                logsum=logsum, normed_two=normed_two,
                gate_vals=gate_vals, up_vals=up_vals, activation=activation,
            )
            rec["weights"] = (in_w, out_w, up_w, down_w)
            records.append(rec)

        grad_stream = bring_in(cotangent).astype(f32)
        out_grads = [None] * LAYERS
        share_sums = []
        folded = [None] * LAYERS
        points = []
        came = [[] for _ in range(LAYERS)]
        for layer in reversed(range(LAYERS)):
            rec = records[layer]
            in_w, out_w, up_w, down_w = rec["weights"]
            grad_masked = grad_stream * own_valid
            if layer == LAYERS - 1:
                grad_ffn = gather_rows(grad_masked.astype(bf16))
            else:
                grad_ffn = gather_rows(grad_masked.astype(bf16))
            points.append([grad_ffn])
            grad_activation = matmul(grad_ffn, down_w)
            grad_down = product_tn(grad_ffn, rec["activation"])
            gate_vals = rec["gate_vals"]
            grad_gate = grad_activation * rec["up_vals"] * silu_grad(gate_vals)
            grad_upper = grad_activation * jax.nn.silu(gate_vals)
            grad_gate_up = jnp.concatenate([grad_gate, grad_upper], axis=1).astype(bf16)
            if layer + 1 < LAYERS:
                came[layer + 1].append(
                    after(group_swap(after(folded[layer + 1][0], grad_ffn)), grad_gate_up)
                )
            grad_upw = product_tn(rec["normed_two"], grad_gate_up)
            grad_normed_two = scatter_product(grad_gate_up, up_w)
            grad_middle_norm, grad_gain_two = rec["norm_two_back"](grad_normed_two)
            grad_middle = grad_masked + grad_middle_norm
            ffn_blocks = jnp.concatenate([grad_upw, grad_down], axis=1).reshape(
                ctx_count, depth, 3 * ff_own
            )
            folded[layer] = [fold_halves(ffn_blocks)]
            early = (ffn_blocks,) if layer + 1 == LAYERS else (ffn_blocks, folded[layer + 1][1])
            branch_rows = gather_rows(after(grad_middle.astype(bf16), early))
            points[-1].append(branch_rows)
            grad_mixer = matmul(branch_rows, out_w)
            out_blocks = product_tn(branch_rows, rec["mixer"]).reshape(
                ctx_count, depth, HD + width
            )
            if layer == 0:
                folded[layer].append(fold_halves(out_blocks))
            gated_scale = rec["gated_scale"]
            scale_part = jnp.sum(grad_mixer[:, HD:] * rec["gated_low"].astype(f32), axis=-1)
            grad_scale = after(sum_slot(scale_part), out_blocks)
            grad_squares = grad_scale * -0.5 * gated_scale * gated_scale * gated_scale / (MH * P_SIZE)
            if layer + 1 < LAYERS:
                came[layer + 1].append(group_swap(after(folded[layer + 1][1], branch_rows)))
            grad_q, grad_kv = run_attend_back(
                plan, query_part, rec["queries"], rec["keyval"], rec["logsum"], grad_mixer,
                *tables,
            )
            grad_bc, grad_pair, grad_step, taps_grad, grad_conv, heads_grad = run_backward(
                plan, core_scalar, rec["mixed"], tap_rows[layer], shared_rows[layer], head_rows[layer],
                rec["ssm_y"], rec["states"], grad_mixer,
                jnp.concatenate([gated_scale, 2.0 * grad_squares], axis=1),
            )
            chan_grad = taps_grad[: CONV + 2]
            grad_conv = grad_conv[: CONV + 1]
            grad_heads = jnp.concatenate(
                [heads_grad[:2, :heads], jnp.sum(taps_grad[6].reshape(heads, lanes), axis=1)[None]]
            )
            grad_mix_own = jnp.concatenate([grad_q, grad_pair], axis=1)
            grad_in = jnp.concatenate([grad_bc, grad_kv, grad_mix_own, grad_step], axis=1)
            if layer == 0:
                grad_in = after(grad_in, folded[layer][0])
            at_heads = [
                jnp.where(kv_head == head, grad_kv[:, part * HD : (part + 1) * HD], 0)
                for part in range(2)
                for head in range(KVH)
            ]
            step_cols = lax.dynamic_update_slice(
                jnp.zeros((seq_len, 128), bf16), grad_step[:, :heads], (0, dt_start - dt_cols)
            )
            grad_share = jnp.concatenate([grad_bc] + at_heads + [step_cols], axis=1)
            if layer == 0:
                grad_share = after(grad_share, folded[0][1])
            scattered = scatter_product(grad_in, in_w, grad_share)
            if layer > 0:
                scattered = after(scattered, folded[layer][0])
            grad_normed_one = scattered[:, :D]
            share_sums.append(share_columns(scattered[:, D:].astype(bf16)))
            points[-1] += [grad_in, grad_normed_one]
            grad_stream_norm, grad_gain_one = rec["norm_one_back"](grad_normed_one)
            grad_stream = grad_middle + grad_stream_norm
            grad_mix = product_tn(rec["normed"], grad_mix_own)[:, : HD + 2 * width]
            mix_blocks = grad_mix.reshape(ctx_count, depth, HD + 2 * width)
            if layer == 0:
                folded[layer].append(fold_last(mix_blocks))
            else:
                folded[layer].append(fold_halves(jnp.concatenate([out_blocks, mix_blocks], axis=2)))
            out_grads[layer] = (
                jnp.stack([grad_gain_one, grad_gain_two]), chan_grad, grad_conv, grad_heads,
            )
        last = points[-1]
        mix_kept, mix_got = folded[0][2]
        mix_sum = (mix_kept + after(mix_got, last[3]).astype(f32)).astype(bf16)
        out_sum, mix_sum = after((folded[0][1], mix_sum), last[3])
        came[0] = [
            group_swap(after(folded[0][0], last[3])),
            group_swap(jnp.concatenate([out_sum, mix_sum], axis=2)),
        ]

        share_grads = []
        for layer in range(LAYERS):
            normed = records[layer]["normed"]
            grad_share = share_sums[LAYERS - 1 - layer]
            near = lax.dynamic_slice_in_dim(normed, (slot * members + me) * depth, depth, 1)
            far = lax.dynamic_slice_in_dim(normed, ((1 - slot) * members + me) * depth, depth, 1)
            share_far = product_tn(far, grad_share)
            if layer == 0:
                share_far = after(share_far, came[0][1])
            share_far = lax.ppermute(share_far, half_axis, SWAP)
            if layer > 0:
                share_far = after(share_far, last[3])
            share_sum = product_tn(near, grad_share).astype(f32) + share_far.astype(f32)
            share_sum = share_sum.astype(bf16)
            for axis in tp_axes[::-1]:
                got = lax.ppermute(share_sum, axis, SWAP)
                first = lax.axis_index(axis) == 0
                share_sum = jnp.where(
                    first,
                    jnp.concatenate([share_sum, got], 1),
                    jnp.concatenate([got, share_sum], 1),
                )
            share_grads.append(share_sum[:, :share_cols].astype(f32))
        share_g = jnp.stack(share_grads)
        both_out = bring_out(jnp.stack([stream, grad_stream]))
        activations, input_grad = both_out[:, :, 0], both_out[:, :, 1]

        def weight_grads(layer):
            got = came[layer] if layer == 0 else after(came[layer], last[3])
            ffn_came, both_came = got
            out_came, mix_came = both_came[:, :, : HD + width], both_came[:, :, HD + width :]
            mix = jnp.concatenate(
                [
                    join_heads(mix_came[:, :, HD : HD + width], 1),
                    join_heads(mix_came[:, :, HD + width :], 1),
                    join_query_heads(mix_came[:, :, :HD], 1),
                ],
                axis=1,
            ).astype(f32)
            out = jnp.concatenate(
                [join_heads(out_came[:, :, HD:], 1), join_query_heads(out_came[:, :, :HD], 1)],
                axis=1,
            )
            up = jnp.concatenate(
                [
                    ffn_came[g, :, part * ff_own : (part + 1) * ff_own]
                    for part in range(2)
                    for g in range(members)
                ],
                axis=1,
            ).astype(f32)
            down = jnp.concatenate([ffn_came[g, :, 2 * ff_own :] for g in range(members)], axis=1)
            return mix, out.T.astype(f32), up, down.T.astype(f32)

        by_layer = [weight_grads(layer) for layer in range(LAYERS)]
        mix_g, out_g, up_g, down_g = (jnp.stack(grads) for grads in zip(*by_layer))
        gain_g, chan_g, conv_g, head_g = (jnp.stack(grads) for grads in zip(*out_grads))
        chan_rows = jnp.zeros((LAYERS, CONV + 2, HGROUPS, heads, replicas, lanes), f32)
        chan_rows = lax.dynamic_update_slice(
            chan_rows,
            chan_g.reshape(LAYERS, CONV + 2, 1, heads, 1, lanes),
            (0, 0, head_group, 0, head_part, 0),
        ).reshape(LAYERS, CONV + 2, ssm_cols)
        head_rows = lax.dynamic_update_slice(
            jnp.zeros((LAYERS, 3, HGROUPS, heads), f32), head_g[:, :, None], (0, 0, head_group, 0)
        ).reshape(LAYERS, 3, tp_heads)

        def packed(arrays):
            flat = jnp.concatenate([a.reshape(-1) for a in arrays])
            return jnp.pad(flat, (0, -flat.shape[0] % 1024)).reshape(-1, 128)

        def unpacked(flat, arrays):
            flat, marks = flat.reshape(-1), [0]
            for a in arrays:
                marks.append(marks[-1] + a.size)
            return [flat[marks[k] : marks[k + 1]].reshape(a.shape) for k, a in enumerate(arrays)]

        early = (conv_g, gain_g[0, 1], gain_g[1:])
        whole = sum_over(packed(early), tp_axes[::-1])
        local_sums = (chan_rows, head_rows, whole)
        chan_sum, head_sum, whole = unpacked(
            sum_over(packed(local_sums), group_axes[::-1] + (half_axis,)), local_sums
        )
        conv_sum, gain_two, gain_rest = unpacked(whole, early)
        ctx_index = slot * members + me
        last_gain = jnp.repeat(gain_g[0, 0].reshape(ctx_count, 1, depth), 4, axis=1)
        last_gain = lax.all_to_all(
            last_gain.reshape(4 * ctx_count, 1, depth), all_axes, 0, 0, tiled=True
        )
        last_gain = jnp.sum(last_gain, axis=0)
        gain_rest = lax.dynamic_slice_in_dim(gain_rest, ctx_index * depth, depth, 2)
        gain_two = lax.dynamic_slice_in_dim(gain_two, ctx_index * depth, depth, 0)
        gain_own = jnp.concatenate([jnp.concatenate([last_gain, gain_two[None]])[None], gain_rest])
        return (
            activations,
            input_grad,
            gain_own,
            mix_g,
            share_g,
            chan_sum,
            conv_sum,
            head_sum,
            out_g,
            up_g,
            down_g,
        )

    return local


def solution(mesh):
    ctx_bits = mesh.shape["ctx"].bit_length() - 1
    tp_bits = mesh.shape["tp"].bit_length() - 1
    ctx_axes = tuple(f"c{k}" for k in range(ctx_bits))
    tp_axes = tuple(f"t{k}" for k in range(tp_bits))
    fine = Mesh(mesh.devices.reshape((2,) * (ctx_bits + tp_bits)), ctx_axes + tp_axes)
    return jax.shard_map(
        build(ctx_axes, tp_axes),
        mesh=fine,
        in_specs=(
            P(None, None, ctx_axes, None),
            P(None, None, ctx_axes, None),
            P(),
            P(None, None, ctx_axes),
            P(None, ctx_axes, tp_axes),
            P(None, ctx_axes, None),
            P(None, None, tp_axes),
            P(),
            P(None, None, tp_axes),
            P(None, tp_axes, ctx_axes),
            P(None, ctx_axes, tp_axes),
            P(None, tp_axes, ctx_axes),
        ),
        out_specs=(
            P(None, None, ctx_axes, None),
            P(None, None, ctx_axes, None),
            P(None, None, ctx_axes),
            P(None, ctx_axes, tp_axes),
            P(None, ctx_axes, None),
            P(None, None, tp_axes),
            P(),
            P(None, None, tp_axes),
            P(None, tp_axes, ctx_axes),
            P(None, ctx_axes, tp_axes),
            P(None, tp_axes, ctx_axes),
        ),
        check_vma=False,
    )
```

```python
import functools

import jax
import jax.numpy as jnp
from jax import lax
from jax.experimental import pallas as pl
from jax.experimental.pallas import tpu as pltpu
from jax.sharding import Mesh
from jax.sharding import PartitionSpec as P

D = 2048
MH = 48
P_SIZE = 64
N = 256
CONV = 4
AH = 8
KVH = 2
HD = 128
FF = 4096
LAYERS = 2
HGROUPS = 4
PAD = 8

eps_norm = 1e-05
rope_base = 100000000000.0
highest = lax.Precision.HIGHEST
SWAP = [(0, 1), (1, 0)]
bf16 = jnp.bfloat16
f32 = jnp.float32


def matmul(left_op, right_op):
    return jnp.dot(left_op, right_op, preferred_element_type=f32)


def matmul_tn(left_op, right_op):
    return lax.dot_general(left_op, right_op, (((0,), (0,)), ((), ())), preferred_element_type=f32)


def matmul_nt(left_op, right_op):
    return lax.dot_general(left_op, right_op, (((1,), (1,)), ((), ())), preferred_element_type=f32)


def product_tn_block(left, right, out):
    out[...] = dot_tn(left[...], right[...]).astype(bf16)


def product_tn(left, right):
    rows, m = left.shape
    n = right.shape[1]
    block = min(m, 1024 if rows <= 768 else 256)
    return pl.pallas_call(
        product_tn_block,
        grid=(m // block,),
        in_specs=[
            pl.BlockSpec((rows, block), lambda i: (0, i)),
            pl.BlockSpec((rows, n), lambda i: (0, 0)),
        ],
        out_specs=pl.BlockSpec((block, n), lambda i: (i, 0)),
        out_shape=jax.ShapeDtypeStruct((m, n), bf16),
        compiler_params=pltpu.CompilerParams(vmem_limit_bytes=30 * 2**20),
        cost_estimate=pl.CostEstimate(
            flops=2 * rows * m * n, bytes_accessed=2 * (rows * m + rows * n + m * n), transcendentals=0
        ),
    )(left, right)


def silu_grad(inputs):
    sigmoid = jax.nn.sigmoid(inputs)
    return sigmoid * (1.0 + inputs * (1.0 - sigmoid))


def after(x, point):
    return lax.optimization_barrier((x, point))[0]


def pick(x, dim, index):
    return lax.dynamic_index_in_dim(x, index, dim, keepdims=False)


def norm_piece(stream, gain_row):
    factor = lax.rsqrt(jnp.mean(stream * stream, axis=-1, keepdims=True) + eps_norm)
    return stream * factor * gain_row


def dot_nn(a, b):
    return lax.dot_general(a, b, (((1,), (0,)), ((), ())), preferred_element_type=f32)


def dot_nt(a, b):
    return lax.dot_general(a, b, (((1,), (1,)), ((), ())), preferred_element_type=f32)


def dot_tn(a, b):
    return lax.dot_general(a, b, (((0,), (0,)), ((), ())), preferred_element_type=f32)


def dot_exact(a, b):
    return lax.dot_general(
        a, b, (((1,), (0,)), ((), ())), precision=highest, preferred_element_type=f32
    )


def sigmoid(v):
    return 1.0 / (1.0 + jnp.exp(-v))


def block_place(block, members):
    quarter, at = block // members, block % members
    if quarter < 2:
        return at, 0, quarter
    return members - 1 - at, 1, 3 - quarter


class Plan:
    def __init__(self, seq_len, block_len, heads, lanes):
        self.seq_len = seq_len
        self.block_len = block_len
        self.heads = heads
        self.lanes = lanes
        self.width = heads * lanes
        self.members = seq_len // (4 * block_len)
        self.chunk = 4 * block_len
        self.chunks = seq_len // self.chunk
        self.query_parts = self.members // 2
        self.query_rows = seq_len // self.query_parts
        self.bc = 2 * N
        self.key_at = self.bc
        self.value_at = self.bc + HD
        self.q_at = self.bc + 2 * HD
        self.gate_at = self.bc + 3 * HD
        self.pair_cols = 2 * self.width
        self.pair_tiles = self.pair_cols + -self.pair_cols % 128
        self.step_at = self.gate_at + self.pair_tiles
        self.cols = self.step_at + 128

    def rows(self, core, block):
        member, half, place = block_place(block, self.members)
        other = core if place == 0 else 1 - core
        start = other * (self.seq_len // 2) + (2 * member + half) * self.block_len
        return pl.ds(pl.multiple_of(start, 16), self.block_len)

    def blocks(self):
        return range(self.seq_len // self.block_len)


def head_masks(plan):
    lane = lax.broadcasted_iota(jnp.int32, (1, plan.width), 1)
    return [
        ((lane >= h * plan.lanes) & (lane < (h + 1) * plan.lanes)).astype(f32)
        for h in range(plan.heads)
    ]


def over_heads(plan, tile, masks):
    return sum(tile[:, h : h + 1] * masks[h] for h in range(plan.heads))


def per_head(plan, values, masks):
    lane = lax.broadcasted_iota(jnp.int32, (1, 128), 1)
    total = None
    for h in range(plan.heads):
        column = jnp.sum(values * masks[h], axis=1, keepdims=True)
        part = column * (lane == h).astype(f32)
        total = part if total is None else total + part
    return total


def conv_values(source, taps_ref, rows, start, low, high):
    total = taps_ref[CONV : CONV + 1, low:high]
    for k in range(CONV):
        at = PAD + start - (CONV - 1) + k
        total = total + taps_ref[k : k + 1, low:high] * source[pl.ds(at, rows), low:high]
    return total


def prepare(plan, core, mixed, nat_bc, nat_x, nat_step):
    width = plan.width
    nat_bc[0:PAD, :] = jnp.zeros((PAD, plan.bc), f32)
    nat_x[0:PAD, :] = jnp.zeros((PAD, width), f32)
    for block in plan.blocks():
        at = PAD + block * plan.block_len
        rows = plan.rows(core, block)
        nat_bc[pl.ds(at, plan.block_len), :] = mixed[rows, 0 : plan.bc]
        pair = mixed[rows, plan.gate_at : plan.gate_at + plan.pair_tiles]
        nat_x[pl.ds(at, plan.block_len), :] = pltpu.roll(pair, plan.pair_tiles - width, 1)[:, :width]
        nat_step[pl.ds(at - PAD, plan.block_len), :] = mixed[rows, plan.step_at : plan.step_at + 128]


def chunk_decays(plan, nat_step, head_rows, c, tri):
    q = plan.chunk
    real = lax.broadcasted_iota(jnp.int32, (1, 128), 1) < plan.heads
    raw = jnp.where(real, nat_step[pl.ds(c * q, q), :] + head_rows[1:2, :], 0.0)
    step = jnp.where(real, jnp.maximum(raw, 0.0) + jnp.log(1.0 + jnp.exp(-jnp.abs(raw))), 0.0)
    cumulative = dot_exact(tri, step * head_rows[0:1, :])
    return raw, step, cumulative


def triangle(plan):
    q = plan.chunk
    row = lax.broadcasted_iota(jnp.int32, (q, q), 0)
    col = lax.broadcasted_iota(jnp.int32, (q, q), 1)
    return row, col


def ssm_forward(plan, core_ref, mixed, taps, shared_taps, head_rows, y_out, low_out, states_out, squares_out,
                nat_bc, nat_x, nat_step):
    q = plan.chunk
    masks = head_masks(plan)
    core = core_ref[0]
    prepare(plan, core, mixed, nat_bc, nat_x, nat_step)
    row, col = triangle(plan)
    lower = row >= col
    tri = lower.astype(f32)
    state = jnp.zeros((N, plan.width), f32)
    for c in range(plan.chunks):
        start = c * q
        x = conv_values(nat_x, taps, q, start, 0, plan.width)
        x = x * sigmoid(x)
        bc = conv_values(nat_bc, shared_taps, q, start, 0, plan.bc)
        bc = (bc * sigmoid(bc)).astype(bf16)
        b, cc = bc[:, :N], bc[:, N:]
        _, step, cum = chunk_decays(plan, nat_step, head_rows, c, tri)
        cum_rows = cum.T
        cum_full = over_heads(plan, cum, masks)
        total_full = cum_full[q - 1 : q, :]
        u = x * over_heads(plan, step, masks)
        inner = dot_nt(cc, b)
        states_out[c] = state
        y = dot_nn(cc, state.astype(bf16)) * jnp.exp(cum_full) + taps[6:7, :] * x
        for h in range(plan.heads):
            seg = jnp.where(lower, cum[:, h : h + 1] - cum_rows[h : h + 1, :], -1e30)
            mixing = (jnp.exp(seg) * inner).astype(bf16)
            y = y + dot_nn(mixing, (u * masks[h]).astype(bf16))
        weighted = (u * jnp.exp(total_full - cum_full)).astype(bf16)
        state = jnp.exp(total_full) * state + dot_tn(b, weighted)
        for k in range(4):
            block = 4 * c + k
            y_out[plan.rows(core, block), :] = y[k * plan.block_len : (k + 1) * plan.block_len, :]
    z = mixed[:, plan.gate_at : plan.gate_at + plan.width]
    gated = y_out[...] * (z * sigmoid(z))
    low_out[...] = (gated * taps[5:6, :]).astype(bf16)
    squares_out[...] = lax.dot_general(
        jnp.ones((8, plan.width), f32), gated * gated, (((1,), (1,)), ((), ())),
        precision=highest, preferred_element_type=f32,
    )


def ssm_backward(plan, core_ref, mixed, taps, shared_taps, head_rows, y_in, states, grad_mixer, scales,
                 bc_out, pair_out, step_out, taps_out, shared_out, heads_out,
                 nat_bc, nat_x, nat_step, nat_dy, grad_x, grad_bc, grad_y_ref):
    q = plan.chunk
    width = plan.width
    masks = head_masks(plan)
    core = core_ref[0]
    prepare(plan, core, mixed, nat_bc, nat_x, nat_step)
    row, col = triangle(plan)
    lower, upper = row >= col, row <= col
    strict_lower, strict_upper = row > col, row < col
    tri, tri_back = lower.astype(f32), upper.astype(f32)

    z = mixed[:, plan.gate_at : plan.gate_at + width]
    y = y_in[...]
    sig = sigmoid(z)
    silu = z * sig
    gated = y * silu
    scaled = grad_mixer[:, HD : HD + width] * scales[:, 0:1]
    grad_gated = scaled * taps[5:6, :] + scales[:, 1:2] * gated
    gain_grad = jnp.sum(scaled * gated, axis=0, keepdims=True)
    grad_z = grad_gated * y * (sig * (1.0 + z * (1.0 - sig)))
    spare = plan.pair_tiles - width
    pair_out[...] = jnp.concatenate(
        [grad_z, jnp.zeros((plan.seq_len, spare), f32)], axis=1
    ).astype(bf16)
    grad_y_ref[...] = grad_gated * silu
    for block in plan.blocks():
        at = block * plan.block_len
        nat_dy[pl.ds(at, plan.block_len), :] = grad_y_ref[plan.rows(core, block), :]

    grad_x[plan.seq_len : plan.seq_len + PAD, :] = jnp.zeros((PAD, width), f32)
    grad_bc[plan.seq_len : plan.seq_len + PAD, :] = jnp.zeros((PAD, plan.bc), f32)
    grad_state = jnp.zeros((N, width), f32)
    skip_grad = jnp.zeros((1, width), f32)
    rate_grad = jnp.zeros((1, 128), f32)
    bias_grad = jnp.zeros((1, 128), f32)
    for c in reversed(range(plan.chunks)):
        start = c * q
        x_lin = conv_values(nat_x, taps, q, start, 0, width)
        x_sig = sigmoid(x_lin)
        x = x_lin * x_sig
        bc_lin = conv_values(nat_bc, shared_taps, q, start, 0, plan.bc)
        bc_sig = sigmoid(bc_lin)
        bc = (bc_lin * bc_sig).astype(bf16)
        b, cc = bc[:, :N], bc[:, N:]
        raw, step, cum = chunk_decays(plan, nat_step, head_rows, c, tri)
        cum_rows = cum.T
        cum_full = over_heads(plan, cum, masks)
        total_full = cum_full[q - 1 : q, :]
        step_full = over_heads(plan, step, masks)
        u = x * step_full
        u_low = u.astype(bf16)
        dy = nat_dy[pl.ds(start, q), :]
        dy_low = dy.astype(bf16)
        state = states[c]
        state_low = state.astype(bf16)
        grad_state_low = grad_state.astype(bf16)
        entry = jnp.exp(cum_full)
        exit_w = jnp.exp(total_full - cum_full)
        total_decay = jnp.exp(total_full)
        dy_entry = (dy * entry).astype(bf16)
        grad_c = dot_nt(dy_entry, state_low)
        carried = dot_nn(cc, state_low) * entry
        du_state = dot_nn(b, grad_state_low) * exit_w
        grad_b = dot_nt((u * exit_w).astype(bf16), grad_state_low)
        inner = dot_nt(cc, b)
        inner_t = dot_nt(b, cc)
        du = du_state
        grad_inner = jnp.zeros((q, q), f32)
        grad_inner_t = jnp.zeros((q, q), f32)
        lane = lax.broadcasted_iota(jnp.int32, (1, 128), 1)
        dcum = per_head(plan, dy * carried - u * du_state, masks)
        for h in range(plan.heads):
            here = (lane == h).astype(f32)
            u_head = (u * masks[h]).astype(bf16)
            dy_head = (dy * masks[h]).astype(bf16)
            seg = cum[:, h : h + 1] - cum_rows[h : h + 1, :]
            decay = jnp.exp(jnp.where(lower, seg, -1e30))
            decay_t = jnp.exp(jnp.where(upper, -seg, -1e30))
            grad_mix = dot_nt(dy_head, u_low) * decay
            grad_mix_t = dot_nt(u_head, dy_low) * decay_t
            grad_inner = grad_inner + grad_mix
            grad_inner_t = grad_inner_t + grad_mix_t
            du = du + dot_nn((decay_t * inner_t).astype(bf16), dy_head)
            out_sum = jnp.sum(jnp.where(strict_lower, grad_mix * inner, 0.0), axis=1, keepdims=True)
            in_sum = jnp.sum(
                jnp.where(strict_upper, grad_mix_t * inner_t, 0.0), axis=1, keepdims=True
            )
            dcum = dcum + (out_sum - in_sum) * here
        grad_c = grad_c + dot_nn(grad_inner.astype(bf16), b)
        grad_b = grad_b + dot_nn(grad_inner_t.astype(bf16), cc)
        whole = jnp.sum(u * du_state, axis=0, keepdims=True) + jnp.sum(
            grad_state * state, axis=0, keepdims=True
        ) * total_decay
        dlog = dot_exact(tri_back, dcum) + per_head(plan, whole, masks)
        rate_grad = rate_grad + jnp.sum(dlog * step, axis=0, keepdims=True)
        grad_step = dlog * head_rows[0:1, :] + per_head(plan, du * x, masks)
        grad_raw = grad_step * sigmoid(raw)
        bias_grad = bias_grad + jnp.sum(grad_raw, axis=0, keepdims=True)
        grad_xc = du * step_full + taps[6:7, :] * dy
        skip_grad = skip_grad + jnp.sum(dy * x, axis=0, keepdims=True)
        grad_state = total_decay * grad_state + dot_tn(cc, dy_entry)
        grad_x[pl.ds(start, q), :] = grad_xc * (x_sig * (1.0 + x_lin * (1.0 - x_sig)))
        grad_bc[pl.ds(start, q), :] = jnp.concatenate([grad_b, grad_c], axis=1) * (
            bc_sig * (1.0 + bc_lin * (1.0 - bc_sig))
        )
        for k in range(4):
            step_out[plan.rows(core, 4 * c + k), :] = grad_raw[
                k * plan.block_len : (k + 1) * plan.block_len, :
            ].astype(bf16)

    size = plan.block_len
    tap_grads = [jnp.zeros((1, width), f32) for _ in range(CONV + 1)]
    shared_grads = [jnp.zeros((1, plan.bc), f32) for _ in range(CONV + 1)]
    lane = lax.broadcasted_iota(jnp.int32, (1, plan.pair_tiles), 1)
    for c in range(plan.chunks):
        start = c * q
        dx = grad_x[pl.ds(start, q), :]
        dbc = grad_bc[pl.ds(start, q), :]
        tap_grads[CONV] += jnp.sum(dx, axis=0, keepdims=True)
        shared_grads[CONV] += jnp.sum(dbc, axis=0, keepdims=True)
        pre_dx = None
        pre_dbc = None
        for k in range(CONV):
            at = PAD + start - (CONV - 1) + k
            tap_grads[k] += jnp.sum(dx * nat_x[pl.ds(at, q), :], axis=0, keepdims=True)
            shared_grads[k] += jnp.sum(dbc * nat_bc[pl.ds(at, q), :], axis=0, keepdims=True)
            ahead = start + (CONV - 1) - k
            part = taps[k : k + 1, :] * grad_x[pl.ds(ahead, q), :]
            pre_dx = part if k == 0 else pre_dx + part
            part = shared_taps[k : k + 1, :] * grad_bc[pl.ds(ahead, q), :]
            pre_dbc = part if k == 0 else pre_dbc + part
        tile = jnp.concatenate([pre_dx, jnp.zeros((q, spare), f32)], axis=1)
        tile = pltpu.roll(tile, width, 1).astype(bf16)
        for k in range(4):
            rows = plan.rows(core, 4 * c + k)
            pair_out[rows, :] = jnp.where(
                lane < width, pair_out[rows, :], tile[k * size : (k + 1) * size, :]
            )
            bc_out[rows, :] = pre_dbc[k * size : (k + 1) * size, :].astype(bf16)
    for k in range(CONV + 1):
        taps_out[k : k + 1, :] = tap_grads[k]
        shared_out[k : k + 1, :] = shared_grads[k]
    taps_out[5:6, :] = gain_grad
    taps_out[6:7, :] = skip_grad
    heads_out[0:1, :] = rate_grad * head_rows[0:1, :]
    heads_out[1:2, :] = bias_grad


def whole_specs(arrays):
    def spec(array):
        zeros = (0,) * len(array.shape)
        return pl.BlockSpec(array.shape, lambda i: zeros, pipeline_mode=pl.Buffered(1))

    return [spec(array) for array in arrays]


def call_whole(plan, kernel, outs, scratch, flops, inputs, scalars=()):
    return pl.pallas_call(
        kernel,
        grid=(1,),
        in_specs=[pl.BlockSpec(memory_space=pltpu.SMEM) for _ in scalars] + whole_specs(inputs),
        out_specs=tuple(whole_specs(outs)),
        out_shape=tuple(outs),
        scratch_shapes=scratch,
        compiler_params=ssm_params(plan),
        cost_estimate=pl.CostEstimate(
            flops=flops, bytes_accessed=plan.seq_len * 8192, transcendentals=0
        ),
    )(*scalars, *inputs)


def ssm_params(plan):
    limit = 58 * 2**20
    return pltpu.CompilerParams(vmem_limit_bytes=limit)


def run_forward(plan, core, *inputs):
    t, w = plan.seq_len, plan.width
    outs = [
        jax.ShapeDtypeStruct((t, w), f32),
        jax.ShapeDtypeStruct((t, w), bf16),
        jax.ShapeDtypeStruct((plan.chunks, N, w), f32),
        jax.ShapeDtypeStruct((8, t), f32),
    ]
    scratch = [
        pltpu.VMEM((PAD + t, plan.bc), f32),
        pltpu.VMEM((PAD + t, w), f32),
        pltpu.VMEM((t, 128), f32),
    ]
    return call_whole(
        plan, functools.partial(ssm_forward, plan), outs, scratch, 40000 * t * w, inputs, (core,)
    )


def run_backward(plan, core, *inputs):
    t, w = plan.seq_len, plan.width
    outs = [
        jax.ShapeDtypeStruct((t, plan.bc), bf16),
        jax.ShapeDtypeStruct((t, plan.pair_tiles), bf16),
        jax.ShapeDtypeStruct((t, 128), bf16),
        jax.ShapeDtypeStruct((8, w), f32),
        jax.ShapeDtypeStruct((8, plan.bc), f32),
        jax.ShapeDtypeStruct((8, 128), f32),
    ]
    scratch = [
        pltpu.VMEM((PAD + t, plan.bc), f32),
        pltpu.VMEM((PAD + t, w), f32),
        pltpu.VMEM((t, 128), f32),
        pltpu.VMEM((t, w), f32),
        pltpu.VMEM((t + PAD, w), f32),
        pltpu.VMEM((t + PAD, plan.bc), f32),
        pltpu.VMEM((t, w), f32),
    ]
    return call_whole(
        plan, functools.partial(ssm_backward, plan), outs, scratch, 90000 * t * w, inputs, (core,)
    )


def attend_scores(plan, queries, keys, query_pos, key_pos):
    scores = dot_nt(queries, keys) * HD ** (-0.5)
    return jnp.where(key_pos <= query_pos, scores, -1e30)


def turned(x, cosine, sine):
    return x * cosine + pltpu.roll(x, HD // 2, 1) * sine


def attend_forward(plan, part, mixed, cosine, sine, query_pos, key_pos,
                   att_out, log_out, q_out, kv_out):
    rows = pl.ds(pl.multiple_of(part[0] * plan.query_rows, 8), plan.query_rows)
    keys = turned(mixed[:, plan.key_at : plan.key_at + HD], cosine[...], sine[...]).astype(bf16)
    values = mixed[:, plan.value_at : plan.value_at + HD].astype(bf16)
    kv_out[:, :HD] = keys
    kv_out[:, HD:] = values
    queries = mixed[rows, plan.q_at : plan.q_at + HD]
    queries = turned(queries, cosine[rows, :], sine[rows, :]).astype(bf16)
    q_out[...] = queries
    scores = attend_scores(plan, queries, keys, query_pos[rows, :], key_pos[...])
    peak = jnp.max(scores, axis=1, keepdims=True)
    weights = jnp.exp(scores - peak)
    total = jnp.sum(weights, axis=1, keepdims=True)
    probs = (weights / total).astype(bf16)
    att_out[...] = jnp.zeros((plan.seq_len, HD), bf16)
    att_out[rows, :] = dot_nn(probs, values).astype(bf16)
    log_out[...] = peak + jnp.log(total)


def attend_backward(plan, part, queries, kv, logs, grad_mixer, cosine, sine, query_pos, key_pos,
                    q_out, kv_out):
    rows = pl.ds(pl.multiple_of(part[0] * plan.query_rows, 8), plan.query_rows)
    keys, values = kv[:, :HD], kv[:, HD:]
    scale = HD ** (-0.5)
    q, grad = queries[...], grad_mixer[rows, :HD].astype(bf16)
    probs = jnp.exp(attend_scores(plan, q, keys, query_pos[rows, :], key_pos[...]) - logs[...])
    grad_probs = dot_nt(grad, values)
    inner = jnp.sum(probs * grad_probs, axis=1, keepdims=True)
    grad_scores = (probs * (grad_probs - inner)).astype(bf16)
    grad_q = dot_nn(grad_scores, keys) * scale
    q_out[...] = jnp.zeros((plan.seq_len, HD), bf16)
    q_out[rows, :] = turned(grad_q, cosine[rows, :], -sine[rows, :]).astype(bf16)
    grad_k = dot_tn(grad_scores, q) * scale
    kv_out[:, :HD] = turned(grad_k, cosine[...], -sine[...]).astype(bf16)
    kv_out[:, HD:] = dot_tn(probs.astype(bf16), grad).astype(bf16)


def run_attend(plan, part, *inputs):
    t, rows = plan.seq_len, plan.query_rows
    outs = [
        jax.ShapeDtypeStruct((t, HD), bf16),
        jax.ShapeDtypeStruct((rows, 1), f32),
        jax.ShapeDtypeStruct((rows, HD), bf16),
        jax.ShapeDtypeStruct((t, 2 * HD), bf16),
    ]
    kernel = functools.partial(attend_forward, plan)
    return call_whole(plan, kernel, outs, [], 4 * rows * t * HD, inputs, (part,))


def run_attend_back(plan, part, *inputs):
    t = plan.seq_len
    outs = [jax.ShapeDtypeStruct((t, HD), bf16), jax.ShapeDtypeStruct((t, 2 * HD), bf16)]
    kernel = functools.partial(attend_backward, plan)
    return call_whole(plan, kernel, outs, [], 10 * plan.query_rows * t * HD, inputs, (part,))


def build(ctx_axes, tp_axes):
    half_axis = ctx_axes[0]
    group_axes = ctx_axes[1:]
    t_half, t_core = tp_axes
    ring_axes = group_axes + (t_half,)
    slot_axes = group_axes + tp_axes
    all_axes = ctx_axes + tp_axes
    span = len(ring_axes)

    def column_parts(width):
        unit = width // 128
        marks = [0] + [128 * (unit * (k + 1) // 3) for k in range(3)]
        return list(zip(marks[:-1], marks[1:]))

    def rotated(part):
        turn = part % span
        return ring_axes[turn:] + ring_axes[:turn]

    def gather_rows(x):
        rows, width = x.shape
        parts = []
        for part, (low, high) in enumerate(column_parts(width)):
            held = x[:, low:high].reshape((1,) * span + (rows, high - low))
            for axis in rotated(part):
                dim = ring_axes.index(axis)
                got = lax.ppermute(held, axis, SWAP)
                first = lax.axis_index(axis) == 0
                held = jnp.where(
                    first, jnp.concatenate([held, got], dim), jnp.concatenate([got, held], dim)
                )
            parts.append(held)
        held = lax.optimization_barrier(jnp.concatenate(parts, -1).reshape(-1, width))
        return jnp.concatenate([held, lax.ppermute(held, t_core, SWAP)])

    def scatter_product(left, right, extra=None):
        total = left.shape[0]
        width = right.shape[0]
        peers = 2 ** (span + 1)
        rows = total // peers
        own = total // 2
        sent = matmul_nt(left[own:], right).astype(bf16)
        kept = matmul_nt(left[:own], right)
        if extra is not None:
            width += extra.shape[1]
            sent = jnp.concatenate([sent, extra[own:]], axis=1)
            kept = jnp.concatenate([kept, extra[:own].astype(f32)], axis=1)
        held = kept + lax.ppermute(sent, t_core, SWAP).astype(f32)
        parts = []
        for part, (low, high) in enumerate(column_parts(width)):
            piece = held[:, low:high].reshape((2,) * span + (rows, high - low))
            names = list(ring_axes)
            for axis in rotated(part):
                dim = names.index(axis)
                names.pop(dim)
                index = lax.axis_index(axis)
                got = lax.ppermute(pick(piece, dim, 1 - index).astype(bf16), axis, SWAP)
                piece = pick(piece, dim, index) + got.astype(f32)
            parts.append(piece)
        return jnp.concatenate(parts, -1)

    def sum_slot(x):
        turn = lax.axis_index(t_core) == 1
        x = x.reshape(2, -1, 128)
        x = jnp.where(turn, x[::-1], x)
        came = lax.all_to_all(
            jnp.broadcast_to(x[None], (2 ** (span + 1),) + x.shape), slot_axes, 0, 0, tiled=True
        )
        x = jnp.sum(came, axis=0)
        return jnp.where(turn, x[::-1], x).reshape(-1, 1)

    def sum_over(x, axes):
        for axis in axes:
            x = x + lax.ppermute(x, axis, SWAP)
        return x

    def group_index():
        return lax.axis_index(group_axes)

    def group_swap(blocks):
        return lax.all_to_all(blocks, group_axes, 0, 0, tiled=True)

    def both_halves(came):
        return lax.all_gather(came, half_axis, axis=0, tiled=True)

    def spread_first(blocks):
        return lax.all_to_all(jnp.concatenate([blocks, blocks]), ctx_axes, 0, 0, tiled=True)

    def fold_halves(blocks):
        return lax.psum_scatter(blocks.astype(bf16), half_axis, scatter_dimension=0, tiled=True)

    def fold_last(blocks):
        half = lax.axis_index(half_axis)
        paired = blocks.reshape((2, blocks.shape[0] // 2) + blocks.shape[1:])
        got = lax.ppermute(pick(paired, 0, 1 - half).astype(bf16), half_axis, SWAP)
        return pick(paired, 0, half).astype(f32), got

    def gather_lanes(x):
        for axis in ctx_axes[::-1]:
            got = lax.ppermute(x, axis, SWAP)
            first = lax.axis_index(axis) == 0
            x = jnp.where(first, jnp.concatenate([x, got], -1), jnp.concatenate([got, x], -1))
        return x

    def local(
        hidden,
        cotangent,
        lengths,
        norm_gains,
        mix_weight,
        share_weight,
        chan_params,
        shared_conv,
        head_params,
        out_weight,
        up_weight,
        down_weight,
    ):
        members = 2 ** len(group_axes)
        ctx_count = 2 * members
        replicas = members // HGROUPS
        slot = lax.axis_index(half_axis)
        me = group_index()
        head_group = me // replicas
        head_part = me % replicas
        tp_half = lax.axis_index(t_half)
        tp_core = lax.axis_index(t_core)
        tp_index = tp_half * 2 + tp_core
        block_len = hidden.shape[2]
        depth = mix_weight.shape[1]
        seq_len = 2 * ctx_count * block_len
        own_len = 4 * block_len
        tp_heads = chan_params.shape[2] // P_SIZE
        heads = tp_heads // HGROUPS
        lanes = P_SIZE // replicas
        width = heads * lanes
        ssm_cols = tp_heads * P_SIZE
        qheads = AH // 4
        q_cols = qheads * HD
        ff_tp = FF // 4
        ff_own = ff_tp // members
        plan = Plan(seq_len, block_len, heads, lanes)
        own_head = me // plan.query_parts
        core_scalar = tp_core.astype(jnp.int32).reshape(1)
        query_part = (me % plan.query_parts).astype(jnp.int32).reshape(1)
        share_cols = share_weight.shape[2]
        kv_cols = 2 * N
        dt_cols = 2 * N + 2 * KVH * HD
        kv_head = tp_index * qheads // (AH // KVH)
        score_scale = HD ** (-0.5)

        def block_of(member, half, cube):
            near = cube * members + member
            return jnp.where(half == 0, near, 2 * ctx_count - 1 - near)

        within = jnp.arange(block_len)
        own_pos = block_of(me, tp_half, tp_core) * block_len + within
        own_valid = (own_pos < lengths[slot]).astype(f32)[:, None]
        ring = jnp.arange(2 * members)

        def core_positions(core):
            first = block_of(ring // 2, ring % 2, core) * block_len
            return (first[:, None] + within[None, :]).reshape(-1)

        key_pos = jnp.concatenate([core_positions(tp_core), core_positions(1 - tp_core)])
        half_dim = HD // 2
        inverse = jnp.exp(-jnp.log(rope_base) * (2.0 * jnp.arange(half_dim, dtype=f32) / HD))
        angles = key_pos.astype(f32)[:, None] * inverse
        cosine = jnp.concatenate([jnp.cos(angles)] * 2, axis=1)
        sine = jnp.concatenate([-jnp.sin(angles), jnp.sin(angles)], axis=1)

        tables = (cosine, sine, key_pos[:, None], key_pos[None, :])

        def cut_query_heads(x, axis):
            shape = x.shape
            split = x.reshape(shape[:axis] + (qheads, HD) + shape[axis + 1 :])
            return jnp.repeat(jnp.moveaxis(split, axis, 0), plan.query_parts, axis=0)

        def join_query_heads(x, axis):
            summed = jnp.sum(
                x.astype(f32).reshape((qheads, plan.query_parts) + x.shape[1:]), axis=1
            ).astype(bf16)
            joined = jnp.moveaxis(summed, 0, axis)
            shape = joined.shape
            return joined.reshape(shape[:axis] + (q_cols,) + shape[axis + 2 :])

        def bring_in(x):
            got = lax.ppermute(
                pick(pick(x, 0, 1 - slot), 0, tp_half), (half_axis, t_core), [(0, 2), (3, 1)]
            )
            return jnp.where(tp_core == slot, pick(pick(x, 0, slot), 0, tp_half), got)

        def share_columns(own):
            quarter = own.shape[1] // 4
            chunks = jnp.moveaxis(own.reshape(block_len, 4, quarter), 1, 0)
            chunks = jnp.broadcast_to(chunks[None], (members,) + chunks.shape)
            rows = lax.all_to_all(
                chunks.reshape(4 * members, block_len, quarter), slot_axes, 0, 0, tiled=True
            )
            rows = jnp.moveaxis(rows.reshape(2 * members, 2, block_len, quarter), 1, 0)
            return jnp.where(tp_core == 0, rows, rows[::-1]).reshape(seq_len, quarter)

        def bring_out(x):
            x = x.astype(bf16)
            got = lax.ppermute(x, (half_axis, t_core), [(1, 3), (2, 0)])
            pair = jnp.where(slot == 0, jnp.stack([x, got]), jnp.stack([got, x]))
            other = lax.ppermute(pair, t_core, SWAP)
            pair = jnp.where(tp_core == slot, pair, other)
            other = lax.ppermute(pair, t_half, SWAP)
            both = jnp.where(tp_half == 0, jnp.stack([pair, other], 1), jnp.stack([other, pair], 1))
            return both.astype(f32)

        def cut_heads(x, axis):
            shape = x.shape
            split = x.reshape(
                shape[:axis] + (HGROUPS, heads, replicas, lanes) + shape[axis + 1 :]
            )
            split = jnp.moveaxis(split, (axis, axis + 2), (0, 1))
            return split.reshape((members,) + shape[:axis] + (width,) + shape[axis + 1 :])

        def join_heads(x, axis):
            if replicas == 1:
                return jnp.concatenate([x[g] for g in range(members)], axis=axis)
            shape = x.shape[1:]
            split = x.reshape(
                (HGROUPS, replicas) + shape[:axis] + (heads, lanes) + shape[axis + 1 :]
            )
            split = jnp.moveaxis(split, (0, 1), (axis, axis + 2))
            return split.reshape(shape[:axis] + (ssm_cols,) + shape[axis + 1 :])

        gains = gather_lanes(norm_gains).astype(f32)
        hidden_rows = bring_in(after(hidden, gains))
        stream = hidden_rows.astype(f32)
        own_chan = pick(cut_heads(chan_params, 2), 0, me)
        own_heads = pick(head_params.reshape(LAYERS, 3, HGROUPS, heads), 2, head_group)
        skip_full = jnp.repeat(own_heads[:, 2], lanes, axis=1)[:, None]
        tap_rows = jnp.concatenate([own_chan, skip_full, jnp.zeros_like(skip_full)], axis=1)
        shared_rows = jnp.pad(shared_conv, ((0, 0), (0, 3), (0, 0)))
        head_rows = jnp.pad(
            jnp.stack([-jnp.exp(own_heads[:, 0]), own_heads[:, 1]], axis=1),
            ((0, 0), (0, 6), (0, 128 - heads)),
        )
        share_rows = lax.dynamic_slice_in_dim(share_weight, tp_core * (depth // 2), depth // 2, 1)
        dt_start = dt_cols + tp_index * tp_heads + head_group * heads

        def weight_blocks(layer):
            mix = mix_weight[layer]
            mix_blocks = jnp.concatenate(
                [
                    cut_query_heads(mix[:, 2 * ssm_cols :], 1),
                    cut_heads(mix[:, :ssm_cols], 1),
                    cut_heads(mix[:, ssm_cols : 2 * ssm_cols], 1),
                ],
                2,
            )
            out = out_weight[layer].T
            out_blocks = jnp.concatenate(
                [cut_query_heads(out[:, ssm_cols:], 1), cut_heads(out[:, :ssm_cols], 1)], 2
            )
            up = up_weight[layer]
            down = down_weight[layer].T
            ffn_blocks = jnp.stack(
                [
                    jnp.concatenate(
                        [
                            up[:, g * ff_own : (g + 1) * ff_own],
                            up[:, ff_tp + g * ff_own : ff_tp + (g + 1) * ff_own],
                            down[:, g * ff_own : (g + 1) * ff_own],
                        ],
                        axis=1,
                    )
                    for g in range(members)
                ]
            )
            return mix_blocks, out_blocks, ffn_blocks

        def share_whole(share):
            share = jnp.concatenate(
                [
                    share[:, :kv_cols],
                    lax.dynamic_slice_in_dim(share, kv_cols + kv_head * HD, HD, 1),
                    lax.dynamic_slice_in_dim(share, kv_cols + (KVH + kv_head) * HD, HD, 1),
                    share[:, dt_cols:],
                ],
                axis=1,
            )
            return lax.all_gather(share, ctx_axes + (t_core,), axis=0, tiled=True)

        def input_weights(mix_own, share):
            dt_w = lax.dynamic_slice_in_dim(share, kv_cols + 2 * HD + dt_start - dt_cols, heads, 1)
            return jnp.concatenate(
                [
                    share[:, : plan.q_at],
                    jnp.pad(
                        mix_own.reshape(D, HD + 2 * width),
                        ((0, 0), (0, plan.pair_tiles - plan.pair_cols)),
                    ),
                    jnp.pad(dt_w, ((0, 0), (0, 128 - heads))),
                ],
                axis=1,
            )

        def ffn_weights(ffn_own):
            ffn_own = ffn_own.reshape(D, 3 * ff_own)
            return ffn_own[:, : 2 * ff_own], ffn_own[:, 2 * ff_own :]

        blocks = [weight_blocks(layer) for layer in range(LAYERS)]
        mix_own = [None] * LAYERS
        out_own = [None] * LAYERS
        ffn_own = [None] * LAYERS
        shares = [None] * LAYERS
        mix_own[0] = spread_first(after(blocks[0][0], hidden_rows))
        out_cols = HD + width
        hidden_all = gather_rows(hidden_rows)
        swapped = [[group_swap(x) for x in after(blocks[0][1:], hidden_all)]]
        for layer in range(1, LAYERS):
            both = group_swap(jnp.concatenate(blocks[layer][:2], axis=2))
            swapped.append([both[:, :, -out_cols:], group_swap(blocks[layer][2])])
            mix_own[layer] = both_halves(both[:, :, :-out_cols])
        for layer in range(LAYERS):
            shares[layer] = share_whole(share_rows[layer])
            out_own[layer] = both_halves(swapped[layer][0])
            ffn_own[layer] = both_halves(swapped[layer][1])

        records = []
        for layer in range(LAYERS):
            rec = {}
            normed_f, rec["norm_one_back"] = jax.vjp(norm_piece, stream, gains[layer, 0])
            if layer == 0:
                normed = norm_piece(hidden_all.astype(f32), gains[0, 0]).astype(bf16)
            else:
                normed = gather_rows(normed_f.astype(bf16))
            in_w = input_weights(*after((mix_own[layer], shares[layer]), normed))
            mixed = matmul(normed, in_w)
            mixed_here = mixed
            if layer == 0:
                mixed_here = after(mixed, (swapped[0][1], swapped[1][0]))
            ssm_y, gated_low, states, squares = run_forward(
                plan, core_scalar, mixed, tap_rows[layer], shared_rows[layer], head_rows[layer]
            )
            sum_squares = sum_slot(squares[0])
            gated_scale = lax.rsqrt(sum_squares / (MH * P_SIZE) + eps_norm)
            scaled_low = (gated_low.astype(f32) * gated_scale).astype(bf16)
            attended, logsum, queries, keyval = run_attend(plan, query_part, mixed_here, *tables)
            mixer = jnp.concatenate([attended, scaled_low], axis=1)
            out_w = after(out_own[layer], gated_low).reshape(D, HD + width)
            middle = stream + scatter_product(mixer, out_w)
            normed_two_f, rec["norm_two_back"] = jax.vjp(norm_piece, middle, gains[layer, 1])
            normed_two = gather_rows(normed_two_f.astype(bf16))
            up_w, down_w = ffn_weights(after(ffn_own[layer], normed_two))
            gate_up = matmul(normed_two, up_w)
            gate_vals, up_vals = gate_up[:, :ff_own], gate_up[:, ff_own:]
            activation = (jax.nn.silu(gate_vals) * up_vals).astype(bf16)
            stream = (middle + scatter_product(activation, down_w)) * own_valid
            rec.update(
                normed=normed, mixed=mixed, ssm_y=ssm_y, gated_low=gated_low, states=states,
                mixer=mixer, gated_scale=gated_scale, queries=queries, keyval=keyval,
                logsum=logsum, normed_two=normed_two,
                gate_vals=gate_vals, up_vals=up_vals, activation=activation,
            )
            rec["weights"] = (in_w, out_w, up_w, down_w)
            records.append(rec)

        grad_stream = bring_in(cotangent).astype(f32)
        out_grads = [None] * LAYERS
        share_sums = []
        folded = [None] * LAYERS
        points = []
        came = [[] for _ in range(LAYERS)]
        for layer in reversed(range(LAYERS)):
            rec = records[layer]
            in_w, out_w, up_w, down_w = rec["weights"]
            grad_masked = grad_stream * own_valid
            if layer == LAYERS - 1:
                grad_ffn = gather_rows(grad_masked.astype(bf16))
            else:
                grad_ffn = gather_rows(grad_masked.astype(bf16))
            points.append([grad_ffn])
            grad_activation = matmul(grad_ffn, down_w)
            grad_down = product_tn(grad_ffn, rec["activation"])
            gate_vals = rec["gate_vals"]
            grad_gate = grad_activation * rec["up_vals"] * silu_grad(gate_vals)
            grad_upper = grad_activation * jax.nn.silu(gate_vals)
            grad_gate_up = jnp.concatenate([grad_gate, grad_upper], axis=1).astype(bf16)
            if layer + 1 < LAYERS:
                came[layer + 1].append(
                    after(group_swap(after(folded[layer + 1][0], grad_ffn)), grad_gate_up)
                )
            grad_upw = product_tn(rec["normed_two"], grad_gate_up)
            grad_normed_two = scatter_product(grad_gate_up, up_w)
            grad_middle_norm, grad_gain_two = rec["norm_two_back"](grad_normed_two)
            grad_middle = grad_masked + grad_middle_norm
            ffn_blocks = jnp.concatenate([grad_upw, grad_down], axis=1).reshape(
                ctx_count, depth, 3 * ff_own
            )
            folded[layer] = [fold_halves(ffn_blocks)]
            early = (ffn_blocks,) if layer + 1 == LAYERS else (ffn_blocks, folded[layer + 1][1])
            branch_rows = gather_rows(after(grad_middle.astype(bf16), early))
            points[-1].append(branch_rows)
            grad_mixer = matmul(branch_rows, out_w)
            out_blocks = product_tn(branch_rows, rec["mixer"]).reshape(
                ctx_count, depth, HD + width
            )
            if layer == 0:
                folded[layer].append(fold_halves(out_blocks))
            gated_scale = rec["gated_scale"]
            scale_part = jnp.sum(grad_mixer[:, HD:] * rec["gated_low"].astype(f32), axis=-1)
            grad_scale = after(sum_slot(scale_part), out_blocks)
            grad_squares = grad_scale * -0.5 * gated_scale * gated_scale * gated_scale / (MH * P_SIZE)
            if layer + 1 < LAYERS:
                came[layer + 1].append(group_swap(after(folded[layer + 1][1], branch_rows)))
            grad_q, grad_kv = run_attend_back(
                plan, query_part, rec["queries"], rec["keyval"], rec["logsum"], grad_mixer,
                *tables,
            )
            grad_bc, grad_pair, grad_step, taps_grad, grad_conv, heads_grad = run_backward(
                plan, core_scalar, rec["mixed"], tap_rows[layer], shared_rows[layer], head_rows[layer],
                rec["ssm_y"], rec["states"], grad_mixer,
                jnp.concatenate([gated_scale, 2.0 * grad_squares], axis=1),
            )
            chan_grad = taps_grad[: CONV + 2]
            grad_conv = grad_conv[: CONV + 1]
            grad_heads = jnp.concatenate(
                [heads_grad[:2, :heads], jnp.sum(taps_grad[6].reshape(heads, lanes), axis=1)[None]]
            )
            grad_mix_own = jnp.concatenate([grad_q, grad_pair], axis=1)
            grad_in = jnp.concatenate([grad_bc, grad_kv, grad_mix_own, grad_step], axis=1)
            if layer == 0:
                grad_in = after(grad_in, folded[layer][0])
            at_heads = [
                jnp.where(kv_head == head, grad_kv[:, part * HD : (part + 1) * HD], 0)
                for part in range(2)
                for head in range(KVH)
            ]
            step_cols = lax.dynamic_update_slice(
                jnp.zeros((seq_len, 128), bf16), grad_step[:, :heads], (0, dt_start - dt_cols)
            )
            grad_share = jnp.concatenate([grad_bc] + at_heads + [step_cols], axis=1)
            if layer == 0:
                grad_share = after(grad_share, folded[0][1])
            scattered = scatter_product(grad_in, in_w, grad_share)
            if layer > 0:
                scattered = after(scattered, folded[layer][0])
            grad_normed_one = scattered[:, :D]
            share_sums.append(share_columns(scattered[:, D:].astype(bf16)))
            points[-1] += [grad_in, grad_normed_one]
            grad_stream_norm, grad_gain_one = rec["norm_one_back"](grad_normed_one)
            grad_stream = grad_middle + grad_stream_norm
            grad_mix = product_tn(rec["normed"], grad_mix_own)[:, : HD + 2 * width]
            mix_blocks = grad_mix.reshape(ctx_count, depth, HD + 2 * width)
            if layer == 0:
                folded[layer].append(fold_last(mix_blocks))
            else:
                folded[layer].append(fold_halves(jnp.concatenate([out_blocks, mix_blocks], axis=2)))
            out_grads[layer] = (
                jnp.stack([grad_gain_one, grad_gain_two]), chan_grad, grad_conv, grad_heads,
            )
        last = points[-1]
        mix_kept, mix_got = folded[0][2]
        mix_sum = (mix_kept + after(mix_got, last[3]).astype(f32)).astype(bf16)
        out_sum, mix_sum = after((folded[0][1], mix_sum), last[3])
        came[0] = [
            group_swap(after(folded[0][0], last[3])),
            group_swap(jnp.concatenate([out_sum, mix_sum], axis=2)),
        ]

        share_grads = []
        for layer in range(LAYERS):
            normed = records[layer]["normed"]
            grad_share = share_sums[LAYERS - 1 - layer]
            near = lax.dynamic_slice_in_dim(normed, (slot * members + me) * depth, depth, 1)
            far = lax.dynamic_slice_in_dim(normed, ((1 - slot) * members + me) * depth, depth, 1)
            share_far = product_tn(far, grad_share)
            if layer == 0:
                share_far = after(share_far, came[0][1])
            share_far = lax.ppermute(share_far, half_axis, SWAP)
            if layer > 0:
                share_far = after(share_far, last[3])
            share_sum = product_tn(near, grad_share).astype(f32) + share_far.astype(f32)
            share_sum = share_sum.astype(bf16)
            for axis in tp_axes[::-1]:
                got = lax.ppermute(share_sum, axis, SWAP)
                first = lax.axis_index(axis) == 0
                share_sum = jnp.where(
                    first,
                    jnp.concatenate([share_sum, got], 1),
                    jnp.concatenate([got, share_sum], 1),
                )
            share_grads.append(share_sum[:, :share_cols].astype(f32))
        share_g = jnp.stack(share_grads)
        both_out = bring_out(jnp.stack([stream, grad_stream]))
        activations, input_grad = both_out[:, :, 0], both_out[:, :, 1]

        def weight_grads(layer):
            got = came[layer] if layer == 0 else after(came[layer], last[3])
            ffn_came, both_came = got
            out_came, mix_came = both_came[:, :, : HD + width], both_came[:, :, HD + width :]
            mix = jnp.concatenate(
                [
                    join_heads(mix_came[:, :, HD : HD + width], 1),
                    join_heads(mix_came[:, :, HD + width :], 1),
                    join_query_heads(mix_came[:, :, :HD], 1),
                ],
                axis=1,
            )
            out = jnp.concatenate(
                [join_heads(out_came[:, :, HD:], 1), join_query_heads(out_came[:, :, :HD], 1)],
                axis=1,
            )
            up = jnp.concatenate(
                [
                    ffn_came[g, :, part * ff_own : (part + 1) * ff_own]
                    for part in range(2)
                    for g in range(members)
                ],
                axis=1,
            )
            down = jnp.concatenate([ffn_came[g, :, 2 * ff_own :] for g in range(members)], axis=1)
            return mix, out.T, up, down.T

        by_layer = [weight_grads(layer) for layer in range(LAYERS)]
        mix_g, out_g, up_g, down_g = (jnp.stack(grads).astype(f32) for grads in zip(*by_layer))
        gain_g, chan_g, conv_g, head_g = (jnp.stack(grads) for grads in zip(*out_grads))
        chan_rows = jnp.zeros((LAYERS, CONV + 2, HGROUPS, heads, replicas, lanes), f32)
        chan_rows = lax.dynamic_update_slice(
            chan_rows,
            chan_g.reshape(LAYERS, CONV + 2, 1, heads, 1, lanes),
            (0, 0, head_group, 0, head_part, 0),
        ).reshape(LAYERS, CONV + 2, ssm_cols)
        head_rows = lax.dynamic_update_slice(
            jnp.zeros((LAYERS, 3, HGROUPS, heads), f32), head_g[:, :, None], (0, 0, head_group, 0)
        ).reshape(LAYERS, 3, tp_heads)

        def packed(arrays):
            flat = jnp.concatenate([a.reshape(-1) for a in arrays])
            return jnp.pad(flat, (0, -flat.shape[0] % 1024)).reshape(-1, 128)

        def unpacked(flat, arrays):
            flat, marks = flat.reshape(-1), [0]
            for a in arrays:
                marks.append(marks[-1] + a.size)
            return [flat[marks[k] : marks[k + 1]].reshape(a.shape) for k, a in enumerate(arrays)]

        early = (conv_g, gain_g[0, 1], gain_g[1:])
        whole = sum_over(packed(early), tp_axes[::-1])
        local_sums = (chan_rows, head_rows, whole)
        chan_sum, head_sum, whole = unpacked(
            sum_over(packed(local_sums), group_axes[::-1] + (half_axis,)), local_sums
        )
        conv_sum, gain_two, gain_rest = unpacked(whole, early)
        ctx_index = slot * members + me
        last_gain = jnp.repeat(gain_g[0, 0].reshape(ctx_count, 1, depth), 4, axis=1)
        last_gain = lax.all_to_all(
            last_gain.reshape(4 * ctx_count, 1, depth), all_axes, 0, 0, tiled=True
        )
        last_gain = jnp.sum(last_gain, axis=0)
        gain_rest = lax.dynamic_slice_in_dim(gain_rest, ctx_index * depth, depth, 2)
        gain_two = lax.dynamic_slice_in_dim(gain_two, ctx_index * depth, depth, 0)
        gain_own = jnp.concatenate([jnp.concatenate([last_gain, gain_two[None]])[None], gain_rest])
        return (
            activations,
            input_grad,
            gain_own,
            mix_g,
            share_g,
            chan_sum,
            conv_sum,
            head_sum,
            out_g,
            up_g,
            down_g,
        )

    return local


def solution(mesh):
    ctx_bits = mesh.shape["ctx"].bit_length() - 1
    tp_bits = mesh.shape["tp"].bit_length() - 1
    ctx_axes = tuple(f"c{k}" for k in range(ctx_bits))
    tp_axes = tuple(f"t{k}" for k in range(tp_bits))
    fine = Mesh(mesh.devices.reshape((2,) * (ctx_bits + tp_bits)), ctx_axes + tp_axes)
    return jax.shard_map(
        build(ctx_axes, tp_axes),
        mesh=fine,
        in_specs=(
            P(None, None, ctx_axes, None),
            P(None, None, ctx_axes, None),
            P(),
            P(None, None, ctx_axes),
            P(None, ctx_axes, tp_axes),
            P(None, ctx_axes, None),
            P(None, None, tp_axes),
            P(),
            P(None, None, tp_axes),
            P(None, tp_axes, ctx_axes),
            P(None, ctx_axes, tp_axes),
            P(None, tp_axes, ctx_axes),
        ),
        out_specs=(
            P(None, None, ctx_axes, None),
            P(None, None, ctx_axes, None),
            P(None, None, ctx_axes),
            P(None, ctx_axes, tp_axes),
            P(None, ctx_axes, None),
            P(None, None, tp_axes),
            P(),
            P(None, None, tp_axes),
            P(None, tp_axes, ctx_axes),
            P(None, ctx_axes, tp_axes),
            P(None, tp_axes, ctx_axes),
        ),
        check_vma=False,
    )
```

```python
import functools

import jax
import jax.numpy as jnp
from jax import lax
from jax.experimental import pallas as pl
from jax.experimental.pallas import tpu as pltpu
from jax.sharding import Mesh
from jax.sharding import PartitionSpec as P

D = 2048
MH = 48
P_SIZE = 64
N = 256
CONV = 4
AH = 8
KVH = 2
HD = 128
FF = 4096
LAYERS = 2
HGROUPS = 4
PAD = 8

eps_norm = 1e-05
rope_base = 100000000000.0
highest = lax.Precision.HIGHEST
SWAP = [(0, 1), (1, 0)]
bf16 = jnp.bfloat16
f32 = jnp.float32


def matmul(left_op, right_op):
    return jnp.dot(left_op, right_op, preferred_element_type=f32)


def matmul_tn(left_op, right_op):
    return lax.dot_general(left_op, right_op, (((0,), (0,)), ((), ())), preferred_element_type=f32)


def matmul_nt(left_op, right_op):
    return lax.dot_general(left_op, right_op, (((1,), (1,)), ((), ())), preferred_element_type=f32)


def product_tn_block(left, right, out):
    out[...] = dot_tn(left[...], right[...]).astype(bf16)


def product_tn(left, right):
    rows, m = left.shape
    n = right.shape[1]
    block = min(m, 1024 if rows <= 768 else 256)
    return pl.pallas_call(
        product_tn_block,
        grid=(m // block,),
        in_specs=[
            pl.BlockSpec((rows, block), lambda i: (0, i)),
            pl.BlockSpec((rows, n), lambda i: (0, 0)),
        ],
        out_specs=pl.BlockSpec((block, n), lambda i: (i, 0)),
        out_shape=jax.ShapeDtypeStruct((m, n), bf16),
        compiler_params=pltpu.CompilerParams(vmem_limit_bytes=30 * 2**20),
        cost_estimate=pl.CostEstimate(
            flops=2 * rows * m * n, bytes_accessed=2 * (rows * m + rows * n + m * n), transcendentals=0
        ),
    )(left, right)


def silu_grad(inputs):
    sigmoid = jax.nn.sigmoid(inputs)
    return sigmoid * (1.0 + inputs * (1.0 - sigmoid))


def after(x, point):
    return lax.optimization_barrier((x, point))[0]


def following(x, *points):
    zero = sum(jnp.minimum(jnp.abs(p.reshape(-1)[0].astype(f32)), 0.0) for p in points)
    return x + zero.astype(x.dtype)


def pick(x, dim, index):
    return lax.dynamic_index_in_dim(x, index, dim, keepdims=False)


def norm_piece(stream, gain_row):
    factor = lax.rsqrt(jnp.mean(stream * stream, axis=-1, keepdims=True) + eps_norm)
    return stream * factor * gain_row


def dot_nn(a, b):
    return lax.dot_general(a, b, (((1,), (0,)), ((), ())), preferred_element_type=f32)


def dot_nt(a, b):
    return lax.dot_general(a, b, (((1,), (1,)), ((), ())), preferred_element_type=f32)


def dot_tn(a, b):
    return lax.dot_general(a, b, (((0,), (0,)), ((), ())), preferred_element_type=f32)


def dot_exact(a, b):
    return lax.dot_general(
        a, b, (((1,), (0,)), ((), ())), precision=highest, preferred_element_type=f32
    )


def sigmoid(v):
    return 1.0 / (1.0 + jnp.exp(-v))


def block_place(block, members):
    quarter, at = block // members, block % members
    if quarter < 2:
        return at, 0, quarter
    return members - 1 - at, 1, 3 - quarter


class Plan:
    def __init__(self, seq_len, block_len, heads, lanes):
        self.seq_len = seq_len
        self.block_len = block_len
        self.heads = heads
        self.lanes = lanes
        self.width = heads * lanes
        self.members = seq_len // (4 * block_len)
        self.chunk = 4 * block_len
        self.chunks = seq_len // self.chunk
        self.query_parts = self.members // 2
        self.query_rows = seq_len // self.query_parts
        self.bc = 2 * N
        self.key_at = self.bc
        self.value_at = self.bc + HD
        self.q_at = self.bc + 2 * HD
        self.gate_at = self.bc + 3 * HD
        self.pair_cols = 2 * self.width
        self.pair_tiles = self.pair_cols + -self.pair_cols % 128
        self.step_at = self.gate_at + self.pair_tiles
        self.cols = self.step_at + 128

    def rows(self, core, block):
        member, half, place = block_place(block, self.members)
        other = core if place == 0 else 1 - core
        start = other * (self.seq_len // 2) + (2 * member + half) * self.block_len
        return pl.ds(pl.multiple_of(start, 16), self.block_len)

    def blocks(self):
        return range(self.seq_len // self.block_len)


def head_masks(plan):
    lane = lax.broadcasted_iota(jnp.int32, (1, plan.width), 1)
    return [
        ((lane >= h * plan.lanes) & (lane < (h + 1) * plan.lanes)).astype(f32)
        for h in range(plan.heads)
    ]


def over_heads(plan, tile, masks):
    return sum(tile[:, h : h + 1] * masks[h] for h in range(plan.heads))


def per_head(plan, values, masks):
    lane = lax.broadcasted_iota(jnp.int32, (1, 128), 1)
    total = None
    for h in range(plan.heads):
        column = jnp.sum(values * masks[h], axis=1, keepdims=True)
        part = column * (lane == h).astype(f32)
        total = part if total is None else total + part
    return total


def conv_values(source, taps_ref, rows, start, low, high):
    total = taps_ref[CONV : CONV + 1, low:high]
    for k in range(CONV):
        at = PAD + start - (CONV - 1) + k
        total = total + taps_ref[k : k + 1, low:high] * source[pl.ds(at, rows), low:high]
    return total


def prepare(plan, core, mixed, nat_bc, nat_x, nat_step):
    width = plan.width
    nat_bc[0:PAD, :] = jnp.zeros((PAD, plan.bc), f32)
    nat_x[0:PAD, :] = jnp.zeros((PAD, width), f32)
    for block in plan.blocks():
        at = PAD + block * plan.block_len
        rows = plan.rows(core, block)
        nat_bc[pl.ds(at, plan.block_len), :] = mixed[rows, 0 : plan.bc]
        pair = mixed[rows, plan.gate_at : plan.gate_at + plan.pair_tiles]
        nat_x[pl.ds(at, plan.block_len), :] = pltpu.roll(pair, plan.pair_tiles - width, 1)[:, :width]
        nat_step[pl.ds(at - PAD, plan.block_len), :] = mixed[rows, plan.step_at : plan.step_at + 128]


def chunk_decays(plan, nat_step, head_rows, c, tri):
    q = plan.chunk
    real = lax.broadcasted_iota(jnp.int32, (1, 128), 1) < plan.heads
    raw = jnp.where(real, nat_step[pl.ds(c * q, q), :] + head_rows[1:2, :], 0.0)
    step = jnp.where(real, jnp.maximum(raw, 0.0) + jnp.log(1.0 + jnp.exp(-jnp.abs(raw))), 0.0)
    cumulative = dot_exact(tri, step * head_rows[0:1, :])
    return raw, step, cumulative


def triangle(plan):
    q = plan.chunk
    row = lax.broadcasted_iota(jnp.int32, (q, q), 0)
    col = lax.broadcasted_iota(jnp.int32, (q, q), 1)
    return row, col


def ssm_forward(plan, core_ref, mixed, taps, shared_taps, head_rows, y_out, low_out, states_out, squares_out,
                nat_bc, nat_x, nat_step):
    q = plan.chunk
    masks = head_masks(plan)
    core = core_ref[0]
    prepare(plan, core, mixed, nat_bc, nat_x, nat_step)
    row, col = triangle(plan)
    lower = row >= col
    tri = lower.astype(f32)
    state = jnp.zeros((N, plan.width), f32)
    for c in range(plan.chunks):
        start = c * q
        x = conv_values(nat_x, taps, q, start, 0, plan.width)
        x = x * sigmoid(x)
        bc = conv_values(nat_bc, shared_taps, q, start, 0, plan.bc)
        bc = (bc * sigmoid(bc)).astype(bf16)
        b, cc = bc[:, :N], bc[:, N:]
        _, step, cum = chunk_decays(plan, nat_step, head_rows, c, tri)
        cum_rows = cum.T
        cum_full = over_heads(plan, cum, masks)
        total_full = cum_full[q - 1 : q, :]
        u = x * over_heads(plan, step, masks)
        inner = dot_nt(cc, b)
        states_out[c] = state
        y = dot_nn(cc, state.astype(bf16)) * jnp.exp(cum_full) + taps[6:7, :] * x
        for h in range(plan.heads):
            seg = jnp.where(lower, cum[:, h : h + 1] - cum_rows[h : h + 1, :], -1e30)
            mixing = (jnp.exp(seg) * inner).astype(bf16)
            y = y + dot_nn(mixing, (u * masks[h]).astype(bf16))
        weighted = (u * jnp.exp(total_full - cum_full)).astype(bf16)
        state = jnp.exp(total_full) * state + dot_tn(b, weighted)
        for k in range(4):
            block = 4 * c + k
            y_out[plan.rows(core, block), :] = y[k * plan.block_len : (k + 1) * plan.block_len, :]
    z = mixed[:, plan.gate_at : plan.gate_at + plan.width]
    gated = y_out[...] * (z * sigmoid(z))
    low_out[...] = (gated * taps[5:6, :]).astype(bf16)
    squares_out[...] = lax.dot_general(
        jnp.ones((8, plan.width), f32), gated * gated, (((1,), (1,)), ((), ())),
        precision=highest, preferred_element_type=f32,
    )


def ssm_backward(plan, core_ref, mixed, taps, shared_taps, head_rows, y_in, states, grad_mixer, scales,
                 bc_out, pair_out, step_out, taps_out, shared_out, heads_out,
                 nat_bc, nat_x, nat_step, nat_dy, grad_x, grad_bc, grad_y_ref):
    q = plan.chunk
    width = plan.width
    masks = head_masks(plan)
    core = core_ref[0]
    prepare(plan, core, mixed, nat_bc, nat_x, nat_step)
    row, col = triangle(plan)
    lower, upper = row >= col, row <= col
    strict_lower, strict_upper = row > col, row < col
    tri, tri_back = lower.astype(f32), upper.astype(f32)

    z = mixed[:, plan.gate_at : plan.gate_at + width]
    y = y_in[...]
    sig = sigmoid(z)
    silu = z * sig
    gated = y * silu
    scaled = grad_mixer[:, HD : HD + width] * scales[:, 0:1]
    grad_gated = scaled * taps[5:6, :] + scales[:, 1:2] * gated
    gain_grad = jnp.sum(scaled * gated, axis=0, keepdims=True)
    grad_z = grad_gated * y * (sig * (1.0 + z * (1.0 - sig)))
    spare = plan.pair_tiles - width
    pair_out[...] = jnp.concatenate(
        [grad_z, jnp.zeros((plan.seq_len, spare), f32)], axis=1
    ).astype(bf16)
    grad_y_ref[...] = grad_gated * silu
    for block in plan.blocks():
        at = block * plan.block_len
        nat_dy[pl.ds(at, plan.block_len), :] = grad_y_ref[plan.rows(core, block), :]

    grad_x[plan.seq_len : plan.seq_len + PAD, :] = jnp.zeros((PAD, width), f32)
    grad_bc[plan.seq_len : plan.seq_len + PAD, :] = jnp.zeros((PAD, plan.bc), f32)
    grad_state = jnp.zeros((N, width), f32)
    skip_grad = jnp.zeros((1, width), f32)
    rate_grad = jnp.zeros((1, 128), f32)
    bias_grad = jnp.zeros((1, 128), f32)
    for c in reversed(range(plan.chunks)):
        start = c * q
        x_lin = conv_values(nat_x, taps, q, start, 0, width)
        x_sig = sigmoid(x_lin)
        x = x_lin * x_sig
        bc_lin = conv_values(nat_bc, shared_taps, q, start, 0, plan.bc)
        bc_sig = sigmoid(bc_lin)
        bc = (bc_lin * bc_sig).astype(bf16)
        b, cc = bc[:, :N], bc[:, N:]
        raw, step, cum = chunk_decays(plan, nat_step, head_rows, c, tri)
        cum_rows = cum.T
        cum_full = over_heads(plan, cum, masks)
        total_full = cum_full[q - 1 : q, :]
        step_full = over_heads(plan, step, masks)
        u = x * step_full
        u_low = u.astype(bf16)
        dy = nat_dy[pl.ds(start, q), :]
        dy_low = dy.astype(bf16)
        state = states[c]
        state_low = state.astype(bf16)
        grad_state_low = grad_state.astype(bf16)
        entry = jnp.exp(cum_full)
        exit_w = jnp.exp(total_full - cum_full)
        total_decay = jnp.exp(total_full)
        dy_entry = (dy * entry).astype(bf16)
        grad_c = dot_nt(dy_entry, state_low)
        carried = dot_nn(cc, state_low) * entry
        du_state = dot_nn(b, grad_state_low) * exit_w
        grad_b = dot_nt((u * exit_w).astype(bf16), grad_state_low)
        inner = dot_nt(cc, b)
        inner_t = dot_nt(b, cc)
        du = du_state
        grad_inner = jnp.zeros((q, q), f32)
        grad_inner_t = jnp.zeros((q, q), f32)
        lane = lax.broadcasted_iota(jnp.int32, (1, 128), 1)
        dcum = per_head(plan, dy * carried - u * du_state, masks)
        for h in range(plan.heads):
            here = (lane == h).astype(f32)
            u_head = (u * masks[h]).astype(bf16)
            dy_head = (dy * masks[h]).astype(bf16)
            seg = cum[:, h : h + 1] - cum_rows[h : h + 1, :]
            decay = jnp.exp(jnp.where(lower, seg, -1e30))
            decay_t = jnp.exp(jnp.where(upper, -seg, -1e30))
            grad_mix = dot_nt(dy_head, u_low) * decay
            grad_mix_t = dot_nt(u_head, dy_low) * decay_t
            grad_inner = grad_inner + grad_mix
            grad_inner_t = grad_inner_t + grad_mix_t
            du = du + dot_nn((decay_t * inner_t).astype(bf16), dy_head)
            out_sum = jnp.sum(jnp.where(strict_lower, grad_mix * inner, 0.0), axis=1, keepdims=True)
            in_sum = jnp.sum(
                jnp.where(strict_upper, grad_mix_t * inner_t, 0.0), axis=1, keepdims=True
            )
            dcum = dcum + (out_sum - in_sum) * here
        grad_c = grad_c + dot_nn(grad_inner.astype(bf16), b)
        grad_b = grad_b + dot_nn(grad_inner_t.astype(bf16), cc)
        whole = jnp.sum(u * du_state, axis=0, keepdims=True) + jnp.sum(
            grad_state * state, axis=0, keepdims=True
        ) * total_decay
        dlog = dot_exact(tri_back, dcum) + per_head(plan, whole, masks)
        rate_grad = rate_grad + jnp.sum(dlog * step, axis=0, keepdims=True)
        grad_step = dlog * head_rows[0:1, :] + per_head(plan, du * x, masks)
        grad_raw = grad_step * sigmoid(raw)
        bias_grad = bias_grad + jnp.sum(grad_raw, axis=0, keepdims=True)
        grad_xc = du * step_full + taps[6:7, :] * dy
        skip_grad = skip_grad + jnp.sum(dy * x, axis=0, keepdims=True)
        grad_state = total_decay * grad_state + dot_tn(cc, dy_entry)
        grad_x[pl.ds(start, q), :] = grad_xc * (x_sig * (1.0 + x_lin * (1.0 - x_sig)))
        grad_bc[pl.ds(start, q), :] = jnp.concatenate([grad_b, grad_c], axis=1) * (
            bc_sig * (1.0 + bc_lin * (1.0 - bc_sig))
        )
        for k in range(4):
            step_out[plan.rows(core, 4 * c + k), :] = grad_raw[
                k * plan.block_len : (k + 1) * plan.block_len, :
            ].astype(bf16)

    size = plan.block_len
    tap_grads = [jnp.zeros((1, width), f32) for _ in range(CONV + 1)]
    shared_grads = [jnp.zeros((1, plan.bc), f32) for _ in range(CONV + 1)]
    lane = lax.broadcasted_iota(jnp.int32, (1, plan.pair_tiles), 1)
    for c in range(plan.chunks):
        start = c * q
        dx = grad_x[pl.ds(start, q), :]
        dbc = grad_bc[pl.ds(start, q), :]
        tap_grads[CONV] += jnp.sum(dx, axis=0, keepdims=True)
        shared_grads[CONV] += jnp.sum(dbc, axis=0, keepdims=True)
        pre_dx = None
        pre_dbc = None
        for k in range(CONV):
            at = PAD + start - (CONV - 1) + k
            tap_grads[k] += jnp.sum(dx * nat_x[pl.ds(at, q), :], axis=0, keepdims=True)
            shared_grads[k] += jnp.sum(dbc * nat_bc[pl.ds(at, q), :], axis=0, keepdims=True)
            ahead = start + (CONV - 1) - k
            part = taps[k : k + 1, :] * grad_x[pl.ds(ahead, q), :]
            pre_dx = part if k == 0 else pre_dx + part
            part = shared_taps[k : k + 1, :] * grad_bc[pl.ds(ahead, q), :]
            pre_dbc = part if k == 0 else pre_dbc + part
        tile = jnp.concatenate([pre_dx, jnp.zeros((q, spare), f32)], axis=1)
        tile = pltpu.roll(tile, width, 1).astype(bf16)
        for k in range(4):
            rows = plan.rows(core, 4 * c + k)
            pair_out[rows, :] = jnp.where(
                lane < width, pair_out[rows, :], tile[k * size : (k + 1) * size, :]
            )
            bc_out[rows, :] = pre_dbc[k * size : (k + 1) * size, :].astype(bf16)
    for k in range(CONV + 1):
        taps_out[k : k + 1, :] = tap_grads[k]
        shared_out[k : k + 1, :] = shared_grads[k]
    taps_out[5:6, :] = gain_grad
    taps_out[6:7, :] = skip_grad
    heads_out[0:1, :] = rate_grad * head_rows[0:1, :]
    heads_out[1:2, :] = bias_grad


def whole_specs(arrays):
    def spec(array):
        zeros = (0,) * len(array.shape)
        return pl.BlockSpec(array.shape, lambda i: zeros, pipeline_mode=pl.Buffered(1))

    return [spec(array) for array in arrays]


def call_whole(plan, kernel, outs, scratch, flops, inputs, scalars=()):
    return pl.pallas_call(
        kernel,
        grid=(1,),
        in_specs=[pl.BlockSpec(memory_space=pltpu.SMEM) for _ in scalars] + whole_specs(inputs),
        out_specs=tuple(whole_specs(outs)),
        out_shape=tuple(outs),
        scratch_shapes=scratch,
        compiler_params=ssm_params(plan),
        cost_estimate=pl.CostEstimate(
            flops=flops, bytes_accessed=plan.seq_len * 8192, transcendentals=0
        ),
    )(*scalars, *inputs)


def ssm_params(plan):
    limit = 58 * 2**20
    return pltpu.CompilerParams(vmem_limit_bytes=limit)


def run_forward(plan, core, *inputs):
    t, w = plan.seq_len, plan.width
    outs = [
        jax.ShapeDtypeStruct((t, w), f32),
        jax.ShapeDtypeStruct((t, w), bf16),
        jax.ShapeDtypeStruct((plan.chunks, N, w), f32),
        jax.ShapeDtypeStruct((8, t), f32),
    ]
    scratch = [
        pltpu.VMEM((PAD + t, plan.bc), f32),
        pltpu.VMEM((PAD + t, w), f32),
        pltpu.VMEM((t, 128), f32),
    ]
    return call_whole(
        plan, functools.partial(ssm_forward, plan), outs, scratch, 40000 * t * w, inputs, (core,)
    )


def run_backward(plan, core, *inputs):
    t, w = plan.seq_len, plan.width
    outs = [
        jax.ShapeDtypeStruct((t, plan.bc), bf16),
        jax.ShapeDtypeStruct((t, plan.pair_tiles), bf16),
        jax.ShapeDtypeStruct((t, 128), bf16),
        jax.ShapeDtypeStruct((8, w), f32),
        jax.ShapeDtypeStruct((8, plan.bc), f32),
        jax.ShapeDtypeStruct((8, 128), f32),
    ]
    scratch = [
        pltpu.VMEM((PAD + t, plan.bc), f32),
        pltpu.VMEM((PAD + t, w), f32),
        pltpu.VMEM((t, 128), f32),
        pltpu.VMEM((t, w), f32),
        pltpu.VMEM((t + PAD, w), f32),
        pltpu.VMEM((t + PAD, plan.bc), f32),
        pltpu.VMEM((t, w), f32),
    ]
    return call_whole(
        plan, functools.partial(ssm_backward, plan), outs, scratch, 90000 * t * w, inputs, (core,)
    )


def attend_scores(plan, queries, keys, query_pos, key_pos):
    scores = dot_nt(queries, keys) * HD ** (-0.5)
    return jnp.where(key_pos <= query_pos, scores, -1e30)


def turned(x, cosine, sine):
    return x * cosine + pltpu.roll(x, HD // 2, 1) * sine


def attend_forward(plan, part, mixed, cosine, sine, query_pos, key_pos,
                   att_out, log_out, q_out, kv_out):
    rows = pl.ds(pl.multiple_of(part[0] * plan.query_rows, 8), plan.query_rows)
    keys = turned(mixed[:, plan.key_at : plan.key_at + HD], cosine[...], sine[...]).astype(bf16)
    values = mixed[:, plan.value_at : plan.value_at + HD].astype(bf16)
    kv_out[:, :HD] = keys
    kv_out[:, HD:] = values
    queries = mixed[rows, plan.q_at : plan.q_at + HD]
    queries = turned(queries, cosine[rows, :], sine[rows, :]).astype(bf16)
    q_out[...] = queries
    scores = attend_scores(plan, queries, keys, query_pos[rows, :], key_pos[...])
    peak = jnp.max(scores, axis=1, keepdims=True)
    weights = jnp.exp(scores - peak)
    total = jnp.sum(weights, axis=1, keepdims=True)
    probs = (weights / total).astype(bf16)
    att_out[...] = jnp.zeros((plan.seq_len, HD), bf16)
    att_out[rows, :] = dot_nn(probs, values).astype(bf16)
    log_out[...] = peak + jnp.log(total)


def attend_backward(plan, part, queries, kv, logs, grad_mixer, cosine, sine, query_pos, key_pos,
                    q_out, kv_out):
    rows = pl.ds(pl.multiple_of(part[0] * plan.query_rows, 8), plan.query_rows)
    keys, values = kv[:, :HD], kv[:, HD:]
    scale = HD ** (-0.5)
    q, grad = queries[...], grad_mixer[rows, :HD].astype(bf16)
    probs = jnp.exp(attend_scores(plan, q, keys, query_pos[rows, :], key_pos[...]) - logs[...])
    grad_probs = dot_nt(grad, values)
    inner = jnp.sum(probs * grad_probs, axis=1, keepdims=True)
    grad_scores = (probs * (grad_probs - inner)).astype(bf16)
    grad_q = dot_nn(grad_scores, keys) * scale
    q_out[...] = jnp.zeros((plan.seq_len, HD), bf16)
    q_out[rows, :] = turned(grad_q, cosine[rows, :], -sine[rows, :]).astype(bf16)
    grad_k = dot_tn(grad_scores, q) * scale
    kv_out[:, :HD] = turned(grad_k, cosine[...], -sine[...]).astype(bf16)
    kv_out[:, HD:] = dot_tn(probs.astype(bf16), grad).astype(bf16)


def run_attend(plan, part, *inputs):
    t, rows = plan.seq_len, plan.query_rows
    outs = [
        jax.ShapeDtypeStruct((t, HD), bf16),
        jax.ShapeDtypeStruct((rows, 1), f32),
        jax.ShapeDtypeStruct((rows, HD), bf16),
        jax.ShapeDtypeStruct((t, 2 * HD), bf16),
    ]
    kernel = functools.partial(attend_forward, plan)
    return call_whole(plan, kernel, outs, [], 4 * rows * t * HD, inputs, (part,))


def run_attend_back(plan, part, *inputs):
    t = plan.seq_len
    outs = [jax.ShapeDtypeStruct((t, HD), bf16), jax.ShapeDtypeStruct((t, 2 * HD), bf16)]
    kernel = functools.partial(attend_backward, plan)
    return call_whole(plan, kernel, outs, [], 10 * plan.query_rows * t * HD, inputs, (part,))


def build(ctx_axes, tp_axes):
    half_axis = ctx_axes[0]
    group_axes = ctx_axes[1:]
    t_half, t_core = tp_axes
    ring_axes = group_axes + (t_half,)
    slot_axes = group_axes + tp_axes
    all_axes = ctx_axes + tp_axes
    span = len(ring_axes)

    def column_parts(width):
        unit = width // 128
        marks = [0] + [128 * (unit * (k + 1) // 3) for k in range(3)]
        return list(zip(marks[:-1], marks[1:]))

    def rotated(part):
        turn = part % span
        return ring_axes[turn:] + ring_axes[:turn]

    def gather_rows(x):
        rows, width = x.shape
        parts = []
        for part, (low, high) in enumerate(column_parts(width)):
            held = x[:, low:high].reshape((1,) * span + (rows, high - low))
            for axis in rotated(part):
                dim = ring_axes.index(axis)
                got = lax.ppermute(held, axis, SWAP)
                first = lax.axis_index(axis) == 0
                held = jnp.where(
                    first, jnp.concatenate([held, got], dim), jnp.concatenate([got, held], dim)
                )
            parts.append(held)
        held = lax.optimization_barrier(jnp.concatenate(parts, -1).reshape(-1, width))
        return jnp.concatenate([held, lax.ppermute(held, t_core, SWAP)])

    def scatter_product(left, right, extra=None):
        total = left.shape[0]
        width = right.shape[0]
        peers = 2 ** (span + 1)
        rows = total // peers
        own = total // 2
        sent = matmul_nt(left[own:], right).astype(bf16)
        kept = matmul_nt(left[:own], right)
        if extra is not None:
            width += extra.shape[1]
            sent = jnp.concatenate([sent, extra[own:]], axis=1)
            kept = jnp.concatenate([kept, extra[:own].astype(f32)], axis=1)
        held = kept + lax.ppermute(sent, t_core, SWAP).astype(f32)
        parts = []
        for part, (low, high) in enumerate(column_parts(width)):
            piece = held[:, low:high].reshape((2,) * span + (rows, high - low))
            names = list(ring_axes)
            for axis in rotated(part):
                dim = names.index(axis)
                names.pop(dim)
                index = lax.axis_index(axis)
                got = lax.ppermute(pick(piece, dim, 1 - index).astype(bf16), axis, SWAP)
                piece = pick(piece, dim, index) + got.astype(f32)
            parts.append(piece)
        return jnp.concatenate(parts, -1)

    def sum_slot(x):
        turn = lax.axis_index(t_core) == 1
        x = x.reshape(2, -1, 128)
        x = jnp.where(turn, x[::-1], x)
        came = lax.all_to_all(
            jnp.broadcast_to(x[None], (2 ** (span + 1),) + x.shape), slot_axes, 0, 0, tiled=True
        )
        x = jnp.sum(came, axis=0)
        return jnp.where(turn, x[::-1], x).reshape(-1, 1)

    def sum_over(x, axes):
        for axis in axes:
            x = x + lax.ppermute(x, axis, SWAP)
        return x

    def group_index():
        return lax.axis_index(group_axes)

    def group_swap(blocks):
        return lax.all_to_all(blocks, group_axes, 0, 0, tiled=True)

    def both_halves(came):
        return lax.all_gather(came, half_axis, axis=0, tiled=True)

    def spread_first(blocks):
        return lax.all_to_all(jnp.concatenate([blocks, blocks]), ctx_axes, 0, 0, tiled=True)

    def fold_halves(blocks):
        return lax.psum_scatter(blocks.astype(bf16), half_axis, scatter_dimension=0, tiled=True)

    def fold_last(blocks):
        half = lax.axis_index(half_axis)
        paired = blocks.reshape((2, blocks.shape[0] // 2) + blocks.shape[1:])
        got = lax.ppermute(pick(paired, 0, 1 - half).astype(bf16), half_axis, SWAP)
        return pick(paired, 0, half).astype(f32), got

    def gather_lanes(x):
        for axis in ctx_axes[::-1]:
            got = lax.ppermute(x, axis, SWAP)
            first = lax.axis_index(axis) == 0
            x = jnp.where(first, jnp.concatenate([x, got], -1), jnp.concatenate([got, x], -1))
        return x

    def local(
        hidden,
        cotangent,
        lengths,
        norm_gains,
        mix_weight,
        share_weight,
        chan_params,
        shared_conv,
        head_params,
        out_weight,
        up_weight,
        down_weight,
    ):
        members = 2 ** len(group_axes)
        ctx_count = 2 * members
        replicas = members // HGROUPS
        slot = lax.axis_index(half_axis)
        me = group_index()
        head_group = me // replicas
        head_part = me % replicas
        tp_half = lax.axis_index(t_half)
        tp_core = lax.axis_index(t_core)
        tp_index = tp_half * 2 + tp_core
        block_len = hidden.shape[2]
        depth = mix_weight.shape[1]
        seq_len = 2 * ctx_count * block_len
        own_len = 4 * block_len
        tp_heads = chan_params.shape[2] // P_SIZE
        heads = tp_heads // HGROUPS
        lanes = P_SIZE // replicas
        width = heads * lanes
        ssm_cols = tp_heads * P_SIZE
        qheads = AH // 4
        q_cols = qheads * HD
        ff_tp = FF // 4
        ff_own = ff_tp // members
        plan = Plan(seq_len, block_len, heads, lanes)
        own_head = me // plan.query_parts
        core_scalar = tp_core.astype(jnp.int32).reshape(1)
        query_part = (me % plan.query_parts).astype(jnp.int32).reshape(1)
        share_cols = share_weight.shape[2]
        kv_cols = 2 * N
        dt_cols = 2 * N + 2 * KVH * HD
        kv_head = tp_index * qheads // (AH // KVH)
        score_scale = HD ** (-0.5)

        def block_of(member, half, cube):
            near = cube * members + member
            return jnp.where(half == 0, near, 2 * ctx_count - 1 - near)

        within = jnp.arange(block_len)
        own_pos = block_of(me, tp_half, tp_core) * block_len + within
        own_valid = (own_pos < lengths[slot]).astype(f32)[:, None]
        ring = jnp.arange(2 * members)

        def core_positions(core):
            first = block_of(ring // 2, ring % 2, core) * block_len
            return (first[:, None] + within[None, :]).reshape(-1)

        key_pos = jnp.concatenate([core_positions(tp_core), core_positions(1 - tp_core)])
        half_dim = HD // 2
        inverse = jnp.exp(-jnp.log(rope_base) * (2.0 * jnp.arange(half_dim, dtype=f32) / HD))
        angles = key_pos.astype(f32)[:, None] * inverse
        cosine = jnp.concatenate([jnp.cos(angles)] * 2, axis=1)
        sine = jnp.concatenate([-jnp.sin(angles), jnp.sin(angles)], axis=1)

        tables = (cosine, sine, key_pos[:, None], key_pos[None, :])

        def cut_query_heads(x, axis):
            shape = x.shape
            split = x.reshape(shape[:axis] + (qheads, HD) + shape[axis + 1 :])
            return jnp.repeat(jnp.moveaxis(split, axis, 0), plan.query_parts, axis=0)

        def join_query_heads(x, axis):
            summed = jnp.sum(
                x.astype(f32).reshape((qheads, plan.query_parts) + x.shape[1:]), axis=1
            ).astype(bf16)
            joined = jnp.moveaxis(summed, 0, axis)
            shape = joined.shape
            return joined.reshape(shape[:axis] + (q_cols,) + shape[axis + 2 :])

        def bring_in(x):
            got = lax.ppermute(
                pick(pick(x, 0, 1 - slot), 0, tp_half), (half_axis, t_core), [(0, 2), (3, 1)]
            )
            return jnp.where(tp_core == slot, pick(pick(x, 0, slot), 0, tp_half), got)

        def share_columns(own):
            quarter = own.shape[1] // 4
            chunks = jnp.moveaxis(own.reshape(block_len, 4, quarter), 1, 0)
            chunks = jnp.broadcast_to(chunks[None], (members,) + chunks.shape)
            rows = lax.all_to_all(
                chunks.reshape(4 * members, block_len, quarter), slot_axes, 0, 0, tiled=True
            )
            rows = jnp.moveaxis(rows.reshape(2 * members, 2, block_len, quarter), 1, 0)
            return jnp.where(tp_core == 0, rows, rows[::-1]).reshape(seq_len, quarter)

        def bring_out(x):
            x = x.astype(bf16)
            got = lax.ppermute(x, (half_axis, t_core), [(1, 3), (2, 0)])
            pair = jnp.where(slot == 0, jnp.stack([x, got]), jnp.stack([got, x]))
            other = lax.ppermute(pair, t_core, SWAP)
            pair = jnp.where(tp_core == slot, pair, other)
            other = lax.ppermute(pair, t_half, SWAP)
            both = jnp.where(tp_half == 0, jnp.stack([pair, other], 1), jnp.stack([other, pair], 1))
            return both.astype(f32)

        def cut_heads(x, axis):
            shape = x.shape
            split = x.reshape(
                shape[:axis] + (HGROUPS, heads, replicas, lanes) + shape[axis + 1 :]
            )
            split = jnp.moveaxis(split, (axis, axis + 2), (0, 1))
            return split.reshape((members,) + shape[:axis] + (width,) + shape[axis + 1 :])

        def join_heads(x, axis):
            if replicas == 1:
                return jnp.concatenate([x[g] for g in range(members)], axis=axis)
            shape = x.shape[1:]
            split = x.reshape(
                (HGROUPS, replicas) + shape[:axis] + (heads, lanes) + shape[axis + 1 :]
            )
            split = jnp.moveaxis(split, (0, 1), (axis, axis + 2))
            return split.reshape(shape[:axis] + (ssm_cols,) + shape[axis + 1 :])

        gains = gather_lanes(norm_gains).astype(f32)
        hidden_rows = bring_in(after(hidden, gains))
        stream = hidden_rows.astype(f32)
        own_chan = pick(cut_heads(chan_params, 2), 0, me)
        own_heads = pick(head_params.reshape(LAYERS, 3, HGROUPS, heads), 2, head_group)
        skip_full = jnp.repeat(own_heads[:, 2], lanes, axis=1)[:, None]
        tap_rows = jnp.concatenate([own_chan, skip_full, jnp.zeros_like(skip_full)], axis=1)
        shared_rows = jnp.pad(shared_conv, ((0, 0), (0, 3), (0, 0)))
        head_rows = jnp.pad(
            jnp.stack([-jnp.exp(own_heads[:, 0]), own_heads[:, 1]], axis=1),
            ((0, 0), (0, 6), (0, 128 - heads)),
        )
        share_rows = lax.dynamic_slice_in_dim(share_weight, tp_core * (depth // 2), depth // 2, 1)
        dt_start = dt_cols + tp_index * tp_heads + head_group * heads

        def weight_blocks(layer):
            mix = mix_weight[layer]
            mix_blocks = jnp.concatenate(
                [
                    cut_query_heads(mix[:, 2 * ssm_cols :], 1),
                    cut_heads(mix[:, :ssm_cols], 1),
                    cut_heads(mix[:, ssm_cols : 2 * ssm_cols], 1),
                ],
                2,
            )
            out = out_weight[layer].T
            out_blocks = jnp.concatenate(
                [cut_query_heads(out[:, ssm_cols:], 1), cut_heads(out[:, :ssm_cols], 1)], 2
            )
            up = up_weight[layer]
            down = down_weight[layer].T
            ffn_blocks = jnp.stack(
                [
                    jnp.concatenate(
                        [
                            up[:, g * ff_own : (g + 1) * ff_own],
                            up[:, ff_tp + g * ff_own : ff_tp + (g + 1) * ff_own],
                            down[:, g * ff_own : (g + 1) * ff_own],
                        ],
                        axis=1,
                    )
                    for g in range(members)
                ]
            )
            return mix_blocks, out_blocks, ffn_blocks

        def share_whole(share):
            share = jnp.concatenate(
                [
                    share[:, :kv_cols],
                    lax.dynamic_slice_in_dim(share, kv_cols + kv_head * HD, HD, 1),
                    lax.dynamic_slice_in_dim(share, kv_cols + (KVH + kv_head) * HD, HD, 1),
                    share[:, dt_cols:],
                ],
                axis=1,
            )
            return lax.all_gather(share, ctx_axes + (t_core,), axis=0, tiled=True)

        def input_weights(mix_own, share):
            dt_w = lax.dynamic_slice_in_dim(share, kv_cols + 2 * HD + dt_start - dt_cols, heads, 1)
            return jnp.concatenate(
                [
                    share[:, : plan.q_at],
                    jnp.pad(
                        mix_own.reshape(D, HD + 2 * width),
                        ((0, 0), (0, plan.pair_tiles - plan.pair_cols)),
                    ),
                    jnp.pad(dt_w, ((0, 0), (0, 128 - heads))),
                ],
                axis=1,
            )

        def ffn_weights(ffn_own):
            ffn_own = ffn_own.reshape(D, 3 * ff_own)
            return ffn_own[:, : 2 * ff_own], ffn_own[:, 2 * ff_own :]

        blocks = [weight_blocks(layer) for layer in range(LAYERS)]
        mix_own = [None] * LAYERS
        out_own = [None] * LAYERS
        ffn_own = [None] * LAYERS
        shares = [None] * LAYERS
        mix_own[0] = spread_first(following(blocks[0][0], hidden_rows, gains))
        out_cols = HD + width
        hidden_all = gather_rows(hidden_rows)
        first_out = group_swap(following(blocks[0][1], mix_own[0]))
        first_ffn = group_swap(following(blocks[0][2], first_out))
        swapped = [[first_out, first_ffn]]
        for layer in range(1, LAYERS):
            both = jnp.concatenate(blocks[layer][:2], axis=2)
            both = group_swap(following(both, swapped[-1][1]))
            ffn_came = group_swap(following(blocks[layer][2], both))
            swapped.append([both[:, :, -out_cols:], ffn_came])
            mix_own[layer] = both_halves(both[:, :, :-out_cols])
        for layer in range(LAYERS):
            shares[layer] = share_whole(share_rows[layer])
            out_own[layer] = both_halves(swapped[layer][0])
            ffn_own[layer] = both_halves(swapped[layer][1])

        records = []
        for layer in range(LAYERS):
            rec = {}
            normed_f, rec["norm_one_back"] = jax.vjp(norm_piece, stream, gains[layer, 0])
            if layer == 0:
                normed = norm_piece(hidden_all.astype(f32), gains[0, 0]).astype(bf16)
            else:
                normed = gather_rows(normed_f.astype(bf16))
            in_w = input_weights(*after((mix_own[layer], shares[layer]), normed))
            mixed = matmul(normed, in_w)
            mixed_here = mixed
            if layer == 0:
                mixed_here = after(mixed, (swapped[0][1], swapped[1][0]))
            ssm_y, gated_low, states, squares = run_forward(
                plan, core_scalar, mixed, tap_rows[layer], shared_rows[layer], head_rows[layer]
            )
            sum_squares = sum_slot(squares[0])
            gated_scale = lax.rsqrt(sum_squares / (MH * P_SIZE) + eps_norm)
            scaled_low = (gated_low.astype(f32) * gated_scale).astype(bf16)
            attended, logsum, queries, keyval = run_attend(plan, query_part, mixed_here, *tables)
            mixer = jnp.concatenate([attended, scaled_low], axis=1)
            out_w = after(out_own[layer], gated_low).reshape(D, HD + width)
            middle = stream + scatter_product(mixer, out_w)
            normed_two_f, rec["norm_two_back"] = jax.vjp(norm_piece, middle, gains[layer, 1])
            normed_two = gather_rows(normed_two_f.astype(bf16))
            up_w, down_w = ffn_weights(after(ffn_own[layer], normed_two))
            gate_up = matmul(normed_two, up_w)
            gate_vals, up_vals = gate_up[:, :ff_own], gate_up[:, ff_own:]
            activation = (jax.nn.silu(gate_vals) * up_vals).astype(bf16)
            stream = (middle + scatter_product(activation, down_w)) * own_valid
            rec.update(
                normed=normed, mixed=mixed, ssm_y=ssm_y, gated_low=gated_low, states=states,
                mixer=mixer, gated_scale=gated_scale, queries=queries, keyval=keyval,
                logsum=logsum, normed_two=normed_two,
                gate_vals=gate_vals, up_vals=up_vals, activation=activation,
            )
            rec["weights"] = (in_w, out_w, up_w, down_w)
            records.append(rec)

        grad_stream = bring_in(cotangent).astype(f32)
        out_grads = [None] * LAYERS
        share_sums = []
        folded = [None] * LAYERS
        points = []
        came = [[] for _ in range(LAYERS)]
        for layer in reversed(range(LAYERS)):
            rec = records[layer]
            in_w, out_w, up_w, down_w = rec["weights"]
            grad_masked = grad_stream * own_valid
            if layer == LAYERS - 1:
                grad_ffn = gather_rows(grad_masked.astype(bf16))
            else:
                grad_ffn = gather_rows(grad_masked.astype(bf16))
            points.append([grad_ffn])
            grad_activation = matmul(grad_ffn, down_w)
            grad_down = product_tn(grad_ffn, rec["activation"])
            gate_vals = rec["gate_vals"]
            grad_gate = grad_activation * rec["up_vals"] * silu_grad(gate_vals)
            grad_upper = grad_activation * jax.nn.silu(gate_vals)
            grad_gate_up = jnp.concatenate([grad_gate, grad_upper], axis=1).astype(bf16)
            if layer + 1 < LAYERS:
                came[layer + 1].append(
                    after(group_swap(after(folded[layer + 1][0], grad_ffn)), grad_gate_up)
                )
            grad_upw = product_tn(rec["normed_two"], grad_gate_up)
            grad_normed_two = scatter_product(grad_gate_up, up_w)
            grad_middle_norm, grad_gain_two = rec["norm_two_back"](grad_normed_two)
            grad_middle = grad_masked + grad_middle_norm
            ffn_blocks = jnp.concatenate([grad_upw, grad_down], axis=1).reshape(
                ctx_count, depth, 3 * ff_own
            )
            folded[layer] = [fold_halves(ffn_blocks)]
            early = (ffn_blocks,) if layer + 1 == LAYERS else (ffn_blocks, folded[layer + 1][1])
            branch_rows = gather_rows(after(grad_middle.astype(bf16), early))
            points[-1].append(branch_rows)
            grad_mixer = matmul(branch_rows, out_w)
            out_blocks = product_tn(branch_rows, rec["mixer"]).reshape(
                ctx_count, depth, HD + width
            )
            if layer == 0:
                folded[layer].append(fold_halves(out_blocks))
            gated_scale = rec["gated_scale"]
            scale_part = jnp.sum(grad_mixer[:, HD:] * rec["gated_low"].astype(f32), axis=-1)
            grad_scale = after(sum_slot(scale_part), out_blocks)
            grad_squares = grad_scale * -0.5 * gated_scale * gated_scale * gated_scale / (MH * P_SIZE)
            if layer + 1 < LAYERS:
                came[layer + 1].append(group_swap(after(folded[layer + 1][1], branch_rows)))
            grad_q, grad_kv = run_attend_back(
                plan, query_part, rec["queries"], rec["keyval"], rec["logsum"], grad_mixer,
                *tables,
            )
            grad_bc, grad_pair, grad_step, taps_grad, grad_conv, heads_grad = run_backward(
                plan, core_scalar, rec["mixed"], tap_rows[layer], shared_rows[layer], head_rows[layer],
                rec["ssm_y"], rec["states"], grad_mixer,
                jnp.concatenate([gated_scale, 2.0 * grad_squares], axis=1),
            )
            chan_grad = taps_grad[: CONV + 2]
            grad_conv = grad_conv[: CONV + 1]
            grad_heads = jnp.concatenate(
                [heads_grad[:2, :heads], jnp.sum(taps_grad[6].reshape(heads, lanes), axis=1)[None]]
            )
            grad_mix_own = jnp.concatenate([grad_q, grad_pair], axis=1)
            grad_in = jnp.concatenate([grad_bc, grad_kv, grad_mix_own, grad_step], axis=1)
            if layer == 0:
                grad_in = after(grad_in, folded[layer][0])
            at_heads = [
                jnp.where(kv_head == head, grad_kv[:, part * HD : (part + 1) * HD], 0)
                for part in range(2)
                for head in range(KVH)
            ]
            step_cols = lax.dynamic_update_slice(
                jnp.zeros((seq_len, 128), bf16), grad_step[:, :heads], (0, dt_start - dt_cols)
            )
            grad_share = jnp.concatenate([grad_bc] + at_heads + [step_cols], axis=1)
            if layer == 0:
                grad_share = after(grad_share, folded[0][1])
            scattered = scatter_product(grad_in, in_w, grad_share)
            if layer > 0:
                scattered = after(scattered, folded[layer][0])
            grad_normed_one = scattered[:, :D]
            share_sums.append(share_columns(scattered[:, D:].astype(bf16)))
            points[-1] += [grad_in, grad_normed_one]
            grad_stream_norm, grad_gain_one = rec["norm_one_back"](grad_normed_one)
            grad_stream = grad_middle + grad_stream_norm
            grad_mix = product_tn(rec["normed"], grad_mix_own)[:, : HD + 2 * width]
            mix_blocks = grad_mix.reshape(ctx_count, depth, HD + 2 * width)
            if layer == 0:
                folded[layer].append(fold_last(mix_blocks))
            else:
                folded[layer].append(fold_halves(jnp.concatenate([out_blocks, mix_blocks], axis=2)))
            out_grads[layer] = (
                jnp.stack([grad_gain_one, grad_gain_two]), chan_grad, grad_conv, grad_heads,
            )
        last = points[-1]
        mix_kept, mix_got = folded[0][2]
        mix_sum = (mix_kept + after(mix_got, last[3]).astype(f32)).astype(bf16)
        out_sum, mix_sum = after((folded[0][1], mix_sum), last[3])
        came[0] = [
            group_swap(after(folded[0][0], last[3])),
            group_swap(jnp.concatenate([out_sum, mix_sum], axis=2)),
        ]

        share_grads = []
        for layer in range(LAYERS):
            normed = records[layer]["normed"]
            grad_share = share_sums[LAYERS - 1 - layer]
            near = lax.dynamic_slice_in_dim(normed, (slot * members + me) * depth, depth, 1)
            far = lax.dynamic_slice_in_dim(normed, ((1 - slot) * members + me) * depth, depth, 1)
            share_far = product_tn(far, grad_share)
            if layer == 0:
                share_far = after(share_far, came[0][1])
            share_far = lax.ppermute(share_far, half_axis, SWAP)
            if layer > 0:
                share_far = after(share_far, last[3])
            share_sum = product_tn(near, grad_share).astype(f32) + share_far.astype(f32)
            share_sum = share_sum.astype(bf16)
            for axis in tp_axes[::-1]:
                got = lax.ppermute(share_sum, axis, SWAP)
                first = lax.axis_index(axis) == 0
                share_sum = jnp.where(
                    first,
                    jnp.concatenate([share_sum, got], 1),
                    jnp.concatenate([got, share_sum], 1),
                )
            share_grads.append(share_sum[:, :share_cols].astype(f32))
        share_g = jnp.stack(share_grads)
        both_out = bring_out(jnp.stack([stream, grad_stream]))
        activations, input_grad = both_out[:, :, 0], both_out[:, :, 1]

        def weight_grads(layer):
            got = came[layer] if layer == 0 else after(came[layer], last[3])
            ffn_came, both_came = got
            out_came, mix_came = both_came[:, :, : HD + width], both_came[:, :, HD + width :]
            mix = jnp.concatenate(
                [
                    join_heads(mix_came[:, :, HD : HD + width], 1),
                    join_heads(mix_came[:, :, HD + width :], 1),
                    join_query_heads(mix_came[:, :, :HD], 1),
                ],
                axis=1,
            )
            out = jnp.concatenate(
                [join_heads(out_came[:, :, HD:], 1), join_query_heads(out_came[:, :, :HD], 1)],
                axis=1,
            )
            up = jnp.concatenate(
                [
                    ffn_came[g, :, part * ff_own : (part + 1) * ff_own]
                    for part in range(2)
                    for g in range(members)
                ],
                axis=1,
            )
            down = jnp.concatenate([ffn_came[g, :, 2 * ff_own :] for g in range(members)], axis=1)
            return mix, out.T, up, down.T

        by_layer = [weight_grads(layer) for layer in range(LAYERS)]
        mix_g, out_g, up_g, down_g = (jnp.stack(grads).astype(f32) for grads in zip(*by_layer))
        gain_g, chan_g, conv_g, head_g = (jnp.stack(grads) for grads in zip(*out_grads))
        chan_rows = jnp.zeros((LAYERS, CONV + 2, HGROUPS, heads, replicas, lanes), f32)
        chan_rows = lax.dynamic_update_slice(
            chan_rows,
            chan_g.reshape(LAYERS, CONV + 2, 1, heads, 1, lanes),
            (0, 0, head_group, 0, head_part, 0),
        ).reshape(LAYERS, CONV + 2, ssm_cols)
        head_rows = lax.dynamic_update_slice(
            jnp.zeros((LAYERS, 3, HGROUPS, heads), f32), head_g[:, :, None], (0, 0, head_group, 0)
        ).reshape(LAYERS, 3, tp_heads)

        def packed(arrays):
            flat = jnp.concatenate([a.reshape(-1) for a in arrays])
            return jnp.pad(flat, (0, -flat.shape[0] % 1024)).reshape(-1, 128)

        def unpacked(flat, arrays):
            flat, marks = flat.reshape(-1), [0]
            for a in arrays:
                marks.append(marks[-1] + a.size)
            return [flat[marks[k] : marks[k + 1]].reshape(a.shape) for k, a in enumerate(arrays)]

        early = (conv_g, gain_g[0, 1], gain_g[1:])
        whole = sum_over(packed(early), tp_axes[::-1])
        local_sums = (chan_rows, head_rows, whole)
        chan_sum, head_sum, whole = unpacked(
            sum_over(packed(local_sums), group_axes[::-1] + (half_axis,)), local_sums
        )
        conv_sum, gain_two, gain_rest = unpacked(whole, early)
        ctx_index = slot * members + me
        last_gain = jnp.repeat(gain_g[0, 0].reshape(ctx_count, 1, depth), 4, axis=1)
        last_gain = lax.all_to_all(
            last_gain.reshape(4 * ctx_count, 1, depth), all_axes, 0, 0, tiled=True
        )
        last_gain = jnp.sum(last_gain, axis=0)
        gain_rest = lax.dynamic_slice_in_dim(gain_rest, ctx_index * depth, depth, 2)
        gain_two = lax.dynamic_slice_in_dim(gain_two, ctx_index * depth, depth, 0)
        gain_own = jnp.concatenate([jnp.concatenate([last_gain, gain_two[None]])[None], gain_rest])
        return (
            activations,
            input_grad,
            gain_own,
            mix_g,
            share_g,
            chan_sum,
            conv_sum,
            head_sum,
            out_g,
            up_g,
            down_g,
        )

    return local


def solution(mesh):
    ctx_bits = mesh.shape["ctx"].bit_length() - 1
    tp_bits = mesh.shape["tp"].bit_length() - 1
    ctx_axes = tuple(f"c{k}" for k in range(ctx_bits))
    tp_axes = tuple(f"t{k}" for k in range(tp_bits))
    fine = Mesh(mesh.devices.reshape((2,) * (ctx_bits + tp_bits)), ctx_axes + tp_axes)
    return jax.shard_map(
        build(ctx_axes, tp_axes),
        mesh=fine,
        in_specs=(
            P(None, None, ctx_axes, None),
            P(None, None, ctx_axes, None),
            P(),
            P(None, None, ctx_axes),
            P(None, ctx_axes, tp_axes),
            P(None, ctx_axes, None),
            P(None, None, tp_axes),
            P(),
            P(None, None, tp_axes),
            P(None, tp_axes, ctx_axes),
            P(None, ctx_axes, tp_axes),
            P(None, tp_axes, ctx_axes),
        ),
        out_specs=(
            P(None, None, ctx_axes, None),
            P(None, None, ctx_axes, None),
            P(None, None, ctx_axes),
            P(None, ctx_axes, tp_axes),
            P(None, ctx_axes, None),
            P(None, None, tp_axes),
            P(),
            P(None, None, tp_axes),
            P(None, tp_axes, ctx_axes),
            P(None, ctx_axes, tp_axes),
            P(None, tp_axes, ctx_axes),
        ),
        check_vma=False,
    )
```

```python
import functools

import jax
import jax.numpy as jnp
from jax import lax
from jax.experimental import pallas as pl
from jax.experimental.pallas import tpu as pltpu
from jax.sharding import Mesh
from jax.sharding import PartitionSpec as P

D = 2048
MH = 48
P_SIZE = 64
N = 256
CONV = 4
AH = 8
KVH = 2
HD = 128
FF = 4096
LAYERS = 2
HGROUPS = 4
PAD = 8

eps_norm = 1e-05
rope_base = 100000000000.0
highest = lax.Precision.HIGHEST
SWAP = [(0, 1), (1, 0)]
bf16 = jnp.bfloat16
f32 = jnp.float32


def matmul(left_op, right_op):
    return jnp.dot(left_op, right_op, preferred_element_type=f32)


def matmul_tn(left_op, right_op):
    return lax.dot_general(left_op, right_op, (((0,), (0,)), ((), ())), preferred_element_type=f32)


def matmul_nt(left_op, right_op):
    return lax.dot_general(left_op, right_op, (((1,), (1,)), ((), ())), preferred_element_type=f32)


def product_tn_block(left, right, out):
    out[...] = dot_tn(left[...], right[...]).astype(bf16)


def product_tn(left, right):
    rows, m = left.shape
    n = right.shape[1]
    block = min(m, 1024 if rows <= 768 else 256)
    return pl.pallas_call(
        product_tn_block,
        grid=(m // block,),
        in_specs=[
            pl.BlockSpec((rows, block), lambda i: (0, i)),
            pl.BlockSpec((rows, n), lambda i: (0, 0)),
        ],
        out_specs=pl.BlockSpec((block, n), lambda i: (i, 0)),
        out_shape=jax.ShapeDtypeStruct((m, n), bf16),
        compiler_params=pltpu.CompilerParams(vmem_limit_bytes=30 * 2**20),
        cost_estimate=pl.CostEstimate(
            flops=2 * rows * m * n, bytes_accessed=2 * (rows * m + rows * n + m * n), transcendentals=0
        ),
    )(left, right)


def silu_grad(inputs):
    sigmoid = jax.nn.sigmoid(inputs)
    return sigmoid * (1.0 + inputs * (1.0 - sigmoid))


def after(x, point):
    return lax.optimization_barrier((x, point))[0]


def following(x, *points):
    zero = sum(jnp.minimum(jnp.abs(p.reshape(-1)[0].astype(f32)), 0.0) for p in points)
    return x + zero.astype(x.dtype)


def pick(x, dim, index):
    return lax.dynamic_index_in_dim(x, index, dim, keepdims=False)


def norm_piece(stream, gain_row):
    factor = lax.rsqrt(jnp.mean(stream * stream, axis=-1, keepdims=True) + eps_norm)
    return stream * factor * gain_row


def dot_nn(a, b):
    return lax.dot_general(a, b, (((1,), (0,)), ((), ())), preferred_element_type=f32)


def dot_nt(a, b):
    return lax.dot_general(a, b, (((1,), (1,)), ((), ())), preferred_element_type=f32)


def dot_tn(a, b):
    return lax.dot_general(a, b, (((0,), (0,)), ((), ())), preferred_element_type=f32)


def dot_exact(a, b):
    return lax.dot_general(
        a, b, (((1,), (0,)), ((), ())), precision=highest, preferred_element_type=f32
    )


def sigmoid(v):
    return 1.0 / (1.0 + jnp.exp(-v))


def block_place(block, members):
    quarter, at = block // members, block % members
    if quarter < 2:
        return at, 0, quarter
    return members - 1 - at, 1, 3 - quarter


class Plan:
    def __init__(self, seq_len, block_len, heads, lanes):
        self.seq_len = seq_len
        self.block_len = block_len
        self.heads = heads
        self.lanes = lanes
        self.width = heads * lanes
        self.members = seq_len // (4 * block_len)
        self.chunk = 4 * block_len
        self.chunks = seq_len // self.chunk
        self.query_parts = self.members // 2
        self.query_rows = seq_len // self.query_parts
        self.bc = 2 * N
        self.key_at = self.bc
        self.value_at = self.bc + HD
        self.q_at = self.bc + 2 * HD
        self.gate_at = self.bc + 3 * HD
        self.pair_cols = 2 * self.width
        self.pair_tiles = self.pair_cols + -self.pair_cols % 128
        self.step_at = self.gate_at + self.pair_tiles
        self.cols = self.step_at + 128

    def rows(self, core, block):
        member, half, place = block_place(block, self.members)
        other = core if place == 0 else 1 - core
        start = other * (self.seq_len // 2) + (2 * member + half) * self.block_len
        return pl.ds(pl.multiple_of(start, 16), self.block_len)

    def blocks(self):
        return range(self.seq_len // self.block_len)


def head_masks(plan):
    lane = lax.broadcasted_iota(jnp.int32, (1, plan.width), 1)
    return [
        ((lane >= h * plan.lanes) & (lane < (h + 1) * plan.lanes)).astype(f32)
        for h in range(plan.heads)
    ]


def over_heads(plan, tile, masks):
    return sum(tile[:, h : h + 1] * masks[h] for h in range(plan.heads))


def per_head(plan, values, masks):
    lane = lax.broadcasted_iota(jnp.int32, (1, 128), 1)
    total = None
    for h in range(plan.heads):
        column = jnp.sum(values * masks[h], axis=1, keepdims=True)
        part = column * (lane == h).astype(f32)
        total = part if total is None else total + part
    return total


def conv_values(source, taps_ref, rows, start, low, high):
    total = taps_ref[CONV : CONV + 1, low:high]
    for k in range(CONV):
        at = PAD + start - (CONV - 1) + k
        total = total + taps_ref[k : k + 1, low:high] * source[pl.ds(at, rows), low:high]
    return total


def prepare(plan, core, mixed, nat_bc, nat_x, nat_step):
    width = plan.width
    nat_bc[0:PAD, :] = jnp.zeros((PAD, plan.bc), f32)
    nat_x[0:PAD, :] = jnp.zeros((PAD, width), f32)
    for block in plan.blocks():
        at = PAD + block * plan.block_len
        rows = plan.rows(core, block)
        nat_bc[pl.ds(at, plan.block_len), :] = mixed[rows, 0 : plan.bc]
        pair = mixed[rows, plan.gate_at : plan.gate_at + plan.pair_tiles]
        nat_x[pl.ds(at, plan.block_len), :] = pltpu.roll(pair, plan.pair_tiles - width, 1)[:, :width]
        nat_step[pl.ds(at - PAD, plan.block_len), :] = mixed[rows, plan.step_at : plan.step_at + 128]


def chunk_decays(plan, nat_step, head_rows, c, tri):
    q = plan.chunk
    real = lax.broadcasted_iota(jnp.int32, (1, 128), 1) < plan.heads
    raw = jnp.where(real, nat_step[pl.ds(c * q, q), :] + head_rows[1:2, :], 0.0)
    step = jnp.where(real, jnp.maximum(raw, 0.0) + jnp.log(1.0 + jnp.exp(-jnp.abs(raw))), 0.0)
    cumulative = dot_exact(tri, step * head_rows[0:1, :])
    return raw, step, cumulative


def triangle(plan):
    q = plan.chunk
    row = lax.broadcasted_iota(jnp.int32, (q, q), 0)
    col = lax.broadcasted_iota(jnp.int32, (q, q), 1)
    return row, col


def ssm_forward(plan, core_ref, mixed, taps, shared_taps, head_rows, y_out, low_out, states_out, squares_out,
                nat_bc, nat_x, nat_step):
    q = plan.chunk
    masks = head_masks(plan)
    core = core_ref[0]
    prepare(plan, core, mixed, nat_bc, nat_x, nat_step)
    row, col = triangle(plan)
    lower = row >= col
    tri = lower.astype(f32)
    state = jnp.zeros((N, plan.width), f32)
    for c in range(plan.chunks):
        start = c * q
        x = conv_values(nat_x, taps, q, start, 0, plan.width)
        x = x * sigmoid(x)
        bc = conv_values(nat_bc, shared_taps, q, start, 0, plan.bc)
        bc = (bc * sigmoid(bc)).astype(bf16)
        b, cc = bc[:, :N], bc[:, N:]
        _, step, cum = chunk_decays(plan, nat_step, head_rows, c, tri)
        cum_rows = cum.T
        cum_full = over_heads(plan, cum, masks)
        total_full = cum_full[q - 1 : q, :]
        u = x * over_heads(plan, step, masks)
        inner = dot_nt(cc, b)
        states_out[c] = state
        y = dot_nn(cc, state.astype(bf16)) * jnp.exp(cum_full) + taps[6:7, :] * x
        for h in range(plan.heads):
            seg = jnp.where(lower, cum[:, h : h + 1] - cum_rows[h : h + 1, :], -1e30)
            mixing = (jnp.exp(seg) * inner).astype(bf16)
            y = y + dot_nn(mixing, (u * masks[h]).astype(bf16))
        weighted = (u * jnp.exp(total_full - cum_full)).astype(bf16)
        state = jnp.exp(total_full) * state + dot_tn(b, weighted)
        for k in range(4):
            block = 4 * c + k
            y_out[plan.rows(core, block), :] = y[k * plan.block_len : (k + 1) * plan.block_len, :]
    z = mixed[:, plan.gate_at : plan.gate_at + plan.width]
    gated = y_out[...] * (z * sigmoid(z))
    low_out[...] = (gated * taps[5:6, :]).astype(bf16)
    squares_out[...] = lax.dot_general(
        jnp.ones((8, plan.width), f32), gated * gated, (((1,), (1,)), ((), ())),
        precision=highest, preferred_element_type=f32,
    )


def ssm_backward(plan, core_ref, mixed, taps, shared_taps, head_rows, y_in, states, grad_mixer, scales,
                 bc_out, pair_out, step_out, taps_out, shared_out, heads_out,
                 nat_bc, nat_x, nat_step, nat_dy, grad_x, grad_bc, grad_y_ref):
    q = plan.chunk
    width = plan.width
    masks = head_masks(plan)
    core = core_ref[0]
    prepare(plan, core, mixed, nat_bc, nat_x, nat_step)
    row, col = triangle(plan)
    lower, upper = row >= col, row <= col
    strict_lower, strict_upper = row > col, row < col
    tri, tri_back = lower.astype(f32), upper.astype(f32)

    z = mixed[:, plan.gate_at : plan.gate_at + width]
    y = y_in[...]
    sig = sigmoid(z)
    silu = z * sig
    gated = y * silu
    scaled = grad_mixer[:, HD : HD + width] * scales[:, 0:1]
    grad_gated = scaled * taps[5:6, :] + scales[:, 1:2] * gated
    gain_grad = jnp.sum(scaled * gated, axis=0, keepdims=True)
    grad_z = grad_gated * y * (sig * (1.0 + z * (1.0 - sig)))
    spare = plan.pair_tiles - width
    pair_out[...] = jnp.concatenate(
        [grad_z, jnp.zeros((plan.seq_len, spare), f32)], axis=1
    ).astype(bf16)
    grad_y_ref[...] = grad_gated * silu
    for block in plan.blocks():
        at = block * plan.block_len
        nat_dy[pl.ds(at, plan.block_len), :] = grad_y_ref[plan.rows(core, block), :]

    grad_x[plan.seq_len : plan.seq_len + PAD, :] = jnp.zeros((PAD, width), f32)
    grad_bc[plan.seq_len : plan.seq_len + PAD, :] = jnp.zeros((PAD, plan.bc), f32)
    grad_state = jnp.zeros((N, width), f32)
    skip_grad = jnp.zeros((1, width), f32)
    rate_grad = jnp.zeros((1, 128), f32)
    bias_grad = jnp.zeros((1, 128), f32)
    for c in reversed(range(plan.chunks)):
        start = c * q
        x_lin = conv_values(nat_x, taps, q, start, 0, width)
        x_sig = sigmoid(x_lin)
        x = x_lin * x_sig
        bc_lin = conv_values(nat_bc, shared_taps, q, start, 0, plan.bc)
        bc_sig = sigmoid(bc_lin)
        bc = (bc_lin * bc_sig).astype(bf16)
        b, cc = bc[:, :N], bc[:, N:]
        raw, step, cum = chunk_decays(plan, nat_step, head_rows, c, tri)
        cum_rows = cum.T
        cum_full = over_heads(plan, cum, masks)
        total_full = cum_full[q - 1 : q, :]
        step_full = over_heads(plan, step, masks)
        u = x * step_full
        u_low = u.astype(bf16)
        dy = nat_dy[pl.ds(start, q), :]
        dy_low = dy.astype(bf16)
        state = states[c]
        state_low = state.astype(bf16)
        grad_state_low = grad_state.astype(bf16)
        entry = jnp.exp(cum_full)
        exit_w = jnp.exp(total_full - cum_full)
        total_decay = jnp.exp(total_full)
        dy_entry = (dy * entry).astype(bf16)
        grad_c = dot_nt(dy_entry, state_low)
        carried = dot_nn(cc, state_low) * entry
        du_state = dot_nn(b, grad_state_low) * exit_w
        grad_b = dot_nt((u * exit_w).astype(bf16), grad_state_low)
        inner = dot_nt(cc, b)
        inner_t = dot_nt(b, cc)
        du = du_state
        grad_inner = jnp.zeros((q, q), f32)
        grad_inner_t = jnp.zeros((q, q), f32)
        lane = lax.broadcasted_iota(jnp.int32, (1, 128), 1)
        dcum = per_head(plan, dy * carried - u * du_state, masks)
        for h in range(plan.heads):
            here = (lane == h).astype(f32)
            u_head = (u * masks[h]).astype(bf16)
            dy_head = (dy * masks[h]).astype(bf16)
            seg = cum[:, h : h + 1] - cum_rows[h : h + 1, :]
            decay = jnp.exp(jnp.where(lower, seg, -1e30))
            decay_t = jnp.exp(jnp.where(upper, -seg, -1e30))
            grad_mix = dot_nt(dy_head, u_low) * decay
            grad_mix_t = dot_nt(u_head, dy_low) * decay_t
            grad_inner = grad_inner + grad_mix
            grad_inner_t = grad_inner_t + grad_mix_t
            du = du + dot_nn((decay_t * inner_t).astype(bf16), dy_head)
            out_sum = jnp.sum(jnp.where(strict_lower, grad_mix * inner, 0.0), axis=1, keepdims=True)
            in_sum = jnp.sum(
                jnp.where(strict_upper, grad_mix_t * inner_t, 0.0), axis=1, keepdims=True
            )
            dcum = dcum + (out_sum - in_sum) * here
        grad_c = grad_c + dot_nn(grad_inner.astype(bf16), b)
        grad_b = grad_b + dot_nn(grad_inner_t.astype(bf16), cc)
        whole = jnp.sum(u * du_state, axis=0, keepdims=True) + jnp.sum(
            grad_state * state, axis=0, keepdims=True
        ) * total_decay
        dlog = dot_exact(tri_back, dcum) + per_head(plan, whole, masks)
        rate_grad = rate_grad + jnp.sum(dlog * step, axis=0, keepdims=True)
        grad_step = dlog * head_rows[0:1, :] + per_head(plan, du * x, masks)
        grad_raw = grad_step * sigmoid(raw)
        bias_grad = bias_grad + jnp.sum(grad_raw, axis=0, keepdims=True)
        grad_xc = du * step_full + taps[6:7, :] * dy
        skip_grad = skip_grad + jnp.sum(dy * x, axis=0, keepdims=True)
        grad_state = total_decay * grad_state + dot_tn(cc, dy_entry)
        grad_x[pl.ds(start, q), :] = grad_xc * (x_sig * (1.0 + x_lin * (1.0 - x_sig)))
        grad_bc[pl.ds(start, q), :] = jnp.concatenate([grad_b, grad_c], axis=1) * (
            bc_sig * (1.0 + bc_lin * (1.0 - bc_sig))
        )
        for k in range(4):
            step_out[plan.rows(core, 4 * c + k), :] = grad_raw[
                k * plan.block_len : (k + 1) * plan.block_len, :
            ].astype(bf16)

    size = plan.block_len
    tap_grads = [jnp.zeros((1, width), f32) for _ in range(CONV + 1)]
    shared_grads = [jnp.zeros((1, plan.bc), f32) for _ in range(CONV + 1)]
    lane = lax.broadcasted_iota(jnp.int32, (1, plan.pair_tiles), 1)
    for c in range(plan.chunks):
        start = c * q
        dx = grad_x[pl.ds(start, q), :]
        dbc = grad_bc[pl.ds(start, q), :]
        tap_grads[CONV] += jnp.sum(dx, axis=0, keepdims=True)
        shared_grads[CONV] += jnp.sum(dbc, axis=0, keepdims=True)
        pre_dx = None
        pre_dbc = None
        for k in range(CONV):
            at = PAD + start - (CONV - 1) + k
            tap_grads[k] += jnp.sum(dx * nat_x[pl.ds(at, q), :], axis=0, keepdims=True)
            shared_grads[k] += jnp.sum(dbc * nat_bc[pl.ds(at, q), :], axis=0, keepdims=True)
            ahead = start + (CONV - 1) - k
            part = taps[k : k + 1, :] * grad_x[pl.ds(ahead, q), :]
            pre_dx = part if k == 0 else pre_dx + part
            part = shared_taps[k : k + 1, :] * grad_bc[pl.ds(ahead, q), :]
            pre_dbc = part if k == 0 else pre_dbc + part
        tile = jnp.concatenate([pre_dx, jnp.zeros((q, spare), f32)], axis=1)
        tile = pltpu.roll(tile, width, 1).astype(bf16)
        for k in range(4):
            rows = plan.rows(core, 4 * c + k)
            pair_out[rows, :] = jnp.where(
                lane < width, pair_out[rows, :], tile[k * size : (k + 1) * size, :]
            )
            bc_out[rows, :] = pre_dbc[k * size : (k + 1) * size, :].astype(bf16)
    for k in range(CONV + 1):
        taps_out[k : k + 1, :] = tap_grads[k]
        shared_out[k : k + 1, :] = shared_grads[k]
    taps_out[5:6, :] = gain_grad
    taps_out[6:7, :] = skip_grad
    heads_out[0:1, :] = rate_grad * head_rows[0:1, :]
    heads_out[1:2, :] = bias_grad


def whole_specs(arrays):
    def spec(array):
        zeros = (0,) * len(array.shape)
        return pl.BlockSpec(array.shape, lambda i: zeros, pipeline_mode=pl.Buffered(1))

    return [spec(array) for array in arrays]


def call_whole(plan, kernel, outs, scratch, flops, inputs, scalars=()):
    return pl.pallas_call(
        kernel,
        grid=(1,),
        in_specs=[pl.BlockSpec(memory_space=pltpu.SMEM) for _ in scalars] + whole_specs(inputs),
        out_specs=tuple(whole_specs(outs)),
        out_shape=tuple(outs),
        scratch_shapes=scratch,
        compiler_params=ssm_params(plan),
        cost_estimate=pl.CostEstimate(
            flops=flops, bytes_accessed=plan.seq_len * 8192, transcendentals=0
        ),
    )(*scalars, *inputs)


def ssm_params(plan):
    limit = 58 * 2**20
    return pltpu.CompilerParams(vmem_limit_bytes=limit)


def run_forward(plan, core, *inputs):
    t, w = plan.seq_len, plan.width
    outs = [
        jax.ShapeDtypeStruct((t, w), f32),
        jax.ShapeDtypeStruct((t, w), bf16),
        jax.ShapeDtypeStruct((plan.chunks, N, w), f32),
        jax.ShapeDtypeStruct((8, t), f32),
    ]
    scratch = [
        pltpu.VMEM((PAD + t, plan.bc), f32),
        pltpu.VMEM((PAD + t, w), f32),
        pltpu.VMEM((t, 128), f32),
    ]
    return call_whole(
        plan, functools.partial(ssm_forward, plan), outs, scratch, 40000 * t * w, inputs, (core,)
    )


def run_backward(plan, core, *inputs):
    t, w = plan.seq_len, plan.width
    outs = [
        jax.ShapeDtypeStruct((t, plan.bc), bf16),
        jax.ShapeDtypeStruct((t, plan.pair_tiles), bf16),
        jax.ShapeDtypeStruct((t, 128), bf16),
        jax.ShapeDtypeStruct((8, w), f32),
        jax.ShapeDtypeStruct((8, plan.bc), f32),
        jax.ShapeDtypeStruct((8, 128), f32),
    ]
    scratch = [
        pltpu.VMEM((PAD + t, plan.bc), f32),
        pltpu.VMEM((PAD + t, w), f32),
        pltpu.VMEM((t, 128), f32),
        pltpu.VMEM((t, w), f32),
        pltpu.VMEM((t + PAD, w), f32),
        pltpu.VMEM((t + PAD, plan.bc), f32),
        pltpu.VMEM((t, w), f32),
    ]
    return call_whole(
        plan, functools.partial(ssm_backward, plan), outs, scratch, 90000 * t * w, inputs, (core,)
    )


def attend_scores(plan, queries, keys, query_pos, key_pos):
    scores = dot_nt(queries, keys) * HD ** (-0.5)
    return jnp.where(key_pos <= query_pos, scores, -1e30)


def turned(x, cosine, sine):
    return x * cosine + pltpu.roll(x, HD // 2, 1) * sine


def attend_forward(plan, part, mixed, cosine, sine, query_pos, key_pos,
                   att_out, log_out, q_out, kv_out):
    rows = pl.ds(pl.multiple_of(part[0] * plan.query_rows, 8), plan.query_rows)
    keys = turned(mixed[:, plan.key_at : plan.key_at + HD], cosine[...], sine[...]).astype(bf16)
    values = mixed[:, plan.value_at : plan.value_at + HD].astype(bf16)
    kv_out[:, :HD] = keys
    kv_out[:, HD:] = values
    queries = mixed[rows, plan.q_at : plan.q_at + HD]
    queries = turned(queries, cosine[rows, :], sine[rows, :]).astype(bf16)
    q_out[...] = queries
    scores = attend_scores(plan, queries, keys, query_pos[rows, :], key_pos[...])
    peak = jnp.max(scores, axis=1, keepdims=True)
    weights = jnp.exp(scores - peak)
    total = jnp.sum(weights, axis=1, keepdims=True)
    probs = (weights / total).astype(bf16)
    att_out[...] = jnp.zeros((plan.seq_len, HD), bf16)
    att_out[rows, :] = dot_nn(probs, values).astype(bf16)
    log_out[...] = peak + jnp.log(total)


def attend_backward(plan, part, queries, kv, logs, grad_mixer, cosine, sine, query_pos, key_pos,
                    q_out, kv_out):
    rows = pl.ds(pl.multiple_of(part[0] * plan.query_rows, 8), plan.query_rows)
    keys, values = kv[:, :HD], kv[:, HD:]
    scale = HD ** (-0.5)
    q, grad = queries[...], grad_mixer[rows, :HD].astype(bf16)
    probs = jnp.exp(attend_scores(plan, q, keys, query_pos[rows, :], key_pos[...]) - logs[...])
    grad_probs = dot_nt(grad, values)
    inner = jnp.sum(probs * grad_probs, axis=1, keepdims=True)
    grad_scores = (probs * (grad_probs - inner)).astype(bf16)
    grad_q = dot_nn(grad_scores, keys) * scale
    q_out[...] = jnp.zeros((plan.seq_len, HD), bf16)
    q_out[rows, :] = turned(grad_q, cosine[rows, :], -sine[rows, :]).astype(bf16)
    grad_k = dot_tn(grad_scores, q) * scale
    kv_out[:, :HD] = turned(grad_k, cosine[...], -sine[...]).astype(bf16)
    kv_out[:, HD:] = dot_tn(probs.astype(bf16), grad).astype(bf16)


def run_attend(plan, part, *inputs):
    t, rows = plan.seq_len, plan.query_rows
    outs = [
        jax.ShapeDtypeStruct((t, HD), bf16),
        jax.ShapeDtypeStruct((rows, 1), f32),
        jax.ShapeDtypeStruct((rows, HD), bf16),
        jax.ShapeDtypeStruct((t, 2 * HD), bf16),
    ]
    kernel = functools.partial(attend_forward, plan)
    return call_whole(plan, kernel, outs, [], 4 * rows * t * HD, inputs, (part,))


def run_attend_back(plan, part, *inputs):
    t = plan.seq_len
    outs = [jax.ShapeDtypeStruct((t, HD), bf16), jax.ShapeDtypeStruct((t, 2 * HD), bf16)]
    kernel = functools.partial(attend_backward, plan)
    return call_whole(plan, kernel, outs, [], 10 * plan.query_rows * t * HD, inputs, (part,))


def build(ctx_axes, tp_axes):
    half_axis = ctx_axes[0]
    group_axes = ctx_axes[1:]
    t_half, t_core = tp_axes
    ring_axes = group_axes + (t_half,)
    slot_axes = group_axes + tp_axes
    all_axes = ctx_axes + tp_axes
    span = len(ring_axes)

    def column_parts(width):
        unit = width // 128
        marks = [0] + [128 * (unit * (k + 1) // 3) for k in range(3)]
        return list(zip(marks[:-1], marks[1:]))

    def rotated(part):
        turn = part % span
        return ring_axes[turn:] + ring_axes[:turn]

    def gather_rows(x):
        rows, width = x.shape
        parts = []
        for part, (low, high) in enumerate(column_parts(width)):
            held = x[:, low:high].reshape((1,) * span + (rows, high - low))
            for axis in rotated(part):
                dim = ring_axes.index(axis)
                got = lax.ppermute(held, axis, SWAP)
                first = lax.axis_index(axis) == 0
                held = jnp.where(
                    first, jnp.concatenate([held, got], dim), jnp.concatenate([got, held], dim)
                )
            parts.append(held)
        held = lax.optimization_barrier(jnp.concatenate(parts, -1).reshape(-1, width))
        return jnp.concatenate([held, lax.ppermute(held, t_core, SWAP)])

    def scatter_product(left, right, extra=None):
        total = left.shape[0]
        width = right.shape[0]
        peers = 2 ** (span + 1)
        rows = total // peers
        own = total // 2
        sent = matmul_nt(left[own:], right).astype(bf16)
        kept = matmul_nt(left[:own], right)
        if extra is not None:
            width += extra.shape[1]
            sent = jnp.concatenate([sent, extra[own:]], axis=1)
            kept = jnp.concatenate([kept, extra[:own].astype(f32)], axis=1)
        held = kept + lax.ppermute(sent, t_core, SWAP).astype(f32)
        parts = []
        for part, (low, high) in enumerate(column_parts(width)):
            piece = held[:, low:high].reshape((2,) * span + (rows, high - low))
            names = list(ring_axes)
            for axis in rotated(part):
                dim = names.index(axis)
                names.pop(dim)
                index = lax.axis_index(axis)
                got = lax.ppermute(pick(piece, dim, 1 - index).astype(bf16), axis, SWAP)
                piece = pick(piece, dim, index) + got.astype(f32)
            parts.append(piece)
        return jnp.concatenate(parts, -1)

    def sum_slot(x):
        turn = lax.axis_index(t_core) == 1
        x = x.reshape(2, -1, 128)
        x = jnp.where(turn, x[::-1], x)
        came = lax.all_to_all(
            jnp.broadcast_to(x[None], (2 ** (span + 1),) + x.shape), slot_axes, 0, 0, tiled=True
        )
        x = jnp.sum(came, axis=0)
        return jnp.where(turn, x[::-1], x).reshape(-1, 1)

    def sum_over(x, axes):
        for axis in axes:
            x = x + lax.ppermute(x, axis, SWAP)
        return x

    def group_index():
        return lax.axis_index(group_axes)

    def group_swap(blocks):
        return lax.all_to_all(blocks, group_axes, 0, 0, tiled=True)

    def both_halves(came):
        return lax.all_gather(came, half_axis, axis=0, tiled=True)

    def spread_first(blocks):
        return lax.all_to_all(jnp.concatenate([blocks, blocks]), ctx_axes, 0, 0, tiled=True)

    def fold_halves(blocks):
        return lax.psum_scatter(blocks.astype(bf16), half_axis, scatter_dimension=0, tiled=True)

    def fold_last(blocks):
        half = lax.axis_index(half_axis)
        paired = blocks.reshape((2, blocks.shape[0] // 2) + blocks.shape[1:])
        got = lax.ppermute(pick(paired, 0, 1 - half).astype(bf16), half_axis, SWAP)
        return pick(paired, 0, half).astype(f32), got

    def gather_lanes(x):
        for axis in ctx_axes[::-1]:
            got = lax.ppermute(x, axis, SWAP)
            first = lax.axis_index(axis) == 0
            x = jnp.where(first, jnp.concatenate([x, got], -1), jnp.concatenate([got, x], -1))
        return x

    def local(
        hidden,
        cotangent,
        lengths,
        norm_gains,
        mix_weight,
        share_weight,
        chan_params,
        shared_conv,
        head_params,
        out_weight,
        up_weight,
        down_weight,
    ):
        members = 2 ** len(group_axes)
        ctx_count = 2 * members
        replicas = members // HGROUPS
        slot = lax.axis_index(half_axis)
        me = group_index()
        head_group = me // replicas
        head_part = me % replicas
        tp_half = lax.axis_index(t_half)
        tp_core = lax.axis_index(t_core)
        tp_index = tp_half * 2 + tp_core
        block_len = hidden.shape[2]
        depth = mix_weight.shape[1]
        seq_len = 2 * ctx_count * block_len
        own_len = 4 * block_len
        tp_heads = chan_params.shape[2] // P_SIZE
        heads = tp_heads // HGROUPS
        lanes = P_SIZE // replicas
        width = heads * lanes
        ssm_cols = tp_heads * P_SIZE
        qheads = AH // 4
        q_cols = qheads * HD
        ff_tp = FF // 4
        ff_own = ff_tp // members
        plan = Plan(seq_len, block_len, heads, lanes)
        own_head = me // plan.query_parts
        core_scalar = tp_core.astype(jnp.int32).reshape(1)
        query_part = (me % plan.query_parts).astype(jnp.int32).reshape(1)
        share_cols = share_weight.shape[2]
        kv_cols = 2 * N
        dt_cols = 2 * N + 2 * KVH * HD
        kv_head = tp_index * qheads // (AH // KVH)
        score_scale = HD ** (-0.5)

        def block_of(member, half, cube):
            near = cube * members + member
            return jnp.where(half == 0, near, 2 * ctx_count - 1 - near)

        within = jnp.arange(block_len)
        own_pos = block_of(me, tp_half, tp_core) * block_len + within
        own_valid = (own_pos < lengths[slot]).astype(f32)[:, None]
        ring = jnp.arange(2 * members)

        def core_positions(core):
            first = block_of(ring // 2, ring % 2, core) * block_len
            return (first[:, None] + within[None, :]).reshape(-1)

        key_pos = jnp.concatenate([core_positions(tp_core), core_positions(1 - tp_core)])
        half_dim = HD // 2
        inverse = jnp.exp(-jnp.log(rope_base) * (2.0 * jnp.arange(half_dim, dtype=f32) / HD))
        angles = key_pos.astype(f32)[:, None] * inverse
        cosine = jnp.concatenate([jnp.cos(angles)] * 2, axis=1)
        sine = jnp.concatenate([-jnp.sin(angles), jnp.sin(angles)], axis=1)

        tables = (cosine, sine, key_pos[:, None], key_pos[None, :])

        def cut_query_heads(x, axis):
            shape = x.shape
            split = x.reshape(shape[:axis] + (qheads, HD) + shape[axis + 1 :])
            return jnp.repeat(jnp.moveaxis(split, axis, 0), plan.query_parts, axis=0)

        def join_query_heads(x, axis):
            summed = jnp.sum(
                x.astype(f32).reshape((qheads, plan.query_parts) + x.shape[1:]), axis=1
            ).astype(bf16)
            joined = jnp.moveaxis(summed, 0, axis)
            shape = joined.shape
            return joined.reshape(shape[:axis] + (q_cols,) + shape[axis + 2 :])

        def bring_in(x):
            got = lax.ppermute(
                pick(pick(x, 0, 1 - slot), 0, tp_half), (half_axis, t_core), [(0, 2), (3, 1)]
            )
            return jnp.where(tp_core == slot, pick(pick(x, 0, slot), 0, tp_half), got)

        def share_columns(own):
            quarter = own.shape[1] // 4
            chunks = jnp.moveaxis(own.reshape(block_len, 4, quarter), 1, 0)
            chunks = jnp.broadcast_to(chunks[None], (members,) + chunks.shape)
            rows = lax.all_to_all(
                chunks.reshape(4 * members, block_len, quarter), slot_axes, 0, 0, tiled=True
            )
            rows = jnp.moveaxis(rows.reshape(2 * members, 2, block_len, quarter), 1, 0)
            return jnp.where(tp_core == 0, rows, rows[::-1]).reshape(seq_len, quarter)

        def bring_out(x):
            x = x.astype(bf16)
            got = lax.ppermute(x, (half_axis, t_core), [(1, 3), (2, 0)])
            pair = jnp.where(slot == 0, jnp.stack([x, got]), jnp.stack([got, x]))
            other = lax.ppermute(pair, t_core, SWAP)
            pair = jnp.where(tp_core == slot, pair, other)
            other = lax.ppermute(pair, t_half, SWAP)
            both = jnp.where(tp_half == 0, jnp.stack([pair, other], 1), jnp.stack([other, pair], 1))
            return both.astype(f32)

        def cut_heads(x, axis):
            shape = x.shape
            split = x.reshape(
                shape[:axis] + (HGROUPS, heads, replicas, lanes) + shape[axis + 1 :]
            )
            split = jnp.moveaxis(split, (axis, axis + 2), (0, 1))
            return split.reshape((members,) + shape[:axis] + (width,) + shape[axis + 1 :])

        def join_heads(x, axis):
            if replicas == 1:
                return jnp.concatenate([x[g] for g in range(members)], axis=axis)
            shape = x.shape[1:]
            split = x.reshape(
                (HGROUPS, replicas) + shape[:axis] + (heads, lanes) + shape[axis + 1 :]
            )
            split = jnp.moveaxis(split, (0, 1), (axis, axis + 2))
            return split.reshape(shape[:axis] + (ssm_cols,) + shape[axis + 1 :])

        gains = gather_lanes(norm_gains).astype(f32)
        hidden_rows = bring_in(after(hidden, gains))
        stream = hidden_rows.astype(f32)
        own_chan = pick(cut_heads(chan_params, 2), 0, me)
        own_heads = pick(head_params.reshape(LAYERS, 3, HGROUPS, heads), 2, head_group)
        skip_full = jnp.repeat(own_heads[:, 2], lanes, axis=1)[:, None]
        tap_rows = jnp.concatenate([own_chan, skip_full, jnp.zeros_like(skip_full)], axis=1)
        shared_rows = jnp.pad(shared_conv, ((0, 0), (0, 3), (0, 0)))
        head_rows = jnp.pad(
            jnp.stack([-jnp.exp(own_heads[:, 0]), own_heads[:, 1]], axis=1),
            ((0, 0), (0, 6), (0, 128 - heads)),
        )
        share_rows = lax.dynamic_slice_in_dim(share_weight, tp_core * (depth // 2), depth // 2, 1)
        dt_start = dt_cols + tp_index * tp_heads + head_group * heads

        def weight_blocks(layer):
            mix = mix_weight[layer]
            mix_blocks = jnp.concatenate(
                [
                    cut_query_heads(mix[:, 2 * ssm_cols :], 1),
                    cut_heads(mix[:, :ssm_cols], 1),
                    cut_heads(mix[:, ssm_cols : 2 * ssm_cols], 1),
                ],
                2,
            )
            out = out_weight[layer].T
            out_blocks = jnp.concatenate(
                [cut_query_heads(out[:, ssm_cols:], 1), cut_heads(out[:, :ssm_cols], 1)], 2
            )
            up = up_weight[layer]
            down = down_weight[layer].T
            ffn_blocks = jnp.stack(
                [
                    jnp.concatenate(
                        [
                            up[:, g * ff_own : (g + 1) * ff_own],
                            up[:, ff_tp + g * ff_own : ff_tp + (g + 1) * ff_own],
                            down[:, g * ff_own : (g + 1) * ff_own],
                        ],
                        axis=1,
                    )
                    for g in range(members)
                ]
            )
            return mix_blocks, out_blocks, ffn_blocks

        def share_whole(share):
            share = jnp.concatenate(
                [
                    share[:, :kv_cols],
                    lax.dynamic_slice_in_dim(share, kv_cols + kv_head * HD, HD, 1),
                    lax.dynamic_slice_in_dim(share, kv_cols + (KVH + kv_head) * HD, HD, 1),
                    share[:, dt_cols:],
                ],
                axis=1,
            )
            return lax.all_gather(share, ctx_axes + (t_core,), axis=0, tiled=True)

        def input_weights(mix_own, share):
            dt_w = lax.dynamic_slice_in_dim(share, kv_cols + 2 * HD + dt_start - dt_cols, heads, 1)
            return jnp.concatenate(
                [
                    share[:, : plan.q_at],
                    jnp.pad(
                        mix_own.reshape(D, HD + 2 * width),
                        ((0, 0), (0, plan.pair_tiles - plan.pair_cols)),
                    ),
                    jnp.pad(dt_w, ((0, 0), (0, 128 - heads))),
                ],
                axis=1,
            )

        def ffn_weights(ffn_own):
            ffn_own = ffn_own.reshape(D, 3 * ff_own)
            return ffn_own[:, : 2 * ff_own], ffn_own[:, 2 * ff_own :]

        blocks = [weight_blocks(layer) for layer in range(LAYERS)]
        mix_own = [None] * LAYERS
        out_own = [None] * LAYERS
        ffn_own = [None] * LAYERS
        shares = [None] * LAYERS
        mix_own[0] = spread_first(blocks[0][0])
        out_cols = HD + width
        hidden_all = gather_rows(hidden_rows)
        swapped = [[group_swap(following(x, mix_own[0])) for x in blocks[0][1:]]]
        for layer in range(1, LAYERS):
            both = group_swap(jnp.concatenate(blocks[layer][:2], axis=2))
            swapped.append([both[:, :, -out_cols:], group_swap(blocks[layer][2])])
            mix_own[layer] = both_halves(both[:, :, :-out_cols])
        for layer in range(LAYERS):
            shares[layer] = share_whole(share_rows[layer])
            out_own[layer] = both_halves(swapped[layer][0])
            ffn_own[layer] = both_halves(swapped[layer][1])

        records = []
        for layer in range(LAYERS):
            rec = {}
            normed_f, rec["norm_one_back"] = jax.vjp(norm_piece, stream, gains[layer, 0])
            if layer == 0:
                normed = norm_piece(hidden_all.astype(f32), gains[0, 0]).astype(bf16)
            else:
                normed = gather_rows(normed_f.astype(bf16))
            in_w = input_weights(*after((mix_own[layer], shares[layer]), normed))
            mixed = matmul(normed, in_w)
            mixed_here = mixed
            if layer == 0:
                mixed_here = after(mixed, (swapped[0][1], swapped[1][0]))
            ssm_y, gated_low, states, squares = run_forward(
                plan, core_scalar, mixed, tap_rows[layer], shared_rows[layer], head_rows[layer]
            )
            sum_squares = sum_slot(squares[0])
            gated_scale = lax.rsqrt(sum_squares / (MH * P_SIZE) + eps_norm)
            scaled_low = (gated_low.astype(f32) * gated_scale).astype(bf16)
            attended, logsum, queries, keyval = run_attend(plan, query_part, mixed_here, *tables)
            mixer = jnp.concatenate([attended, scaled_low], axis=1)
            out_w = after(out_own[layer], gated_low).reshape(D, HD + width)
            middle = stream + scatter_product(mixer, out_w)
            normed_two_f, rec["norm_two_back"] = jax.vjp(norm_piece, middle, gains[layer, 1])
            normed_two = gather_rows(normed_two_f.astype(bf16))
            up_w, down_w = ffn_weights(after(ffn_own[layer], normed_two))
            gate_up = matmul(normed_two, up_w)
            gate_vals, up_vals = gate_up[:, :ff_own], gate_up[:, ff_own:]
            activation = (jax.nn.silu(gate_vals) * up_vals).astype(bf16)
            stream = (middle + scatter_product(activation, down_w)) * own_valid
            rec.update(
                normed=normed, mixed=mixed, ssm_y=ssm_y, gated_low=gated_low, states=states,
                mixer=mixer, gated_scale=gated_scale, queries=queries, keyval=keyval,
                logsum=logsum, normed_two=normed_two,
                gate_vals=gate_vals, up_vals=up_vals, activation=activation,
            )
            rec["weights"] = (in_w, out_w, up_w, down_w)
            records.append(rec)

        grad_stream = bring_in(cotangent).astype(f32)
        out_grads = [None] * LAYERS
        share_sums = []
        folded = [None] * LAYERS
        points = []
        came = [[] for _ in range(LAYERS)]
        for layer in reversed(range(LAYERS)):
            rec = records[layer]
            in_w, out_w, up_w, down_w = rec["weights"]
            grad_masked = grad_stream * own_valid
            if layer == LAYERS - 1:
                grad_ffn = gather_rows(grad_masked.astype(bf16))
            else:
                grad_ffn = gather_rows(grad_masked.astype(bf16))
            points.append([grad_ffn])
            grad_activation = matmul(grad_ffn, down_w)
            grad_down = product_tn(grad_ffn, rec["activation"])
            gate_vals = rec["gate_vals"]
            grad_gate = grad_activation * rec["up_vals"] * silu_grad(gate_vals)
            grad_upper = grad_activation * jax.nn.silu(gate_vals)
            grad_gate_up = jnp.concatenate([grad_gate, grad_upper], axis=1).astype(bf16)
            if layer + 1 < LAYERS:
                came[layer + 1].append(
                    after(group_swap(after(folded[layer + 1][0], grad_ffn)), grad_gate_up)
                )
            grad_upw = product_tn(rec["normed_two"], grad_gate_up)
            grad_normed_two = scatter_product(grad_gate_up, up_w)
            grad_middle_norm, grad_gain_two = rec["norm_two_back"](grad_normed_two)
            grad_middle = grad_masked + grad_middle_norm
            ffn_blocks = jnp.concatenate([grad_upw, grad_down], axis=1).reshape(
                ctx_count, depth, 3 * ff_own
            )
            folded[layer] = [fold_halves(ffn_blocks)]
            early = (ffn_blocks,) if layer + 1 == LAYERS else (ffn_blocks, folded[layer + 1][1])
            branch_rows = gather_rows(after(grad_middle.astype(bf16), early))
            points[-1].append(branch_rows)
            grad_mixer = matmul(branch_rows, out_w)
            out_blocks = product_tn(branch_rows, rec["mixer"]).reshape(
                ctx_count, depth, HD + width
            )
            if layer == 0:
                folded[layer].append(fold_halves(out_blocks))
            gated_scale = rec["gated_scale"]
            scale_part = jnp.sum(grad_mixer[:, HD:] * rec["gated_low"].astype(f32), axis=-1)
            grad_scale = after(sum_slot(scale_part), out_blocks)
            grad_squares = grad_scale * -0.5 * gated_scale * gated_scale * gated_scale / (MH * P_SIZE)
            if layer + 1 < LAYERS:
                came[layer + 1].append(group_swap(after(folded[layer + 1][1], branch_rows)))
            grad_q, grad_kv = run_attend_back(
                plan, query_part, rec["queries"], rec["keyval"], rec["logsum"], grad_mixer,
                *tables,
            )
            grad_bc, grad_pair, grad_step, taps_grad, grad_conv, heads_grad = run_backward(
                plan, core_scalar, rec["mixed"], tap_rows[layer], shared_rows[layer], head_rows[layer],
                rec["ssm_y"], rec["states"], grad_mixer,
                jnp.concatenate([gated_scale, 2.0 * grad_squares], axis=1),
            )
            chan_grad = taps_grad[: CONV + 2]
            grad_conv = grad_conv[: CONV + 1]
            grad_heads = jnp.concatenate(
                [heads_grad[:2, :heads], jnp.sum(taps_grad[6].reshape(heads, lanes), axis=1)[None]]
            )
            grad_mix_own = jnp.concatenate([grad_q, grad_pair], axis=1)
            grad_in = jnp.concatenate([grad_bc, grad_kv, grad_mix_own, grad_step], axis=1)
            if layer == 0:
                grad_in = after(grad_in, folded[layer][0])
            at_heads = [
                jnp.where(kv_head == head, grad_kv[:, part * HD : (part + 1) * HD], 0)
                for part in range(2)
                for head in range(KVH)
            ]
            step_cols = lax.dynamic_update_slice(
                jnp.zeros((seq_len, 128), bf16), grad_step[:, :heads], (0, dt_start - dt_cols)
            )
            grad_share = jnp.concatenate([grad_bc] + at_heads + [step_cols], axis=1)
            if layer == 0:
                grad_share = after(grad_share, folded[0][1])
            scattered = scatter_product(grad_in, in_w, grad_share)
            if layer > 0:
                scattered = after(scattered, folded[layer][0])
            grad_normed_one = scattered[:, :D]
            share_sums.append(share_columns(scattered[:, D:].astype(bf16)))
            points[-1] += [grad_in, grad_normed_one]
            grad_stream_norm, grad_gain_one = rec["norm_one_back"](grad_normed_one)
            grad_stream = grad_middle + grad_stream_norm
            grad_mix = product_tn(rec["normed"], grad_mix_own)[:, : HD + 2 * width]
            mix_blocks = grad_mix.reshape(ctx_count, depth, HD + 2 * width)
            if layer == 0:
                folded[layer].append(fold_last(mix_blocks))
            else:
                folded[layer].append(fold_halves(jnp.concatenate([out_blocks, mix_blocks], axis=2)))
            out_grads[layer] = (
                jnp.stack([grad_gain_one, grad_gain_two]), chan_grad, grad_conv, grad_heads,
            )
        last = points[-1]
        mix_kept, mix_got = folded[0][2]
        mix_sum = (mix_kept + after(mix_got, last[3]).astype(f32)).astype(bf16)
        out_sum, mix_sum = after((folded[0][1], mix_sum), last[3])
        came[0] = [
            group_swap(after(folded[0][0], last[3])),
            group_swap(jnp.concatenate([out_sum, mix_sum], axis=2)),
        ]

        share_grads = []
        for layer in range(LAYERS):
            normed = records[layer]["normed"]
            grad_share = share_sums[LAYERS - 1 - layer]
            near = lax.dynamic_slice_in_dim(normed, (slot * members + me) * depth, depth, 1)
            far = lax.dynamic_slice_in_dim(normed, ((1 - slot) * members + me) * depth, depth, 1)
            share_far = product_tn(far, grad_share)
            if layer == 0:
                share_far = after(share_far, came[0][1])
            share_far = lax.ppermute(share_far, half_axis, SWAP)
            if layer > 0:
                share_far = after(share_far, last[3])
            share_sum = product_tn(near, grad_share).astype(f32) + share_far.astype(f32)
            share_sum = share_sum.astype(bf16)
            for axis in tp_axes[::-1]:
                got = lax.ppermute(share_sum, axis, SWAP)
                first = lax.axis_index(axis) == 0
                share_sum = jnp.where(
                    first,
                    jnp.concatenate([share_sum, got], 1),
                    jnp.concatenate([got, share_sum], 1),
                )
            share_grads.append(share_sum[:, :share_cols].astype(f32))
        share_g = jnp.stack(share_grads)
        both_out = bring_out(jnp.stack([stream, grad_stream]))
        activations, input_grad = both_out[:, :, 0], both_out[:, :, 1]

        def weight_grads(layer):
            got = came[layer] if layer == 0 else after(came[layer], last[3])
            ffn_came, both_came = got
            out_came, mix_came = both_came[:, :, : HD + width], both_came[:, :, HD + width :]
            mix = jnp.concatenate(
                [
                    join_heads(mix_came[:, :, HD : HD + width], 1),
                    join_heads(mix_came[:, :, HD + width :], 1),
                    join_query_heads(mix_came[:, :, :HD], 1),
                ],
                axis=1,
            )
            out = jnp.concatenate(
                [join_heads(out_came[:, :, HD:], 1), join_query_heads(out_came[:, :, :HD], 1)],
                axis=1,
            )
            up = jnp.concatenate(
                [
                    ffn_came[g, :, part * ff_own : (part + 1) * ff_own]
                    for part in range(2)
                    for g in range(members)
                ],
                axis=1,
            )
            down = jnp.concatenate([ffn_came[g, :, 2 * ff_own :] for g in range(members)], axis=1)
            return mix, out.T, up, down.T

        by_layer = [weight_grads(layer) for layer in range(LAYERS)]
        mix_g, out_g, up_g, down_g = (jnp.stack(grads).astype(f32) for grads in zip(*by_layer))
        gain_g, chan_g, conv_g, head_g = (jnp.stack(grads) for grads in zip(*out_grads))
        chan_rows = jnp.zeros((LAYERS, CONV + 2, HGROUPS, heads, replicas, lanes), f32)
        chan_rows = lax.dynamic_update_slice(
            chan_rows,
            chan_g.reshape(LAYERS, CONV + 2, 1, heads, 1, lanes),
            (0, 0, head_group, 0, head_part, 0),
        ).reshape(LAYERS, CONV + 2, ssm_cols)
        head_rows = lax.dynamic_update_slice(
            jnp.zeros((LAYERS, 3, HGROUPS, heads), f32), head_g[:, :, None], (0, 0, head_group, 0)
        ).reshape(LAYERS, 3, tp_heads)

        def packed(arrays):
            flat = jnp.concatenate([a.reshape(-1) for a in arrays])
            return jnp.pad(flat, (0, -flat.shape[0] % 1024)).reshape(-1, 128)

        def unpacked(flat, arrays):
            flat, marks = flat.reshape(-1), [0]
            for a in arrays:
                marks.append(marks[-1] + a.size)
            return [flat[marks[k] : marks[k + 1]].reshape(a.shape) for k, a in enumerate(arrays)]

        early = (conv_g, gain_g[0, 1], gain_g[1:])
        whole = sum_over(packed(early), tp_axes[::-1])
        local_sums = (chan_rows, head_rows, whole)
        chan_sum, head_sum, whole = unpacked(
            sum_over(packed(local_sums), group_axes[::-1] + (half_axis,)), local_sums
        )
        conv_sum, gain_two, gain_rest = unpacked(whole, early)
        ctx_index = slot * members + me
        last_gain = jnp.repeat(gain_g[0, 0].reshape(ctx_count, 1, depth), 4, axis=1)
        last_gain = lax.all_to_all(
            last_gain.reshape(4 * ctx_count, 1, depth), all_axes, 0, 0, tiled=True
        )
        last_gain = jnp.sum(last_gain, axis=0)
        gain_rest = lax.dynamic_slice_in_dim(gain_rest, ctx_index * depth, depth, 2)
        gain_two = lax.dynamic_slice_in_dim(gain_two, ctx_index * depth, depth, 0)
        gain_own = jnp.concatenate([jnp.concatenate([last_gain, gain_two[None]])[None], gain_rest])
        return (
            activations,
            input_grad,
            gain_own,
            mix_g,
            share_g,
            chan_sum,
            conv_sum,
            head_sum,
            out_g,
            up_g,
            down_g,
        )

    return local


def solution(mesh):
    ctx_bits = mesh.shape["ctx"].bit_length() - 1
    tp_bits = mesh.shape["tp"].bit_length() - 1
    ctx_axes = tuple(f"c{k}" for k in range(ctx_bits))
    tp_axes = tuple(f"t{k}" for k in range(tp_bits))
    fine = Mesh(mesh.devices.reshape((2,) * (ctx_bits + tp_bits)), ctx_axes + tp_axes)
    return jax.shard_map(
        build(ctx_axes, tp_axes),
        mesh=fine,
        in_specs=(
            P(None, None, ctx_axes, None),
            P(None, None, ctx_axes, None),
            P(),
            P(None, None, ctx_axes),
            P(None, ctx_axes, tp_axes),
            P(None, ctx_axes, None),
            P(None, None, tp_axes),
            P(),
            P(None, None, tp_axes),
            P(None, tp_axes, ctx_axes),
            P(None, ctx_axes, tp_axes),
            P(None, tp_axes, ctx_axes),
        ),
        out_specs=(
            P(None, None, ctx_axes, None),
            P(None, None, ctx_axes, None),
            P(None, None, ctx_axes),
            P(None, ctx_axes, tp_axes),
            P(None, ctx_axes, None),
            P(None, None, tp_axes),
            P(),
            P(None, None, tp_axes),
            P(None, tp_axes, ctx_axes),
            P(None, ctx_axes, tp_axes),
            P(None, tp_axes, ctx_axes),
        ),
        check_vma=False,
    )
```
